128 devices in a mesh: row: 16 (over y, x), col: 8 (over z, core).
Axes of the slice: x: 4, y: 4, z: 4, core: 2. Of those that a mesh axis runs over, the one named last changes fastest.
Arguments:
- right_sides: float32 [32, 262144], P(None, ('row', 'col')), may hold values from -60 to 60
- diag_blocks: float32 [1024, 256, 256], P(('row', 'col')), may hold values from -1 to 3, as said below
- couplings: float32 [8192, 256, 256], P(('row', 'col')), may hold values from -0.125 to 0.125
- pair_index: int32 [2, 8192], P(None, ('row', 'col')), may hold values from 0 to 1023, as said below
Outputs:
- solution_field: float32 [32, 262144], P(None, ('row', 'col'))
- residual: float32 [32, 262144], P(None, ('row', 'col'))
The draws below stay inside these ranges and needn't reach their ends.
Inputs may be any that keep to these rules, and one draw needn't show every extreme that they name: `diag_blocks`: each block is symmetric; each of its diagonal entries is at least 1 and exceeds the sum of the magnitudes of the other entries of its row. Device i along row+col owns block rows i * 8 to (i + 1) * 8 - 1, and pair_index[0, k] of every block in its part of pair_index is one of them. pair_index[1, k] is a block row of the same device or of a device whose row index and col index each differ from its own by at most one.
All inputs are finite; a program needn't handle non-finite values.
Results may differ from the reference program's by a relative error of at most 0.0003.
Values sent between devices are 32-bit elements; how exact they have to be, the bound alone decides.
No kernel may reach another device: no remote copies, remote signals or barrier semaphores. Data moves between devices by JAX's collectives and lax.ppermute only.
A program may use at most 128 MiB of HBM per device.

```python
import math
import jax
import jax.numpy as jnp
from jax import lax

B = 256
RHS = 32
BR_DEV = 8
NB_DEV = 64
ITERS = 2
NBR = 1024
NB = 8192
NDOF = 262144
N_COL = 8


def draw_right_sides(key, part):
    key = jax.random.fold_in(key, 11)
    noise_key, dof_key, column_key = jax.random.split(key, 3)
    positions = jnp.arange(NDOF).astype(jnp.float32)
    rising = 1.0 + 2.0 * positions / (NDOF - 1)
    dof_scale = jnp.exp(jax.random.uniform(dof_key, (1, NDOF), jnp.float32, 0.0, math.log(10.0)))
    column_scale = jnp.exp(jax.random.uniform(column_key, (RHS, 1), jnp.float32, 0.0, math.log(10.0)))
    blended = jnp.clip(jax.random.normal(noise_key, (RHS, NDOF), jnp.float32), -4.0, 4.0)
    return blended * column_scale * dof_scale * rising[None, :] / 40.0


def draw_diag_blocks(key, part):
    key = jax.random.fold_in(key, 7)
    entry_key, lead_key = jax.random.split(key)
    block_shape = (NBR, B, B)
    entries = jax.random.uniform(entry_key, block_shape, jnp.float32, -1.0, 1.0)
    leading = jnp.exp(jax.random.uniform(lead_key, (NBR, B), jnp.float32, 0.0, math.log(3.0)))
    symmetric = 0.5 * (entries + jnp.swapaxes(entries, 1, 2))
    on_diagonal = jnp.arange(B)[:, None] == jnp.arange(B)[None, :]
    return jnp.where(on_diagonal[None, :, :], leading[:, :, None], 0.95 / (B - 1) * symmetric)


def draw_pair_index(key, part):
    key = jax.random.fold_in(key, 5)
    devices = NBR // BR_DEV
    row_count = devices // N_COL

    def one_device(device):
        own_key = jax.random.fold_in(key, device)
        peer_key, focal_key, column_key, row_key = jax.random.split(own_key, 4)
        my_row = device // N_COL
        my_col = device % N_COL
        focal = jax.random.randint(focal_key, (), 0, 9)
        raw_pick = jax.random.randint(peer_key, (NB_DEV,), 0, 13)
        offset = jnp.where(raw_pick >= 9, focal, raw_pick)
        target_row = my_row + offset // 3 - 1
        target_col = my_col + offset % 3 - 1
        inside = (target_row >= 0) & (target_row < row_count) & (target_col >= 0) & (target_col < N_COL)
        target_row = jnp.where(inside, target_row, my_row)
        target_col = jnp.where(inside, target_col, my_col)
        peer_ids = target_row * N_COL + target_col
        columns = peer_ids * BR_DEV + jax.random.randint(column_key, (NB_DEV,), 0, BR_DEV)
        rows_found = device * BR_DEV + jax.random.randint(row_key, (NB_DEV,), 0, BR_DEV)
        return (rows_found.astype(jnp.int32), columns.astype(jnp.int32))
    row_list, column_list = jax.vmap(one_device)(jnp.arange(devices, dtype=jnp.int32))
    return jnp.stack([row_list.reshape(-1), column_list.reshape(-1)]).astype(jnp.int32)


def levels(key, dims, cuts, low, high):
    def one(position, parts):
        steps = jax.random.uniform(jax.random.fold_in(jax.random.fold_in(key, 6), position), (parts,), jnp.float32, low / len(cuts), high / len(cuts))
        return jnp.repeat(jnp.exp(steps), dims[position] // parts).reshape((-1,) + (1,) * (len(dims) - position - 1))

    factor_of = one(*cuts[0])
    for cut in cuts[1:]:
        factor_of = factor_of * one(*cut)
    return factor_of


def scatter_about(stream_key, dims, deviation, most, pieces=(), kind=jnp.bfloat16):
    loudness = levels(stream_key, dims, pieces, -0.22, 0.18) if pieces else 1.0
    values = jax.random.normal(stream_key, dims, jnp.float32) * deviation * loudness
    return jnp.minimum(jnp.maximum(values, -most), most).astype(kind)


def setup_inputs(seed: int = 0) -> dict:
    keys = jax.random.split(jax.random.key(seed), 5)
    right_sides = draw_right_sides(jax.random.fold_in(keys[4], 71), 0)
    diag_blocks = draw_diag_blocks(jax.random.fold_in(keys[4], 71), 0)
    couplings = scatter_about(keys[2], (NB, B, B), (B * NB_DEV // BR_DEV) ** -0.5, 0.125, ((0, 128),), jnp.float32)
    pair_index = draw_pair_index(jax.random.fold_in(keys[4], 71), 0)
    return {"right_sides": right_sides, "diag_blocks": diag_blocks, "couplings": couplings, "pair_index": pair_index}


FULL_PRECISION = lax.Precision.HIGHEST

def solve_spd(matrix, right_side):
    factor = jnp.linalg.cholesky(matrix)
    return jax.scipy.linalg.cho_solve((factor, True), right_side)

def product(left, right):
    return jnp.dot(left, right, precision=FULL_PRECISION)

def gram_of(left, right):
    return jnp.dot(left, right.T, precision=FULL_PRECISION)

def apply_operator(vector, diag_blocks, couplings, pair_index):
    blocks = vector.reshape(RHS, NBR, B)
    own_part = jnp.einsum('rqj,qij->rqi', blocks, diag_blocks, precision=FULL_PRECISION)
    pulled = jnp.take(blocks, pair_index[1], axis=1)
    strain_terms = jnp.einsum('rkj,kij->rki', pulled, couplings, precision=FULL_PRECISION)
    strain = jnp.zeros((RHS, NBR, B), jnp.float32).at[:, pair_index[0], :].add(strain_terms)
    back_terms = jnp.einsum('rki,kij->rkj', jnp.take(strain, pair_index[0], axis=1), couplings, precision=FULL_PRECISION)
    combined = own_part.at[:, pair_index[1], :].add(back_terms)
    return combined.reshape(RHS, NDOF)

def reference(right_sides, diag_blocks, couplings, pair_index):
    solution_field = jnp.zeros_like(right_sides)
    residual = right_sides
    direction = right_sides
    current = gram_of(residual, residual)
    for iteration in range(ITERS):
        applied = apply_operator(direction, diag_blocks, couplings, pair_index)
        curvature = gram_of(direction, applied)
        step_size = solve_spd(curvature, current)
        solution_field = solution_field + product(step_size.T, direction)
        residual = residual - product(step_size.T, applied)
        if iteration + 1 < ITERS:
            following = gram_of(residual, residual)
            beta_mix = solve_spd(current, following)
            direction = residual + product(beta_mix.T, direction)
            current = following
    return (solution_field, residual)
```

```python
import jax
import jax.numpy as jnp
from jax import lax
from jax.experimental import pallas as pl
from jax.experimental.pallas import tpu as pltpu
from jax.sharding import PartitionSpec as P

F32 = jnp.float32
BF16 = jnp.bfloat16
HIGHEST = lax.Precision.HIGHEST
VMEM_SPEC = pl.BlockSpec(memory_space=pltpu.VMEM)
SMEM_SPEC = pl.BlockSpec(memory_space=pltpu.SMEM)
CHUNK = 8


def in_vmem(value):
    return pltpu.with_memory_space_constraint(value, pltpu.VMEM)


def pairs_of(count, shift):
    found = []
    for place in range(count):
        partner = ((place + shift) ^ 1) - shift
        if 0 <= partner < count:
            found.append((place, partner))
    return found


def swapped(value, axis, shift):
    return lax.ppermute(value, axis, pairs_of(lax.axis_size(axis), shift))


def slot_of(target, mine):
    return jnp.where(target == mine, 0, jnp.where(target == (mine ^ 1), 1, 2))


def split(value):
    high = value.astype(BF16)
    return high, (value - high.astype(F32)).astype(BF16)


def dot_nt(left, right):
    return lax.dot_general(left, right, (((1,), (1,)), ((), ())), preferred_element_type=F32)


def dot_nn(left, right):
    return lax.dot_general(left, right, (((1,), (0,)), ((), ())), preferred_element_type=F32)


def full_nn(left, right):
    return lax.dot_general(left, right, (((1,), (0,)), ((), ())), precision=HIGHEST, preferred_element_type=F32)


def full_tn(left, right):
    return lax.dot_general(left, right, (((0,), (0,)), ((), ())), precision=HIGHEST, preferred_element_type=F32)


def gram(left, right):
    both = dot_nt(left, right)
    half = both.shape[0] // 2
    return both[:half, :half] + both[:half, half:] + both[half:, :half] + both[half:, half:]


def times(dot, stacked, high, low):
    half = stacked.shape[0] // 2
    first = dot(stacked, high)
    return first[:half] + first[half:] + dot(stacked[:half], low)


def stacked_split(value):
    return jnp.concatenate(split(value), axis=0)


def call(body, out_shape, n_smem, args, scratch=(), limit=24 << 20):
    return pl.pallas_call(
        body,
        out_shape=out_shape,
        in_specs=[SMEM_SPEC] * n_smem + [VMEM_SPEC] * (len(args) - n_smem),
        out_specs=jax.tree.map(lambda _: VMEM_SPEC, out_shape),
        scratch_shapes=list(scratch),
        compiler_params=pltpu.CompilerParams(vmem_limit_bytes=limit),
    )(*args[:n_smem], *[in_vmem(a) for a in args[n_smem:]])


def prepare_body(couplings, diag, right, c_high, c_low, d_high, d_low, own, grams):
    step = pl.program_id(0)
    per = couplings.shape[0]
    for place in range(per):
        high, low = split(couplings[place])
        c_high[step * per + place] = high
        c_low[step * per + place] = low
    high, low = split(diag[0])
    d_high[step] = high
    d_low[step] = low
    vector = stacked_split(right[...])
    term = times(dot_nt, vector, high, low)
    own[step] = term

    @pl.when(step == 0)
    def _():
        grams[...] = jnp.zeros_like(grams)

    grams[0] += gram(vector, vector)
    grams[1] += gram(stacked_split(term), vector)


def prepare(couplings, diag, right):
    count, width = couplings.shape[0], couplings.shape[1]
    blocks, rows = diag.shape[0], right.shape[0]
    per = count // blocks
    return pl.pallas_call(
        prepare_body,
        grid=(blocks,),
        in_specs=[
            pl.BlockSpec((per, width, width), lambda i: (i, 0, 0)),
            pl.BlockSpec((1, width, width), lambda i: (i, 0, 0)),
            pl.BlockSpec((rows, width), lambda i: (0, i)),
        ],
        out_specs=[VMEM_SPEC] * 6,
        out_shape=[
            pltpu.VMEM((count, width, width), BF16),
            pltpu.VMEM((count, width, width), BF16),
            pltpu.VMEM((blocks, width, width), BF16),
            pltpu.VMEM((blocks, width, width), BF16),
            pltpu.VMEM((blocks, rows, width), F32),
            pltpu.VMEM((2, rows, rows), F32),
        ],
        compiler_params=pltpu.CompilerParams(vmem_limit_bytes=24 << 20),
    )(couplings, diag, right)


def stack_flat_body(own, first, second, out):
    blocks, width = out.shape[1], out.shape[3]
    for slot, source in enumerate((own, first, second)):
        for q in range(blocks):
            out[slot, q] = source[:, q * width:(q + 1) * width]


def stack_body(own, first, second, out):
    for slot, source in enumerate((own, first, second)):
        out[slot] = source[...]


def operator_body(table_row, local_row, t0, t1, t2, c_high, c_low, p0, p1, p2, g_out, table, strain, strain_hl, pieces):
    blocks, rows, width = t0.shape[1], t0.shape[2], t0.shape[3]
    count = c_high.shape[0]
    for group, source in enumerate((t0, t1, t2)):
        for slot in range(3):
            def fill(q, carry, group=group, slot=slot, source=source):
                table[(group * 3 + slot) * blocks + q] = stacked_split(source[slot, q])
                return carry
            lax.fori_loop(0, blocks, fill, 0, unroll=True)
    strain[...] = jnp.zeros_like(strain)
    pieces[...] = jnp.zeros_like(pieces)

    def pull(chunk, carry):
        terms = []
        for place in range(CHUNK):
            k = chunk * CHUNK + place
            terms.append((local_row[k], times(dot_nt, table[table_row[k]], c_high[k], c_low[k])))
        for row, term in terms:
            strain[row] += term
        return carry

    lax.fori_loop(0, count // CHUNK, pull, 0)
    total = jnp.zeros((rows, rows), F32)
    for q in range(blocks):
        both = stacked_split(strain[q])
        strain_hl[q] = both
        total += gram(both, both)
    g_out[...] = total

    def push(chunk, carry):
        terms = []
        for place in range(CHUNK):
            k = chunk * CHUNK + place
            terms.append((table_row[k], times(dot_nn, strain_hl[local_row[k]], c_high[k], c_low[k])))
        for row, term in terms:
            pieces[row] += term
        return carry

    lax.fori_loop(0, count // CHUNK, push, 0)
    for group, target in enumerate((p0, p1, p2)):
        for slot in range(3):
            for q in range(blocks):
                target[slot, q] = pieces[(group * 3 + slot) * blocks + q]


def apply_couplings(tables, c_high, c_low, table_row, local_row):
    _, blocks, rows, width = tables[0].shape
    piece = pltpu.VMEM((3, blocks, rows, width), F32)
    return call(
        operator_body,
        [piece, piece, piece, pltpu.VMEM((rows, rows), F32)],
        2,
        (table_row, local_row, *tables, c_high, c_low),
        [
            pltpu.VMEM((9 * blocks, 2 * rows, width), BF16),
            pltpu.VMEM((blocks, rows, width), F32),
            pltpu.VMEM((blocks, 2 * rows, width), BF16),
            pltpu.VMEM((9 * blocks, rows, width), F32),
        ],
    )


def middle_body(p0, q1, q2, own, m0, m1, m2):
    m1[...] = p0[1] + q1[1] + q2[1]
    m2[...] = p0[2] + q1[2] + q2[2]
    m0[...] = p0[0] + q1[0] + q2[0] + own[...]


def returned(p0, p1, p2, own):
    q1 = swapped(p1, "col", 0)
    q2 = swapped(p2, "col", 1)
    shape = pltpu.VMEM(own.shape, F32)
    m0, m1, m2 = call(middle_body, [shape] * 3, 0, (p0, q1, q2, own))
    return m0, swapped(m1, "row", 0), swapped(m2, "row", 1)


def sum_body(m0, a, b, out):
    out[...] = m0[...] + a[...] + b[...]


def diag_body(vector, d_high, d_low, own, grams):
    g2 = jnp.zeros(grams.shape[1:], F32)
    g3 = jnp.zeros(grams.shape[1:], F32)
    for q in range(vector.shape[0]):
        both = stacked_split(vector[q])
        term = times(dot_nt, both, d_high[q], d_low[q])
        own[q] = term
        g2 += gram(both, both)
        g3 += gram(stacked_split(term), both)
    grams[0] = g2
    grams[1] = g3


def eliminated(matrix, right):
    size = matrix.shape[0]
    work = jnp.concatenate([matrix, right], axis=1)
    rows = lax.broadcasted_iota(jnp.int32, work.shape, 0)
    for k in range(size):
        pivot_row = work[k:k + 1, :] / work[k:k + 1, k:k + 1]
        work = jnp.where(rows == k, pivot_row, work - work[:, k:k + 1] * pivot_row)
    return work[:, size:]


def finish_body(grams, right, u, m0, a, b, x_out, r_out):
    size = grams.shape[0]
    g0, g1, g2, g3 = (grams[:, i * size:(i + 1) * size] for i in range(4))
    eye = (lax.broadcasted_iota(jnp.int32, (size, size), 0) == lax.broadcasted_iota(jnp.int32, (size, size), 1)).astype(F32)
    alpha = eliminated(g1, g0)
    inverse = eliminated(g0, eye)
    fresh = (g0 - full_nn(g1, alpha)) - full_tn(alpha, g1 - full_nn(g2, alpha))
    mix = eye + full_nn(inverse, fresh)
    e1 = full_nn(g1, mix) - full_nn(g2, alpha)
    e2 = full_nn(g2, mix) - full_nn(g3, alpha)
    curvature = full_tn(mix, e1) - full_tn(alpha, e2)
    second = eliminated(curvature, fresh)
    p = alpha + full_nn(mix, second)
    q = full_nn(alpha, second)
    width = u.shape[2]
    for block in range(u.shape[0]):
        lanes = slice(block * width, (block + 1) * width)
        w = m0[block] + a[block] + b[block]
        x_out[:, lanes] = full_tn(p, right[:, lanes]) - full_tn(q, u[block])
        r_out[:, lanes] = right[:, lanes] - full_tn(p, u[block]) + full_tn(q, w)


def total_over_devices(value):
    count = lax.axis_size("row") * lax.axis_size("col")
    for mask in (1, 2, 6, 8, 24, 32, 96):
        moved = lax.ppermute(value, ("row", "col"), [(i, i ^ mask) for i in range(count)])
        value = value + moved
    return value


def per_device(right_sides, diag_blocks, couplings, pair_index):
    blocks, width = diag_blocks.shape[0], diag_blocks.shape[1]
    rows = right_sides.shape[0]
    col_size = lax.axis_size("col")
    my_row, my_col = lax.axis_index("row"), lax.axis_index("col")
    local_row = pair_index[0] - (my_row * col_size + my_col) * blocks
    owner = pair_index[1] // blocks
    slot = slot_of(owner % col_size, my_col) * 3 + slot_of(owner // col_size, my_row)
    table_row = slot * blocks + pair_index[1] % blocks

    block_shape = pltpu.VMEM((blocks, rows, width), F32)
    stack_shape = pltpu.VMEM((3, blocks, rows, width), F32)
    gram_shape = pltpu.VMEM((2, rows, rows), F32)

    first = swapped(right_sides, "row", 0)
    second = swapped(right_sides, "row", 1)
    c_high, c_low, d_high, d_low, own, g01 = prepare(couplings, diag_blocks, right_sides)
    t0 = call(stack_flat_body, stack_shape, 0, (right_sides, first, second))
    tables = (t0, swapped(t0, "col", 0), swapped(t0, "col", 1))
    p0, p1, p2, g1s = apply_couplings(tables, c_high, c_low, table_row, local_row)
    m0, a, b = returned(p0, p1, p2, own)
    u = call(sum_body, block_shape, 0, (m0, a, b))

    first = swapped(u, "row", 0)
    second = swapped(u, "row", 1)
    own, g23 = call(diag_body, [block_shape, gram_shape], 0, (u, d_high, d_low))
    t0 = call(stack_body, stack_shape, 0, (u, first, second))
    tables = (t0, swapped(t0, "col", 0), swapped(t0, "col", 1))
    p0, p1, p2, g3s = apply_couplings(tables, c_high, c_low, table_row, local_row)
    grams = jnp.concatenate([g01[0], g01[1] + g1s, g23[0], g23[1] + g3s], axis=1)
    grams = total_over_devices(grams)
    m0, a, b = returned(p0, p1, p2, own)
    flat = jax.ShapeDtypeStruct(right_sides.shape, F32)
    return tuple(call(finish_body, [flat, flat], 0, (grams, right_sides, u, m0, a, b)))


def solution(mesh):
    return jax.shard_map(
        per_device,
        mesh=mesh,
        in_specs=(
            P(None, ("row", "col")),
            P(("row", "col"), None, None),
            P(("row", "col"), None, None),
            P(None, ("row", "col")),
        ),
        out_specs=(P(None, ("row", "col")), P(None, ("row", "col"))),
        check_vma=False,
    )
```

```python
import jax
import jax.numpy as jnp
from jax import lax
from jax.experimental import pallas as pl
from jax.experimental.pallas import tpu as pltpu
from jax.sharding import PartitionSpec as P

F32 = jnp.float32
BF16 = jnp.bfloat16
HIGHEST = lax.Precision.HIGHEST
VMEM_SPEC = pl.BlockSpec(memory_space=pltpu.VMEM)
SMEM_SPEC = pl.BlockSpec(memory_space=pltpu.SMEM)
CHUNK = 8
HALVES = 2
TOKEN = pltpu.VMEM((8, 128), F32)


def in_vmem(value):
    return pltpu.with_memory_space_constraint(value, pltpu.VMEM)


def in_hbm(value):
    return pltpu.with_memory_space_constraint(value, pltpu.HBM)


def pairs_of(count, shift):
    found = []
    for place in range(count):
        partner = ((place + shift) ^ 1) - shift
        if 0 <= partner < count:
            found.append((place, partner))
    return found


def swapped(value, axis, shift):
    return lax.ppermute(value, axis, pairs_of(lax.axis_size(axis), shift))


def slot_of(target, mine):
    return jnp.where(target == mine, 0, jnp.where(target == (mine ^ 1), 1, 2))


def split(value):
    high = value.astype(BF16)
    return high, (value - high.astype(F32)).astype(BF16)


def dot_nt(left, right):
    return lax.dot_general(left, right, (((1,), (1,)), ((), ())), preferred_element_type=F32)


def dot_nn(left, right):
    return lax.dot_general(left, right, (((1,), (0,)), ((), ())), preferred_element_type=F32)


def full_nn(left, right):
    return lax.dot_general(left, right, (((1,), (0,)), ((), ())), precision=HIGHEST, preferred_element_type=F32)


def full_tn(left, right):
    return lax.dot_general(left, right, (((0,), (0,)), ((), ())), precision=HIGHEST, preferred_element_type=F32)


def gram(left, right):
    both = dot_nt(left, right)
    half = both.shape[0] // 2
    return both[:half, :half] + both[:half, half:] + both[half:, :half] + both[half:, half:]


def times(dot, stacked, high, low):
    half = stacked.shape[0] // 2
    first = dot(stacked, high)
    return first[:half] + first[half:] + dot(stacked[:half], low)


def stacked_split(value):
    return jnp.concatenate(split(value), axis=0)


def call(body, out_shape, n_smem, args, scratch=(), aliases=None, limit=12 << 20):
    return pl.pallas_call(
        body,
        out_shape=out_shape,
        in_specs=[SMEM_SPEC] * n_smem + [VMEM_SPEC] * (len(args) - n_smem),
        out_specs=jax.tree.map(lambda _: VMEM_SPEC, out_shape),
        scratch_shapes=list(scratch),
        name=body.__name__,
        input_output_aliases=aliases or {},
        compiler_params=pltpu.CompilerParams(vmem_limit_bytes=limit),
    )(*args[:n_smem], *[in_vmem(a) for a in args[n_smem:]])


def prepare_body(couplings, c_high, c_low, token):
    per = couplings.shape[0]
    first = pl.program_id(0) * per
    token[...] = jnp.zeros_like(token)
    for place in range(per):
        high, low = split(couplings[place])
        c_high[first + place] = high
        c_low[first + place] = low


def prepare(couplings, part):
    count, width = couplings.shape[0] // HALVES, couplings.shape[1]
    steps = count // CHUNK
    half = pltpu.VMEM((count, width, width), BF16)
    return pl.pallas_call(
        prepare_body,
        grid=(steps,),
        in_specs=[pl.BlockSpec((CHUNK, width, width), lambda i: (i + part * steps, 0, 0))],
        out_specs=[VMEM_SPEC] * 3,
        out_shape=[half, half, TOKEN],
        name="prepare",
        compiler_params=pltpu.CompilerParams(vmem_limit_bytes=12 << 20),
    )(in_hbm(couplings))


def block_of(source, q, width):
    return source[q] if len(source.shape) == 3 else source[:, q * width:(q + 1) * width]


def stack_body(first, second, *rest):
    out = rest[-1]
    blocks, width = out.shape[1], out.shape[3]
    for slot, source in enumerate((first, second)):
        for q in range(blocks):
            out[slot, q] = block_of(source, q, width)


def accumulate(dot, far, routes, near, source_row, target_row, source, target, halves):
    for half in range(HALVES):
        c_high, c_low = halves[2 * half], halves[2 * half + 1]

        def step(chunk, carry):
            terms = []
            for place in range(CHUNK):
                i = chunk * CHUNK + place
                k = routes[half, 0, i]
                terms.append((routes[half, target_row, i], times(dot, source[routes[half, source_row, i]], c_high[k], c_low[k])))
            for row, term in terms:
                target[row] += term
            return carry

        edge = near[half] // CHUNK
        first, last = (edge, routes.shape[2] // CHUNK) if far else (0, edge)
        lax.fori_loop(first, last, step, 0)


def pull_near_body(routes, near, own, ra, rb, ca, cb, *refs):
    *halves, table, strain = refs
    blocks, width = strain.shape[0], strain.shape[2]
    for slot, source in enumerate((own, ra, rb, ca, cb)):
        for q in range(blocks):
            table[slot * blocks + q] = stacked_split(block_of(source, q, width))
    strain[...] = jnp.zeros_like(strain)
    accumulate(dot_nt, False, routes, near, 1, 2, table, strain, halves)


def pull_far_body(routes, near, table_in, strain_in, da, db, *refs):
    halves, refs = refs[:2 * HALVES], refs[2 * HALVES:]
    *grams, table, strain_hl, g_out, strain = refs
    blocks = strain.shape[0]
    for group, source in enumerate((da, db)):
        for slot in range(2):
            for q in range(blocks):
                table[(5 + 2 * group + slot) * blocks + q] = stacked_split(source[slot, q])
    strain[...] = strain_in[...]
    accumulate(dot_nt, True, routes, near, 1, 2, table, strain, halves)
    total = jnp.zeros((strain.shape[1],) * 2, F32)
    for q in range(blocks):
        both = stacked_split(strain[q])
        strain_hl[q] = both
        total += gram(both, both)
    if not grams:
        g_out[...] = total
    else:
        g01, g1, g23 = grams
        size = total.shape[0]
        for i, part in enumerate((g01[0], g01[1] + g1[...], g23[0], g23[1] + total)):
            g_out[:, i * size:(i + 1) * size] = part


def push_far_body(routes, near, strain_hl, *refs):
    *halves, pieces, da, db = refs
    blocks = strain_hl.shape[0]
    pieces[...] = jnp.zeros_like(pieces)
    accumulate(dot_nn, True, routes, near, 2, 1, strain_hl, pieces, halves)
    for group, target in enumerate((da, db)):
        for slot in range(2):
            for q in range(blocks):
                target[slot, q] = pieces[(5 + 2 * group + slot) * blocks + q]


def push_near_body(routes, near, strain_hl, *refs):
    halves, pieces_in = refs[:2 * HALVES], refs[2 * HALVES]
    own, ra, rb, ca, cb, pieces = refs[-6:]
    blocks = strain_hl.shape[0]
    pieces[...] = pieces_in[:pieces.shape[0]]
    accumulate(dot_nn, False, routes, near, 2, 1, strain_hl, pieces, halves)
    for slot, target in enumerate((own, ra, rb, ca, cb)):
        for q in range(blocks):
            target[q] = pieces[slot * blocks + q]


def diag_body(vector, diag, own, grams):
    size = grams.shape[1]
    first = jnp.zeros((size, size), F32)
    second = jnp.zeros((size, size), F32)
    width = diag.shape[1]
    for q in range(diag.shape[0]):
        both = stacked_split(block_of(vector, q, width))
        term = times(dot_nn, both, *split(diag[q]))
        own[q] = term
        first += gram(both, both)
        second += gram(stacked_split(term), both)
    grams[0] = first
    grams[1] = second


def middle_body(ra, rb, qa, qb, ma, mb):
    ma[...] = ra[...] + qa[0] + qb[0]
    mb[...] = rb[...] + qa[1] + qb[1]


def middle_gram_body(ra, rb, qa, qb, g, moved, ma, mb, g_out):
    middle_body(ra, rb, qa, qb, ma, mb)
    g_out[...] = g[...] + moved[...]


def sum_body(own, diag, ca, cb, ra, rb, out):
    out[...] = (own[...] + diag[...]) + (ca[...] + cb[...]) + (ra[...] + rb[...])


def eliminated(matrix, right):
    size = matrix.shape[0]
    work = jnp.concatenate([matrix, right], axis=1)
    rows = lax.broadcasted_iota(jnp.int32, work.shape, 0)
    for k in range(0, size, 2):
        upper, lower = work[k:k + 1, :], work[k + 1:k + 2, :]
        upper = upper / upper[:, k:k + 1]
        lower = lower - lower[:, k:k + 1] * upper
        lower = lower / lower[:, k + 1:k + 2]
        upper = upper - upper[:, k + 1:k + 2] * lower
        rest = work - work[:, k:k + 1] * upper - work[:, k + 1:k + 2] * lower
        work = jnp.where(rows == k, upper, jnp.where(rows == k + 1, lower, rest))
    return work[:, size:]


def finish_body(grams, moved, right, u, own, diag, ca, cb, ra, rb, x_out, r_out):
    size = grams.shape[0]
    total = grams[...] + moved[...]
    g0, g1, g2, g3 = (total[:, i * size:(i + 1) * size] for i in range(4))
    eye = (lax.broadcasted_iota(jnp.int32, (size, size), 0) == lax.broadcasted_iota(jnp.int32, (size, size), 1)).astype(F32)
    alpha = eliminated(g1, g0)
    inverse = eliminated(g0, eye)
    fresh = (g0 - full_nn(g1, alpha)) - full_tn(alpha, g1 - full_nn(g2, alpha))
    mix = eye + full_nn(inverse, fresh)
    e1 = full_nn(g1, mix) - full_nn(g2, alpha)
    e2 = full_nn(g2, mix) - full_nn(g3, alpha)
    curvature = full_tn(mix, e1) - full_tn(alpha, e2)
    second = eliminated(curvature, fresh)
    p = alpha + full_nn(mix, second)
    q = full_nn(alpha, second)
    width = u.shape[2]
    for block in range(u.shape[0]):
        lanes = slice(block * width, (block + 1) * width)
        w = (own[block] + diag[block]) + (ca[block] + cb[block]) + (ra[block] + rb[block])
        x_out[:, lanes] = full_tn(p, right[:, lanes]) - full_tn(q, u[block])
        r_out[:, lanes] = right[:, lanes] - full_tn(p, u[block]) + full_tn(q, w)


MASKS = (1, 2, 6, 8, 24, 32, 96)


def exchanged(value, mask):
    count = lax.axis_size("row") * lax.axis_size("col")
    return lax.ppermute(value, ("row", "col"), [(i, i ^ mask) for i in range(count)])


def routing(pair_index, blocks):
    count = pair_index.shape[1]
    col_size = lax.axis_size("col")
    my_row, my_col = lax.axis_index("row"), lax.axis_index("col")
    local_row = pair_index[0] - (my_row * col_size + my_col) * blocks
    owner = pair_index[1] // blocks
    row_slot = slot_of(owner // col_size, my_row)
    col_slot = slot_of(owner % col_size, my_col)
    far = (row_slot > 0) & (col_slot > 0)
    slot = jnp.where(far, 2 + 2 * col_slot + row_slot, jnp.where(col_slot > 0, 2 + col_slot, row_slot))
    table_row = slot * blocks + pair_index[1] % blocks
    count = count // HALVES
    number = jnp.arange(count, dtype=jnp.int32)
    far = far.reshape(HALVES, count)
    key = jnp.where(far, count, 0) + number
    rank = jnp.sum((key[:, None, :] < key[:, :, None]).astype(jnp.int32), axis=2)
    placed = rank[:, None, :] == number[:, None]
    columns = [jnp.broadcast_to(number, far.shape), table_row.reshape(far.shape), local_row.reshape(far.shape)]
    routes = jnp.stack([jnp.sum(jnp.where(placed, c[:, None, :], 0), axis=2) for c in columns], axis=1)
    near = count - jnp.sum(far.astype(jnp.int32), axis=1)
    return routes, near


def per_device(right_sides, diag_blocks, couplings, pair_index):
    blocks, width = diag_blocks.shape[0], diag_blocks.shape[1]
    rows = right_sides.shape[0]
    block_shape = pltpu.VMEM((blocks, rows, width), F32)
    pair_shape = pltpu.VMEM((2, blocks, rows, width), F32)
    table_shape = pltpu.VMEM((9 * blocks, 2 * rows, width), BF16)
    split_shape = pltpu.VMEM((blocks, 2 * rows, width), BF16)
    pieces_shape = pltpu.VMEM((9 * blocks, rows, width), F32)
    near_pieces_shape = pltpu.VMEM((5 * blocks, rows, width), F32)
    gram_shape = pltpu.VMEM((rows, rows), F32)
    grams_shape = pltpu.VMEM((2, rows, rows), F32)
    all_grams_shape = pltpu.VMEM((rows, 4 * rows), F32)

    def spread(vector, *after):
        ra, rb = swapped(vector, "row", 0), swapped(vector, "row", 1)
        ca, cb = swapped(vector, "col", 0), swapped(vector, "col", 1)
        both = call(stack_body, pair_shape, 0, (ra, rb) + (after or (ca, cb)))
        return (vector, ra, rb, ca, cb), swapped(both, "col", 0), swapped(both, "col", 1)

    def pulled(near_tables, da, db, split_couplings, *grams):
        table, strain = call(pull_near_body, [table_shape, block_shape], 2, (routes, near, *near_tables, *split_couplings))
        _, strain_hl, g = call(
            pull_far_body, [table_shape, split_shape, all_grams_shape if grams else gram_shape], 2,
            (routes, near, table, strain, da, db, *split_couplings, *grams), [block_shape], aliases={2: 0})
        return strain_hl, g

    def pushed(strain_hl, split_couplings, *after):
        pieces, da, db = call(push_far_body, [pieces_shape, pair_shape, pair_shape], 2, (routes, near, strain_hl, *split_couplings))
        da, db = swapped(da, "col", 0), swapped(db, "col", 1)
        own, ra, rb, ca, cb = call(
            push_near_body, [block_shape] * 5, 2, (routes, near, strain_hl, *split_couplings, pieces, *after), [near_pieces_shape])
        return own, ra, rb, swapped(ca, "col", 0), swapped(cb, "col", 1), da, db

    routes, near = routing(pair_index, blocks)
    *early, token = prepare(couplings, 0)
    near_tables, da, db = spread(right_sides, token)
    *late, _ = prepare(couplings, 1)
    split_couplings = early + late
    strain_hl, g1s = pulled(near_tables, da, db, split_couplings)
    own, ra, rb, ca, cb, da, db = pushed(strain_hl, split_couplings)
    diag, g01 = call(diag_body, [block_shape, grams_shape], 0, (right_sides, diag_blocks))
    ra, rb = call(middle_body, [block_shape] * 2, 0, (ra, rb, da, db))
    ra, rb = swapped(ra, "row", 0), swapped(rb, "row", 1)
    u = call(sum_body, block_shape, 0, (own, diag, ca, cb, ra, rb))

    near_tables, da, db = spread(u)
    diag, g23 = call(diag_body, [block_shape, grams_shape], 0, (u, diag_blocks))
    strain_hl, grams = pulled(near_tables, da, db, split_couplings, g01, g1s, g23)
    grams = grams + exchanged(grams, MASKS[0])
    own, ra, rb, ca, cb, da, db = pushed(strain_hl, split_couplings, grams)
    for mask in MASKS[1:3]:
        grams = grams + exchanged(grams, mask)
    ra, rb, grams = call(
        middle_gram_body, [block_shape] * 2 + [all_grams_shape], 0,
        (ra, rb, da, db, grams, exchanged(grams, MASKS[3])))
    ra, rb = swapped(ra, "row", 0), swapped(rb, "row", 1)
    for mask in MASKS[4:6]:
        grams = grams + exchanged(grams, mask)
    flat = jax.ShapeDtypeStruct(right_sides.shape, F32)
    return tuple(call(
        finish_body, [flat, flat], 0,
        (grams, exchanged(grams, MASKS[6]), right_sides, u, own, diag, ca, cb, ra, rb)))


def solution(mesh):
    return jax.shard_map(
        per_device,
        mesh=mesh,
        in_specs=(
            P(None, ("row", "col")),
            P(("row", "col"), None, None),
            P(("row", "col"), None, None),
            P(None, ("row", "col")),
        ),
        out_specs=(P(None, ("row", "col")), P(None, ("row", "col"))),
        check_vma=False,
    )
```

```python
import jax
import jax.numpy as jnp
from jax import lax
from jax.experimental import pallas as pl
from jax.experimental.pallas import tpu as pltpu
from jax.sharding import PartitionSpec as P

F32 = jnp.float32
BF16 = jnp.bfloat16
HIGHEST = lax.Precision.HIGHEST
VMEM_SPEC = pl.BlockSpec(memory_space=pltpu.VMEM)
SMEM_SPEC = pl.BlockSpec(memory_space=pltpu.SMEM)
CHUNK = 8
HALVES = 2
TOKEN = pltpu.VMEM((8, 128), F32)


def in_vmem(value):
    return pltpu.with_memory_space_constraint(value, pltpu.VMEM)


def in_hbm(value):
    return pltpu.with_memory_space_constraint(value, pltpu.HBM)


def pairs_of(count, shift):
    return [(place, (((place + shift) ^ 1) - shift) % count) for place in range(count)]


def swapped(value, axis, shift):
    return lax.ppermute(value, axis, pairs_of(lax.axis_size(axis), shift))


def slot_of(target, mine):
    return jnp.where(target == mine, 0, jnp.where(target == (mine ^ 1), 1, 2))


def split(value):
    high = value.astype(BF16)
    return high, (value - high.astype(F32)).astype(BF16)


def dot_nt(left, right):
    return lax.dot_general(left, right, (((1,), (1,)), ((), ())), preferred_element_type=F32)


def dot_nn(left, right):
    return lax.dot_general(left, right, (((1,), (0,)), ((), ())), preferred_element_type=F32)


def full_nn(left, right):
    return lax.dot_general(left, right, (((1,), (0,)), ((), ())), precision=HIGHEST, preferred_element_type=F32)


def full_tn(left, right):
    return lax.dot_general(left, right, (((0,), (0,)), ((), ())), precision=HIGHEST, preferred_element_type=F32)


def gram(left, right):
    both = dot_nt(left, right)
    half = both.shape[0] // 2
    return both[:half, :half] + both[:half, half:] + both[half:, :half] + both[half:, half:]


def times(dot, stacked, high, low):
    half = stacked.shape[0] // 2
    first = dot(stacked, high)
    return first[:half] + first[half:] + dot(stacked[:half], low)


def stacked_split(value):
    return jnp.concatenate(split(value), axis=0)


def call(body, out_shape, n_smem, args, scratch=(), aliases=None, limit=12 << 20):
    return pl.pallas_call(
        body,
        out_shape=out_shape,
        in_specs=[SMEM_SPEC] * n_smem + [VMEM_SPEC] * (len(args) - n_smem),
        out_specs=jax.tree.map(lambda _: VMEM_SPEC, out_shape),
        scratch_shapes=list(scratch),
        name=body.__name__,
        input_output_aliases=aliases or {},
        compiler_params=pltpu.CompilerParams(vmem_limit_bytes=limit),
    )(*args[:n_smem], *[in_vmem(a) for a in args[n_smem:]])


def prepare_body(couplings, c_high, c_low, token):
    per = couplings.shape[0]
    first = pl.program_id(0) * per
    token[...] = jnp.zeros_like(token)
    for place in range(per):
        high, low = split(couplings[place])
        c_high[first + place] = high
        c_low[first + place] = low


def prepare(couplings, part):
    count, width = couplings.shape[0] // HALVES, couplings.shape[1]
    steps = count // CHUNK
    half = pltpu.VMEM((count, width, width), BF16)
    return pl.pallas_call(
        prepare_body,
        grid=(steps,),
        in_specs=[pl.BlockSpec((CHUNK, width, width), lambda i: (i + part * steps, 0, 0))],
        out_specs=[VMEM_SPEC] * 3,
        out_shape=[half, half, TOKEN],
        name="prepare",
        compiler_params=pltpu.CompilerParams(vmem_limit_bytes=12 << 20),
    )(in_hbm(couplings))


def block_of(source, q, width):
    return source[q] if len(source.shape) == 3 else source[:, q * width:(q + 1) * width]


def stack_body(*refs):
    first, second, out = refs[-3:]
    blocks, width = out.shape[1], out.shape[3]
    for slot, source in enumerate((first, second)):
        for q in range(blocks):
            out[slot, q] = block_of(source, q, width)


def accumulate(dot, far, routes, near, source_row, target_row, source, target, halves):
    for half in range(HALVES):
        c_high, c_low = halves[2 * half], halves[2 * half + 1]

        def step(chunk, carry):
            terms = []
            for place in range(CHUNK):
                i = chunk * CHUNK + place
                k = routes[half, 0, i]
                terms.append((routes[half, target_row, i], times(dot, source[routes[half, source_row, i]], c_high[k], c_low[k])))
            for row, term in terms:
                target[row] += term
            return carry

        edge = near[half] // CHUNK
        first, last = (edge, routes.shape[2] // CHUNK) if far else (0, edge)
        lax.fori_loop(first, last, step, 0)


def pull_near_body(routes, near, own, ra, rb, ca, cb, *refs):
    *halves, table, strain = refs
    blocks, width = strain.shape[0], strain.shape[2]
    for slot, source in enumerate((own, ra, rb, ca, cb)):
        for q in range(blocks):
            table[slot * blocks + q] = stacked_split(block_of(source, q, width))
    strain[...] = jnp.zeros_like(strain)
    accumulate(dot_nt, False, routes, near, 1, 2, table, strain, halves)


def pull_far_body(routes, near, table_in, strain_in, da, db, *refs):
    halves, refs = refs[:2 * HALVES], refs[2 * HALVES:]
    *grams, table, strain_hl, g_out, strain = refs
    blocks = strain.shape[0]
    for group, source in enumerate((da, db)):
        for slot in range(2):
            for q in range(blocks):
                table[(5 + 2 * group + slot) * blocks + q] = stacked_split(source[slot, q])
    strain[...] = strain_in[...]
    accumulate(dot_nt, True, routes, near, 1, 2, table, strain, halves)
    total = jnp.zeros((strain.shape[1],) * 2, F32)
    for q in range(blocks):
        both = stacked_split(strain[q])
        strain_hl[q] = both
        total += gram(both, both)
    if not grams:
        g_out[...] = total
    else:
        g01, g1, g23 = grams
        size = total.shape[0]
        for i, part in enumerate((g01[0], g01[1] + g1[...], g23[0], g23[1] + total)):
            g_out[:, i * size:(i + 1) * size] = part


def push_far_body(routes, near, strain_hl, *refs):
    halves, (pieces, *targets) = refs[:2 * HALVES], refs[2 * HALVES:]
    blocks = strain_hl.shape[0]
    pieces[...] = jnp.zeros_like(pieces)
    accumulate(dot_nn, True, routes, near, 2, 1, strain_hl, pieces, halves)
    for group, target in enumerate(targets):
        for slot in range(2):
            for q in range(blocks):
                target[slot, q] = pieces[(5 + 2 * group + slot) * blocks + q]


def push_all_body(routes, near, strain_hl, *refs):
    halves, pieces_in = refs[:2 * HALVES], refs[2 * HALVES]
    own, ra, rb, qa, qb, pieces = refs[-6:]
    blocks = strain_hl.shape[0]
    pieces[...] = pieces_in[...]
    accumulate(dot_nn, False, routes, near, 2, 1, strain_hl, pieces, halves)
    for slot, target in enumerate((own, ra, rb)):
        for q in range(blocks):
            target[q] = pieces[slot * blocks + q]
    for group, target in enumerate((qa, qb)):
        for slot, place in enumerate((3 + group, 5 + 2 * group, 6 + 2 * group)):
            for q in range(blocks):
                target[slot, q] = pieces[place * blocks + q]


def push_near_body(routes, near, strain_hl, *refs):
    halves, pieces_in = refs[:2 * HALVES], refs[2 * HALVES]
    own, ra, rb, ca, cb, pieces = refs[-6:]
    blocks = strain_hl.shape[0]
    pieces[...] = pieces_in[:pieces.shape[0]]
    accumulate(dot_nn, False, routes, near, 2, 1, strain_hl, pieces, halves)
    for slot, target in enumerate((own, ra, rb, ca, cb)):
        for q in range(blocks):
            target[q] = pieces[slot * blocks + q]


def diag_body(vector, diag, own, grams):
    size = grams.shape[1]
    first = jnp.zeros((size, size), F32)
    second = jnp.zeros((size, size), F32)
    width = diag.shape[1]
    for q in range(diag.shape[0]):
        both = stacked_split(block_of(vector, q, width))
        term = times(dot_nn, both, *split(diag[q]))
        own[q] = term
        first += gram(both, both)
        second += gram(stacked_split(term), both)
    grams[0] = first
    grams[1] = second


def middle_body(ra, rb, qa, qb, ma, mb):
    ma[...] = ra[...] + qa[0] + qb[0]
    mb[...] = rb[...] + qa[1] + qb[1]


def middle_last_body(own, ra, rb, qa, qb, diag, grams, rest, ma, mb):
    rest[...] = (own[...] + diag[...]) + (qa[0] + qb[0])
    ma[...] = ra[...] + qa[1] + qb[1]
    mb[...] = rb[...] + qa[2] + qb[2]


def sum_body(own, diag, ca, cb, ra, rb, out):
    out[...] = (own[...] + diag[...]) + (ca[...] + cb[...]) + (ra[...] + rb[...])


def eliminated(matrix, right):
    size = matrix.shape[0]
    work = jnp.concatenate([matrix, right], axis=1)
    rows = lax.broadcasted_iota(jnp.int32, work.shape, 0)
    for k in range(0, size, 2):
        upper, lower = work[k:k + 1, :], work[k + 1:k + 2, :]
        upper = upper / upper[:, k:k + 1]
        lower = lower - lower[:, k:k + 1] * upper
        lower = lower / lower[:, k + 1:k + 2]
        upper = upper - upper[:, k + 1:k + 2] * lower
        rest = work - work[:, k:k + 1] * upper - work[:, k + 1:k + 2] * lower
        work = jnp.where(rows == k, upper, jnp.where(rows == k + 1, lower, rest))
    return work[:, size:]


def solve_body(grams, moved, p, q):
    size = grams.shape[0]
    total = grams[...] + moved[...]
    g0, g1, g2, g3 = (total[:, i * size:(i + 1) * size] for i in range(4))
    eye = (lax.broadcasted_iota(jnp.int32, (size, size), 0) == lax.broadcasted_iota(jnp.int32, (size, size), 1)).astype(F32)
    alpha = eliminated(g1, g0)
    inverse = eliminated(g0, eye)
    fresh = (g0 - full_nn(g1, alpha)) - full_tn(alpha, g1 - full_nn(g2, alpha))
    mix = eye + full_nn(inverse, fresh)
    e1 = full_nn(g1, mix) - full_nn(g2, alpha)
    e2 = full_nn(g2, mix) - full_nn(g3, alpha)
    curvature = full_tn(mix, e1) - full_tn(alpha, e2)
    second = eliminated(curvature, fresh)
    p[...] = alpha + full_nn(mix, second)
    q[...] = full_nn(alpha, second)


def finish_body(p, q, right, u, rest, ra, rb, x_out, r_out):
    width = u.shape[2]
    for block in range(u.shape[0]):
        lanes = slice(block * width, (block + 1) * width)
        w = rest[block] + ra[block] + rb[block]
        x_out[:, lanes] = full_tn(p[...], right[:, lanes]) - full_tn(q[...], u[block])
        r_out[:, lanes] = right[:, lanes] - full_tn(p[...], u[block]) + full_tn(q[...], w)


MASKS = (2, 8, 24, 32, 96, 1, 6)


def exchanged(value, mask):
    count = lax.axis_size("row") * lax.axis_size("col")
    return lax.ppermute(value, ("row", "col"), [(i, i ^ mask) for i in range(count)])


def routing(pair_index, blocks):
    count = pair_index.shape[1]
    col_size = lax.axis_size("col")
    my_row, my_col = lax.axis_index("row"), lax.axis_index("col")
    local_row = pair_index[0] - (my_row * col_size + my_col) * blocks
    owner = pair_index[1] // blocks
    row_slot = slot_of(owner // col_size, my_row)
    col_slot = slot_of(owner % col_size, my_col)
    far = (row_slot > 0) & (col_slot > 0)
    slot = jnp.where(far, 2 + 2 * col_slot + row_slot, jnp.where(col_slot > 0, 2 + col_slot, row_slot))
    table_row = slot * blocks + pair_index[1] % blocks
    count = count // HALVES
    number = jnp.arange(count, dtype=jnp.int32)
    far = far.reshape(HALVES, count)
    key = jnp.where(far, count, 0) + number
    rank = jnp.sum((key[:, None, :] < key[:, :, None]).astype(jnp.int32), axis=2)
    placed = rank[:, None, :] == number[:, None]
    columns = [jnp.broadcast_to(number, far.shape), table_row.reshape(far.shape), local_row.reshape(far.shape)]
    routes = jnp.stack([jnp.sum(jnp.where(placed, c[:, None, :], 0), axis=2) for c in columns], axis=1)
    near = count - jnp.sum(far.astype(jnp.int32), axis=1)
    return routes, near


def per_device(right_sides, diag_blocks, couplings, pair_index):
    blocks, width = diag_blocks.shape[0], diag_blocks.shape[1]
    rows = right_sides.shape[0]
    block_shape = pltpu.VMEM((blocks, rows, width), F32)
    stack_shape = pltpu.VMEM((3, blocks, rows, width), F32)
    pair_shape = pltpu.VMEM((2, blocks, rows, width), F32)
    table_shape = pltpu.VMEM((9 * blocks, 2 * rows, width), BF16)
    split_shape = pltpu.VMEM((blocks, 2 * rows, width), BF16)
    pieces_shape = pltpu.VMEM((9 * blocks, rows, width), F32)
    near_pieces_shape = pltpu.VMEM((5 * blocks, rows, width), F32)
    gram_shape = pltpu.VMEM((rows, rows), F32)
    grams_shape = pltpu.VMEM((2, rows, rows), F32)
    all_grams_shape = pltpu.VMEM((rows, 4 * rows), F32)

    def spread(vector, *after):
        ra, rb = swapped(vector, "row", 0), swapped(vector, "row", 1)
        ca, cb = swapped(vector, "col", 0), swapped(vector, "col", 1)
        both = call(stack_body, pair_shape, 0, (after or (ca, cb)) + (ra, rb))
        return (vector, ra, rb, ca, cb), swapped(both, "col", 0), swapped(both, "col", 1)

    def pulled(near_tables, da, db, split_couplings, *grams):
        table, strain = call(pull_near_body, [table_shape, block_shape], 2, (routes, near, *near_tables, *split_couplings))
        _, strain_hl, g = call(
            pull_far_body, [table_shape, split_shape, all_grams_shape if grams else gram_shape], 2,
            (routes, near, table, strain, da, db, *split_couplings, *grams), [block_shape], aliases={2: 0})
        return strain_hl, g

    def pushed(strain_hl, split_couplings):
        pieces, da, db = call(push_far_body, [pieces_shape, pair_shape, pair_shape], 2, (routes, near, strain_hl, *split_couplings))
        da, db = swapped(da, "col", 0), swapped(db, "col", 1)
        own, ra, rb, ca, cb = call(
            push_near_body, [block_shape] * 5, 2, (routes, near, strain_hl, *split_couplings, pieces), [near_pieces_shape])
        return own, ra, rb, swapped(ca, "col", 0), swapped(cb, "col", 1), da, db

    routes, near = routing(pair_index, blocks)
    *early, token = prepare(couplings, 0)
    near_tables, da, db = spread(right_sides, token)
    *late, _ = prepare(couplings, 1)
    split_couplings = early + late
    strain_hl, g1s = pulled(near_tables, da, db, split_couplings)
    own, ra, rb, ca, cb, da, db = pushed(strain_hl, split_couplings)
    diag, g01 = call(diag_body, [block_shape, grams_shape], 0, (right_sides, diag_blocks))
    ra, rb = call(middle_body, [block_shape] * 2, 0, (ra, rb, da, db))
    ra, rb = swapped(ra, "row", 0), swapped(rb, "row", 1)
    u = call(sum_body, block_shape, 0, (own, diag, ca, cb, ra, rb))

    near_tables, da, db = spread(u)
    diag, g23 = call(diag_body, [block_shape, grams_shape], 0, (u, diag_blocks))
    strain_hl, grams = pulled(near_tables, da, db, split_couplings, g01, g1s, g23)
    pieces, = call(push_far_body, [pieces_shape], 2, (routes, near, strain_hl, *split_couplings))
    grams = grams + exchanged(grams, MASKS[0])
    own, ra, rb, qa, qb = call(
        push_all_body, [block_shape] * 3 + [stack_shape] * 2, 2,
        (routes, near, strain_hl, *split_couplings, pieces, grams), [pieces_shape])
    qa, qb = swapped(qa, "col", 0), swapped(qb, "col", 1)
    for mask in MASKS[1:-1]:
        grams = grams + exchanged(grams, mask)
    moved = exchanged(grams, MASKS[-1])
    rest, ra, rb = call(middle_last_body, [block_shape] * 3, 0, (own, ra, rb, qa, qb, diag, moved))
    ra, rb = swapped(ra, "row", 0), swapped(rb, "row", 1)
    p, q = call(solve_body, [gram_shape] * 2, 0, (grams, moved))
    flat = jax.ShapeDtypeStruct(right_sides.shape, F32)
    return tuple(call(finish_body, [flat, flat], 0, (p, q, right_sides, u, rest, ra, rb)))


def solution(mesh):
    return jax.shard_map(
        per_device,
        mesh=mesh,
        in_specs=(
            P(None, ("row", "col")),
            P(("row", "col"), None, None),
            P(("row", "col"), None, None),
            P(None, ("row", "col")),
        ),
        out_specs=(P(None, ("row", "col")), P(None, ("row", "col"))),
        check_vma=False,
    )
```

```python
import jax
import jax.numpy as jnp
from jax import lax
from jax.experimental import pallas as pl
from jax.experimental.pallas import tpu as pltpu
from jax.sharding import PartitionSpec as P

F32 = jnp.float32
BF16 = jnp.bfloat16
HIGHEST = lax.Precision.HIGHEST
VMEM_SPEC = pl.BlockSpec(memory_space=pltpu.VMEM)
SMEM_SPEC = pl.BlockSpec(memory_space=pltpu.SMEM)
CHUNK = 8
PREPARED = 4
PARTS = 2
NEAR_TABLES = 7
TOKEN = pltpu.VMEM((8, 128), F32)


def in_vmem(value):
    return pltpu.with_memory_space_constraint(value, pltpu.VMEM)


def in_hbm(value):
    return pltpu.with_memory_space_constraint(value, pltpu.HBM)


def pairs_of(count, shift):
    return [(place, (((place + shift) ^ 1) - shift) % count) for place in range(count)]


def swapped(value, axis, shift):
    return lax.ppermute(value, axis, pairs_of(lax.axis_size(axis), shift))


def slot_of(target, mine):
    return jnp.where(target == mine, 0, jnp.where(target == (mine ^ 1), 1, 2))


def split(value):
    high = value.astype(BF16)
    return high, (value - high.astype(F32)).astype(BF16)


def dot_nt(left, right):
    return lax.dot_general(left, right, (((1,), (1,)), ((), ())), preferred_element_type=F32)


def dot_nn(left, right):
    return lax.dot_general(left, right, (((1,), (0,)), ((), ())), preferred_element_type=F32)


def full_nn(left, right):
    return lax.dot_general(left, right, (((1,), (0,)), ((), ())), precision=HIGHEST, preferred_element_type=F32)


def full_tn(left, right):
    return lax.dot_general(left, right, (((0,), (0,)), ((), ())), precision=HIGHEST, preferred_element_type=F32)


def gram(left, right):
    both = dot_nt(left, right)
    half = both.shape[0] // 2
    return both[:half, :half] + both[:half, half:] + both[half:, :half] + both[half:, half:]


def times(dot, stacked, high, low):
    half = stacked.shape[0] // 2
    first = dot(stacked, high)
    return first[:half] + first[half:] + dot(stacked[:half], low)


def stacked_split(value):
    return jnp.concatenate(split(value), axis=0)


def call(body, out_shape, n_smem, args, scratch=(), aliases=None, limit=12 << 20):
    return pl.pallas_call(
        body,
        out_shape=out_shape,
        in_specs=[SMEM_SPEC] * n_smem + [VMEM_SPEC] * (len(args) - n_smem),
        out_specs=jax.tree.map(lambda _: VMEM_SPEC, out_shape),
        scratch_shapes=list(scratch),
        name=body.__name__,
        input_output_aliases=aliases or {},
        compiler_params=pltpu.CompilerParams(vmem_limit_bytes=limit),
    )(*args[:n_smem], *[in_vmem(a) for a in args[n_smem:]])


def prepare_body(couplings, c_high, c_low, token):
    per = couplings.shape[0]
    first = pl.program_id(0) * per
    token[...] = jnp.zeros_like(token)
    for place in range(per):
        high, low = split(couplings[place])
        c_high[first + place] = high
        c_low[first + place] = low


def part_edges(count):
    return (0, count * 5 // (8 * CHUNK) * CHUNK, count)


def prepare(couplings, part):
    width = couplings.shape[1]
    first, last = part_edges(couplings.shape[0])[part:part + 2]
    skip = first // PREPARED
    shape = pltpu.VMEM((last - first, width, width), BF16)
    return pl.pallas_call(
        prepare_body,
        grid=((last - first) // PREPARED,),
        in_specs=[pl.BlockSpec((PREPARED, width, width), lambda i: (i + skip, 0, 0))],
        out_specs=[VMEM_SPEC] * 3,
        out_shape=[shape, shape, TOKEN],
        name="prepare",
        compiler_params=pltpu.CompilerParams(vmem_limit_bytes=12 << 20),
    )(in_hbm(couplings))


def block_of(source, q, width):
    return source[q] if len(source.shape) == 3 else source[:, q * width:(q + 1) * width]


def stack_body(*refs):
    vectors, whole, pair = refs[-5:-2], refs[-2], refs[-1]
    blocks, width = whole.shape[1], whole.shape[3]
    for slot, source in enumerate(vectors):
        for q in range(blocks):
            block = block_of(source, q, width)
            whole[slot, q] = block
            if slot:
                pair[slot - 1, q] = block


def accumulate(dot, late, routes, edges, source_row, target_row, source, target, parts):
    for part in range(PARTS):
        c_high, c_low = parts[2 * part], parts[2 * part + 1]

        def step(chunk, carry):
            terms = []
            for place in range(CHUNK):
                i = chunk * CHUNK + place
                k = routes[0, i]
                terms.append((routes[target_row, i], times(dot, source[routes[source_row, i]], c_high[k], c_low[k])))
            for row, term in terms:
                target[row] += term
            return carry

        low, high = part_edges(routes.shape[1])[part:part + 2]
        middle = edges[part] // CHUNK
        first, last = (middle, high // CHUNK) if late else (low // CHUNK, middle)
        lax.fori_loop(first, last, step, 0)


def pull_near_body(routes, edges, qa, whole, cb, *refs):
    parts, (table, strain) = refs[:2 * PARTS], refs[2 * PARTS:]
    blocks = strain.shape[0]
    for place, (source, slot) in enumerate(
            ((whole, 0), (whole, 1), (whole, 2), (qa, 0), (cb, None), (qa, 1), (qa, 2))):
        for q in range(blocks):
            block = block_of(source, q, strain.shape[2]) if slot is None else source[slot, q]
            table[place * blocks + q] = stacked_split(block)
    strain[...] = jnp.zeros_like(strain)
    accumulate(dot_nt, False, routes, edges, 1, 2, table, strain, parts)


def pull_late_body(routes, edges, table_in, strain_in, db, *refs):
    parts, refs = refs[:2 * PARTS], refs[2 * PARTS:]
    *grams, table, strain_hl, g_out, strain = refs
    blocks = strain.shape[0]
    for slot in range(2):
        for q in range(blocks):
            table[(NEAR_TABLES + slot) * blocks + q] = stacked_split(db[slot, q])
    strain[...] = strain_in[...]
    accumulate(dot_nt, True, routes, edges, 1, 2, table, strain, parts)
    total = jnp.zeros((strain.shape[1],) * 2, F32)
    for q in range(blocks):
        both = stacked_split(strain[q])
        strain_hl[q] = both
        total += gram(both, both)
    if not grams:
        g_out[...] = total
    else:
        g01, g1, g23 = grams
        size = total.shape[0]
        for i, part in enumerate((g01[0], g01[1] + g1[...], g23[0], g23[1] + total)):
            g_out[:, i * size:(i + 1) * size] = part


def push_late_body(routes, edges, strain_hl, *refs):
    parts, (pieces, *targets) = refs[:2 * PARTS], refs[2 * PARTS:]
    blocks = strain_hl.shape[0]
    pieces[...] = jnp.zeros_like(pieces)
    accumulate(dot_nn, True, routes, edges, 2, 1, strain_hl, pieces, parts)
    for db in targets:
        for slot in range(2):
            for q in range(blocks):
                db[slot, q] = pieces[(NEAR_TABLES + slot) * blocks + q]


def push_near(routes, edges, strain_hl, parts, pieces_in, pieces, targets):
    blocks = strain_hl.shape[0]
    pieces[...] = pieces_in[:pieces.shape[0]]
    accumulate(dot_nn, False, routes, edges, 2, 1, strain_hl, pieces, parts)
    for target, place in targets:
        for q in range(blocks):
            target[q] = pieces[place * blocks + q]


def push_near_body(routes, edges, strain_hl, *refs):
    parts, pieces_in, outs = refs[:2 * PARTS], refs[2 * PARTS], refs[2 * PARTS + 1:]
    *outs, pieces = outs
    push_near(routes, edges, strain_hl, parts, pieces_in, pieces, zip(outs, range(NEAR_TABLES)))


def push_last_body(routes, edges, strain_hl, *refs):
    parts, pieces_in, outs = refs[:2 * PARTS], refs[2 * PARTS], refs[2 * PARTS + 2:]
    *outs, qa, qb, pieces = outs
    outs += [qa.at[0], qa.at[1], qa.at[2], qb.at[0], qb.at[1], qb.at[2]]
    push_near(routes, edges, strain_hl, parts, pieces_in, pieces, zip(outs, (0, 1, 2, 3, 5, 6, 4, 7, 8)))


def diag_body(vector, diag, own, grams):
    size = grams.shape[1]
    first = jnp.zeros((size, size), F32)
    second = jnp.zeros((size, size), F32)
    width = diag.shape[1]
    for q in range(diag.shape[0]):
        both = stacked_split(block_of(vector, q, width))
        term = times(dot_nn, both, *split(diag[q]))
        own[q] = term
        first += gram(both, both)
        second += gram(stacked_split(term), both)
    grams[0] = first
    grams[1] = second


def middle_early_body(ra, rb, qa_first, qa_second, db, ma, mb):
    ma[...] = ra[...] + qa_first[...] + db[0]
    mb[...] = rb[...] + qa_second[...] + db[1]


def middle_last_body(own, diag, ra, rb, qa, qb, grams, rest, ma, mb):
    rest[...] = (own[...] + diag[...]) + (qa[0] + qb[0])
    ma[...] = ra[...] + qa[1] + qb[1]
    mb[...] = rb[...] + qa[2] + qb[2]


def sum_body(own, diag, ca, cb, ra, rb, out):
    out[...] = (own[...] + diag[...]) + (ca[...] + cb[...]) + (ra[...] + rb[...])


def eliminated(matrix, right):
    size = matrix.shape[0]
    on_diagonal = lax.broadcasted_iota(jnp.int32, (size, size), 0) == lax.broadcasted_iota(jnp.int32, (size, size), 1)
    diagonal = jnp.where(on_diagonal, matrix, 0.0)
    across = lax.rsqrt(jnp.sum(diagonal, axis=0, keepdims=True))
    down = lax.rsqrt(jnp.sum(diagonal, axis=1, keepdims=True))
    work = jnp.concatenate([matrix * down * across, right * down], axis=1)
    rows = lax.broadcasted_iota(jnp.int32, work.shape, 0)
    for k in range(0, size, 2):
        first = jnp.broadcast_to(work[:, k:k + 1], work.shape)
        second = jnp.broadcast_to(work[:, k + 1:k + 2], work.shape)
        upper, lower = work[k:k + 1, :], work[k + 1:k + 2, :]
        a, b, c, d = first[k:k + 1], second[k:k + 1], first[k + 1:k + 2], second[k + 1:k + 2]
        inverse = 1.0 / (a * d - b * c)
        new_upper = (d * upper - b * lower) * inverse
        new_lower = (a * lower - c * upper) * inverse
        rest = work - first * new_upper - second * new_lower
        work = jnp.where(rows == k, new_upper, jnp.where(rows == k + 1, new_lower, rest))
    return work[:, size:] * down


def solve_body(grams, moved, p, q):
    size = grams.shape[0]
    total = grams[...] + moved[...]
    g0, g1, g2, g3 = (total[:, i * size:(i + 1) * size] for i in range(4))
    eye = (lax.broadcasted_iota(jnp.int32, (size, size), 0) == lax.broadcasted_iota(jnp.int32, (size, size), 1)).astype(F32)
    alpha = eliminated(g1, g0)
    inverse = eliminated(g0, eye)
    fresh = (g0 - full_nn(g1, alpha)) - full_tn(alpha, g1 - full_nn(g2, alpha))
    mix = eye + full_nn(inverse, fresh)
    e1 = full_nn(g1, mix) - full_nn(g2, alpha)
    e2 = full_nn(g2, mix) - full_nn(g3, alpha)
    curvature = full_tn(mix, e1) - full_tn(alpha, e2)
    second = eliminated(curvature, fresh)
    p[...] = alpha + full_nn(mix, second)
    q[...] = full_nn(alpha, second)


def finish_body(p, q, right, u, rest, ra, rb, x_out, r_out):
    width = u.shape[2]
    for block in range(u.shape[0]):
        lanes = slice(block * width, (block + 1) * width)
        w = rest[block] + ra[block] + rb[block]
        x_out[:, lanes] = full_tn(p[...], right[:, lanes]) - full_tn(q[...], u[block])
        r_out[:, lanes] = right[:, lanes] - full_tn(p[...], u[block]) + full_tn(q[...], w)


MASKS = (2, 8, 24, 32, 96, 1, 6)


def exchanged(value, mask):
    count = lax.axis_size("row") * lax.axis_size("col")
    return lax.ppermute(value, ("row", "col"), [(i, i ^ mask) for i in range(count)])


def routing(pair_index, blocks):
    count = pair_index.shape[1]
    col_size = lax.axis_size("col")
    my_row, my_col = lax.axis_index("row"), lax.axis_index("col")
    local_row = pair_index[0] - (my_row * col_size + my_col) * blocks
    owner = pair_index[1] // blocks
    row_slot = slot_of(owner // col_size, my_row)
    col_slot = slot_of(owner % col_size, my_col)
    diagonal = (row_slot > 0) & (col_slot > 0)
    slot = jnp.where(diagonal, 2 + 2 * col_slot + row_slot, jnp.where(col_slot > 0, 2 + col_slot, row_slot))
    table_row = slot * blocks + pair_index[1] % blocks
    late = slot >= NEAR_TABLES
    number = jnp.arange(count, dtype=jnp.int32)
    split_at = part_edges(count)[1]
    part = (number >= split_at).astype(jnp.int32)
    key = (2 * part + late.astype(jnp.int32)) * count + number
    rank = jnp.sum((key[None, :] < key[:, None]).astype(jnp.int32), axis=1)
    placed = rank[None, :] == number[:, None]
    columns = (number - part * split_at, table_row, local_row)
    routes = jnp.stack([jnp.sum(jnp.where(placed, c[None, :], 0), axis=1) for c in columns])
    starts = jnp.arange(PARTS, dtype=jnp.int32)
    early = (part[None, :] == starts[:, None]) & ~late[None, :]
    edges = starts * split_at + jnp.sum(early.astype(jnp.int32), axis=1)
    return routes, edges


def per_device(right_sides, diag_blocks, couplings, pair_index):
    blocks, width = diag_blocks.shape[0], diag_blocks.shape[1]
    rows = right_sides.shape[0]
    block_shape = pltpu.VMEM((blocks, rows, width), F32)
    stack_shape = pltpu.VMEM((3, blocks, rows, width), F32)
    pair_shape = pltpu.VMEM((2, blocks, rows, width), F32)
    table_shape = pltpu.VMEM((9 * blocks, 2 * rows, width), BF16)
    split_shape = pltpu.VMEM((blocks, 2 * rows, width), BF16)
    pieces_shape = pltpu.VMEM((9 * blocks, rows, width), F32)
    near_pieces_shape = pltpu.VMEM((NEAR_TABLES * blocks, rows, width), F32)
    gram_shape = pltpu.VMEM((rows, rows), F32)
    grams_shape = pltpu.VMEM((2, rows, rows), F32)
    all_grams_shape = pltpu.VMEM((rows, 4 * rows), F32)

    def spread(vector, *after):
        cb = swapped(vector, "col", 1)
        ra, rb = swapped(vector, "row", 0), swapped(vector, "row", 1)
        whole, pair = call(stack_body, [stack_shape, pair_shape], 0, (after or (cb,)) + (vector, ra, rb))
        return (swapped(whole, "col", 0), whole, cb), swapped(pair, "col", 1)

    def pulled(near_tables, db, couplings, *grams):
        table, strain = call(pull_near_body, [table_shape, block_shape], 2, (routes, edges, *near_tables, *couplings))
        _, strain_hl, g = call(
            pull_late_body, [table_shape, split_shape, all_grams_shape if grams else gram_shape], 2,
            (routes, edges, table, strain, db, *couplings, *grams), [block_shape], aliases={2: 0})
        return strain_hl, g

    routes, edges = routing(pair_index, blocks)
    *larger, token = prepare(couplings, 0)
    near_tables, db = spread(right_sides, token)
    *smaller, _ = prepare(couplings, 1)
    couplings = larger + smaller
    strain_hl, g1s = pulled(near_tables, db, couplings)

    pieces, db = call(push_late_body, [pieces_shape, pair_shape], 2, (routes, edges, strain_hl, *couplings))
    db = swapped(db, "col", 1)
    own, ra, rb, ca, cb, qa_first, qa_second = call(
        push_near_body, [block_shape] * NEAR_TABLES, 2,
        (routes, edges, strain_hl, *couplings, pieces), [near_pieces_shape])
    ca, qa_first, qa_second = (swapped(a, "col", 0) for a in (ca, qa_first, qa_second))
    cb = swapped(cb, "col", 1)
    diag, g01 = call(diag_body, [block_shape, grams_shape], 0, (right_sides, diag_blocks))
    ra, rb = call(middle_early_body, [block_shape] * 2, 0, (ra, rb, qa_first, qa_second, db))
    ra, rb = swapped(ra, "row", 0), swapped(rb, "row", 1)
    u = call(sum_body, block_shape, 0, (own, diag, ca, cb, ra, rb))

    near_tables, db = spread(u)
    diag, g23 = call(diag_body, [block_shape, grams_shape], 0, (u, diag_blocks))
    strain_hl, grams = pulled(near_tables, db, couplings, g01, g1s, g23)
    pieces, = call(push_late_body, [pieces_shape], 2, (routes, edges, strain_hl, *couplings))
    grams = grams + exchanged(grams, MASKS[0])
    own, ra, rb, qa, qb = call(
        push_last_body, [block_shape] * 3 + [stack_shape] * 2, 2,
        (routes, edges, strain_hl, *couplings, pieces, grams), [pieces_shape])
    qa, qb = swapped(qa, "col", 0), swapped(qb, "col", 1)
    for mask in MASKS[1:4]:
        grams = grams + exchanged(grams, mask)
    rest, ra, rb = call(middle_last_body, [block_shape] * 3, 0, (own, diag, ra, rb, qa, qb, grams))
    ra, rb = swapped(ra, "row", 0), swapped(rb, "row", 1)
    for mask in MASKS[4:-1]:
        grams = grams + exchanged(grams, mask)
    p, q = call(solve_body, [gram_shape] * 2, 0, (grams, exchanged(grams, MASKS[-1])))
    flat = jax.ShapeDtypeStruct(right_sides.shape, F32)
    return tuple(call(finish_body, [flat, flat], 0, (p, q, right_sides, u, rest, ra, rb)))


def solution(mesh):
    return jax.shard_map(
        per_device,
        mesh=mesh,
        in_specs=(
            P(None, ("row", "col")),
            P(("row", "col"), None, None),
            P(("row", "col"), None, None),
            P(None, ("row", "col")),
        ),
        out_specs=(P(None, ("row", "col")), P(None, ("row", "col"))),
        check_vma=False,
    )
```

```python
import jax
import jax.numpy as jnp
from jax import lax
from jax.experimental import pallas as pl
from jax.experimental.pallas import tpu as pltpu
from jax.sharding import PartitionSpec as P

F32 = jnp.float32
BF16 = jnp.bfloat16
HIGHEST = lax.Precision.HIGHEST
VMEM_SPEC = pl.BlockSpec(memory_space=pltpu.VMEM)
SMEM_SPEC = pl.BlockSpec(memory_space=pltpu.SMEM)
CHUNK = 8
HALF = 4
PREPARED = 8
NEAR_TABLES = 7
TOKEN = pltpu.VMEM((8, 128), F32)


def in_vmem(value):
    return pltpu.with_memory_space_constraint(value, pltpu.VMEM)


def in_hbm(value):
    return pltpu.with_memory_space_constraint(value, pltpu.HBM)


def pairs_of(count, shift):
    return [(place, (((place + shift) ^ 1) - shift) % count) for place in range(count)]


def swapped(value, axis, shift):
    return lax.ppermute(value, axis, pairs_of(lax.axis_size(axis), shift))


def slot_of(target, mine):
    return jnp.where(target == mine, 0, jnp.where(target == (mine ^ 1), 1, 2))


def split(value):
    high = value.astype(BF16)
    return high, (value - high.astype(F32)).astype(BF16)


def dot_nt(left, right):
    return lax.dot_general(left, right, (((1,), (1,)), ((), ())), preferred_element_type=F32)


def dot_nn(left, right):
    return lax.dot_general(left, right, (((1,), (0,)), ((), ())), preferred_element_type=F32)


def full_nn(left, right):
    return lax.dot_general(left, right, (((1,), (0,)), ((), ())), precision=HIGHEST, preferred_element_type=F32)


def full_tn(left, right):
    return lax.dot_general(left, right, (((0,), (0,)), ((), ())), precision=HIGHEST, preferred_element_type=F32)


def gram(left, right):
    both = dot_nt(left, right)
    half = both.shape[0] // 2
    return both[:half, :half] + both[:half, half:] + both[half:, :half] + both[half:, half:]


def times(dot, stacked, high, low):
    half = stacked.shape[0] // 2
    first = dot(stacked, high)
    return first[:half] + first[half:] + dot(stacked[:half], low)


def stacked_split(value):
    return jnp.concatenate(split(value), axis=0)


def call(body, out_shape, n_smem, args, scratch=(), aliases=None, limit=8 << 20):
    return pl.pallas_call(
        body,
        out_shape=out_shape,
        in_specs=[SMEM_SPEC] * n_smem + [VMEM_SPEC] * (len(args) - n_smem),
        out_specs=jax.tree.map(lambda _: VMEM_SPEC, out_shape),
        scratch_shapes=list(scratch),
        name=body.__name__,
        input_output_aliases=aliases or {},
        compiler_params=pltpu.CompilerParams(vmem_limit_bytes=limit),
    )(*args[:n_smem], *[in_vmem(a) for a in args[n_smem:]])


def prepare_body(routes, edge, couplings, c_high, c_low, token, buffer, arrived):
    count = couplings.shape[0]
    token[...] = jnp.zeros_like(token)
    copies = []
    for i in range(count // PREPARED):
        part = pl.ds(i * PREPARED, PREPARED)
        copies.append(pltpu.make_async_copy(couplings.at[part], buffer.at[part], arrived.at[i]))
    for copy in copies:
        copy.start()
    for i, copy in enumerate(copies):
        copy.wait()
        for k in range(i * PREPARED, (i + 1) * PREPARED):
            c_high[k], c_low[k] = split(buffer[k])


def prepare(couplings, routes, edge):
    shape = pltpu.VMEM(couplings.shape, BF16)
    return pl.pallas_call(
        prepare_body,
        in_specs=[SMEM_SPEC, SMEM_SPEC, pl.BlockSpec(memory_space=pltpu.HBM)],
        out_specs=[VMEM_SPEC] * 3,
        out_shape=[shape, shape, TOKEN],
        scratch_shapes=[
            pltpu.VMEM(couplings.shape, F32),
            pltpu.SemaphoreType.DMA((couplings.shape[0] // PREPARED,)),
        ],
        name="prepare",
        compiler_params=pltpu.CompilerParams(vmem_limit_bytes=17 << 20),
    )(routes, edge, in_hbm(couplings))


def block_of(source, q, width):
    return source[q] if len(source.shape) == 3 else source[:, q * width:(q + 1) * width]


def stack_body(*refs):
    vectors, whole, pair = refs[-5:-2], refs[-2], refs[-1]
    blocks, width = whole.shape[1], whole.shape[3]
    for slot, source in enumerate(vectors):
        for q in range(blocks):
            block = block_of(source, q, width)
            whole[slot, q] = block
            if slot:
                pair[slot - 1, q] = block


def accumulate(dot, first, last, routes, source_row, target_row, source, target, c_high, c_low):
    def step(size, start):
        terms = []
        for place in range(size):
            i = start + place
            k = routes[0, i]
            terms.append((routes[target_row, i], times(dot, source[routes[source_row, i]], c_high[k], c_low[k])))
        for row, term in terms:
            target[row] += term

    def whole(i, carry):
        step(CHUNK, first * HALF + i * CHUNK)
        return carry

    def rest(i, carry):
        step(HALF, (last - 1) * HALF)
        return carry

    lax.fori_loop(0, (last - first) // 2, whole, 0)
    lax.fori_loop(0, (last - first) % 2, rest, 0)


def pull_near_body(routes, edge, qa, whole, cb, *refs):
    c_high, c_low, table, strain = refs
    blocks = strain.shape[0]
    for place, (source, slot) in enumerate(
            ((whole, 0), (whole, 1), (whole, 2), (qa, 0), (cb, None), (qa, 1), (qa, 2))):
        for q in range(blocks):
            block = block_of(source, q, strain.shape[2]) if slot is None else source[slot, q]
            table[place * blocks + q] = stacked_split(block)
    strain[...] = jnp.zeros_like(strain)
    accumulate(dot_nt, 0, edge[0], routes, 1, 2, table, strain, c_high, c_low)


def pull_late_body(routes, edge, table_in, strain_in, db, *refs):
    c_high, c_low, *grams, table, strain_hl, g_out, strain = refs
    blocks = strain.shape[0]
    for slot in range(2):
        for q in range(blocks):
            table[(NEAR_TABLES + slot) * blocks + q] = stacked_split(db[slot, q])
    strain[...] = strain_in[...]
    accumulate(dot_nt, edge[0], routes.shape[1] // HALF, routes, 1, 2, table, strain, c_high, c_low)
    total = jnp.zeros((strain.shape[1],) * 2, F32)
    for q in range(blocks):
        both = stacked_split(strain[q])
        strain_hl[q] = both
        total += gram(both, both)
    if not grams:
        g_out[...] = total
    else:
        g01, g1, g23 = grams
        size = total.shape[0]
        for i, part in enumerate((g01[0], g01[1] + g1[...], g23[0], g23[1] + total)):
            g_out[:, i * size:(i + 1) * size] = part


def push_late_body(routes, edge, strain_hl, c_high, c_low, pieces, *targets):
    blocks = strain_hl.shape[0]
    pieces[...] = jnp.zeros_like(pieces)
    accumulate(dot_nn, edge[0], routes.shape[1] // HALF, routes, 2, 1, strain_hl, pieces, c_high, c_low)
    for db in targets:
        for slot in range(2):
            for q in range(blocks):
                db[slot, q] = pieces[(NEAR_TABLES + slot) * blocks + q]


def push_near_body(routes, edge, strain_hl, c_high, c_low, pieces_in, *refs):
    *outs, pieces = refs
    pieces[...] = pieces_in[:pieces.shape[0]]
    accumulate(dot_nn, 0, edge[0], routes, 2, 1, strain_hl, pieces, c_high, c_low)
    for place, target in enumerate(outs):
        for q in range(target.shape[0]):
            target[q] = pieces[place * target.shape[0] + q]


def push_begin_body(routes, edge, strain_hl, c_high, c_low, pieces_in, pieces):
    accumulate(dot_nn, 0, edge[0] // 2, routes, 2, 1, strain_hl, pieces, c_high, c_low)


def push_end_body(routes, edge, strain_hl, c_high, c_low, pieces_in, own, ra, rb, qa, qb, pieces):
    blocks = strain_hl.shape[0]
    accumulate(dot_nn, edge[0] // 2, edge[0], routes, 2, 1, strain_hl, pieces, c_high, c_low)
    outs = (own, ra, rb, qa.at[0], qa.at[1], qa.at[2], qb.at[0], qb.at[1], qb.at[2])
    for target, place in zip(outs, (0, 1, 2, 3, 5, 6, 4, 7, 8)):
        for q in range(blocks):
            target[q] = pieces[place * blocks + q]


def add_body(grams, moved, after, total):
    total[...] = grams[...] + moved[...]


def diag_body(vector, diag, own, grams):
    size = grams.shape[1]
    first = jnp.zeros((size, size), F32)
    second = jnp.zeros((size, size), F32)
    width = diag.shape[1]
    for q in range(diag.shape[0]):
        both = stacked_split(block_of(vector, q, width))
        term = times(dot_nn, both, *split(diag[q]))
        own[q] = term
        first += gram(both, both)
        second += gram(stacked_split(term), both)
    grams[0] = first
    grams[1] = second


def middle_early_body(ra, rb, qa_first, qa_second, db, ma, mb):
    ma[...] = ra[...] + qa_first[...] + db[0]
    mb[...] = rb[...] + qa_second[...] + db[1]


def middle_last_body(own, diag, ra, rb, qa, qb, grams, rest, ma, mb):
    rest[...] = (own[...] + diag[...]) + (qa[0] + qb[0])
    ma[...] = ra[...] + qa[1] + qb[1]
    mb[...] = rb[...] + qa[2] + qb[2]


def sum_body(own, diag, ca, cb, ra, rb, out):
    out[...] = (own[...] + diag[...]) + (ca[...] + cb[...]) + (ra[...] + rb[...])


def eliminated(matrix, right):
    size = matrix.shape[0]
    on_diagonal = lax.broadcasted_iota(jnp.int32, (size, size), 0) == lax.broadcasted_iota(jnp.int32, (size, size), 1)
    diagonal = jnp.where(on_diagonal, matrix, 0.0)
    across = lax.rsqrt(jnp.sum(diagonal, axis=0, keepdims=True))
    down = lax.rsqrt(jnp.sum(diagonal, axis=1, keepdims=True))
    work = jnp.concatenate([matrix * down * across, right * down], axis=1)
    rows = lax.broadcasted_iota(jnp.int32, work.shape, 0)
    for k in range(0, size, 2):
        first = jnp.broadcast_to(work[:, k:k + 1], work.shape)
        second = jnp.broadcast_to(work[:, k + 1:k + 2], work.shape)
        upper, lower = work[k:k + 1, :], work[k + 1:k + 2, :]
        a, b, c, d = first[k:k + 1], second[k:k + 1], first[k + 1:k + 2], second[k + 1:k + 2]
        inverse = 1.0 / (a * d - b * c)
        new_upper = (d * upper - b * lower) * inverse
        new_lower = (a * lower - c * upper) * inverse
        rest = work - first * new_upper - second * new_lower
        work = jnp.where(rows == k, new_upper, jnp.where(rows == k + 1, new_lower, rest))
    return work[:, size:] * down


def solve_body(grams, moved, p, q):
    size = grams.shape[0]
    total = grams[...] + moved[...]
    g0, g1, g2, g3 = (total[:, i * size:(i + 1) * size] for i in range(4))
    eye = (lax.broadcasted_iota(jnp.int32, (size, size), 0) == lax.broadcasted_iota(jnp.int32, (size, size), 1)).astype(F32)
    alpha = eliminated(g1, g0)
    inverse = eliminated(g0, eye)
    fresh = (g0 - full_nn(g1, alpha)) - full_tn(alpha, g1 - full_nn(g2, alpha))
    mix = eye + full_nn(inverse, fresh)
    e1 = full_nn(g1, mix) - full_nn(g2, alpha)
    e2 = full_nn(g2, mix) - full_nn(g3, alpha)
    curvature = full_tn(mix, e1) - full_tn(alpha, e2)
    second = eliminated(curvature, fresh)
    p[...] = alpha + full_nn(mix, second)
    q[...] = full_nn(alpha, second)


def finish_body(p, q, right, u, rest, ra, rb, x_out, r_out):
    width = u.shape[2]
    for block in range(u.shape[0]):
        lanes = slice(block * width, (block + 1) * width)
        w = rest[block] + ra[block] + rb[block]
        x_out[:, lanes] = full_tn(p[...], right[:, lanes]) - full_tn(q[...], u[block])
        r_out[:, lanes] = right[:, lanes] - full_tn(p[...], u[block]) + full_tn(q[...], w)


MASKS = (2, 6, 8, 24, 32, 96, 1)


def exchanged(value, mask):
    count = lax.axis_size("row") * lax.axis_size("col")
    return lax.ppermute(value, ("row", "col"), [(i, i ^ mask) for i in range(count)])


def routing(pair_index, blocks):
    count = pair_index.shape[1]
    col_size = lax.axis_size("col")
    my_row, my_col = lax.axis_index("row"), lax.axis_index("col")
    local_row = pair_index[0] - (my_row * col_size + my_col) * blocks
    owner, in_owner = lax.div(pair_index[1], blocks), lax.rem(pair_index[1], blocks)
    row_slot = slot_of(lax.div(owner, col_size), my_row)
    col_slot = slot_of(lax.rem(owner, col_size), my_col)
    diagonal = (row_slot > 0) & (col_slot > 0)
    slot = jnp.where(diagonal, 2 + 2 * col_slot + row_slot, jnp.where(col_slot > 0, 2 + col_slot, row_slot))
    table_row = slot * blocks + in_owner
    late = (slot >= NEAR_TABLES).astype(jnp.int32)
    number = jnp.arange(count, dtype=jnp.int32)
    rank = jnp.sum(((late * count + number)[None, :] < (late * count + number)[:, None]).astype(jnp.int32), axis=1)
    placed = rank[None, :] == number[:, None]
    columns = (number, table_row, local_row)
    routes = jnp.stack([jnp.sum(jnp.where(placed, c[None, :], 0), axis=1) for c in columns])
    edge = (count - jnp.sum(late, keepdims=True)) >> (HALF.bit_length() - 1)
    return routes, edge


def per_device(right_sides, diag_blocks, couplings, pair_index):
    blocks, width = diag_blocks.shape[0], diag_blocks.shape[1]
    rows = right_sides.shape[0]
    block_shape = pltpu.VMEM((blocks, rows, width), F32)
    stack_shape = pltpu.VMEM((3, blocks, rows, width), F32)
    pair_shape = pltpu.VMEM((2, blocks, rows, width), F32)
    table_shape = pltpu.VMEM((9 * blocks, 2 * rows, width), BF16)
    split_shape = pltpu.VMEM((blocks, 2 * rows, width), BF16)
    pieces_shape = pltpu.VMEM((9 * blocks, rows, width), F32)
    near_pieces_shape = pltpu.VMEM((NEAR_TABLES * blocks, rows, width), F32)
    gram_shape = pltpu.VMEM((rows, rows), F32)
    grams_shape = pltpu.VMEM((2, rows, rows), F32)
    all_grams_shape = pltpu.VMEM((rows, 4 * rows), F32)

    def spread(vector, *after):
        cb = swapped(vector, "col", 1)
        ra, rb = swapped(vector, "row", 0), swapped(vector, "row", 1)
        whole, pair = call(stack_body, [stack_shape, pair_shape], 0, (*after, cb, vector, ra, rb))
        return (swapped(whole, "col", 0), whole, cb), swapped(pair, "col", 1)

    def pulled(near_tables, db, couplings, *grams):
        table, strain = call(pull_near_body, [table_shape, block_shape], 2, (routes, edge, *near_tables, *couplings))
        _, strain_hl, g = call(
            pull_late_body, [table_shape, split_shape, all_grams_shape if grams else gram_shape], 2,
            (routes, edge, table, strain, db, *couplings, *grams), [block_shape], aliases={2: 0})
        return strain_hl, g

    routes, edge = routing(pair_index, blocks)
    *couplings, token = prepare(couplings, routes, edge)
    near_tables, db = spread(right_sides, token)
    strain_hl, g1s = pulled(near_tables, db, couplings)

    pieces, db = call(push_late_body, [pieces_shape, pair_shape], 2, (routes, edge, strain_hl, *couplings))
    db = swapped(db, "col", 1)
    own, ra, rb, ca, cb, qa_first, qa_second = call(
        push_near_body, [block_shape] * NEAR_TABLES, 2,
        (routes, edge, strain_hl, *couplings, pieces), [near_pieces_shape])
    ca, qa_first, qa_second = (swapped(a, "col", 0) for a in (ca, qa_first, qa_second))
    cb = swapped(cb, "col", 1)
    diag, g01 = call(diag_body, [block_shape, grams_shape], 0, (right_sides, diag_blocks))
    ra, rb = call(middle_early_body, [block_shape] * 2, 0, (ra, rb, qa_first, qa_second, db))
    ra, rb = swapped(ra, "row", 0), swapped(rb, "row", 1)
    u = call(sum_body, block_shape, 0, (own, diag, ca, cb, ra, rb))

    near_tables, db = spread(u)
    diag, g23 = call(diag_body, [block_shape, grams_shape], 0, (u, diag_blocks))
    strain_hl, grams = pulled(near_tables, db, couplings, g01, g1s, g23)
    pieces, = call(push_late_body, [pieces_shape], 2, (routes, edge, strain_hl, *couplings))
    grams = call(add_body, all_grams_shape, 0, (grams, exchanged(grams, MASKS[0]), pieces))
    pieces, = call(push_begin_body, [pieces_shape], 2, (routes, edge, strain_hl, *couplings, pieces), aliases={5: 0})
    grams = call(add_body, all_grams_shape, 0, (grams, exchanged(grams, MASKS[1]), pieces))
    own, ra, rb, qa, qb, _ = call(
        push_end_body, [block_shape] * 3 + [stack_shape] * 2 + [pieces_shape], 2,
        (routes, edge, strain_hl, *couplings, pieces), aliases={5: 5})
    grams = call(add_body, all_grams_shape, 0, (grams, exchanged(grams, MASKS[2]), own))
    qa, qb = swapped(qa, "col", 0), swapped(qb, "col", 1)
    for mask in MASKS[3:6]:
        grams = grams + exchanged(grams, mask)
    rest, ra, rb = call(middle_last_body, [block_shape] * 3, 0, (own, diag, ra, rb, qa, qb, grams))
    ra, rb = swapped(ra, "row", 0), swapped(rb, "row", 1)
    p, q = call(solve_body, [gram_shape] * 2, 0, (grams, exchanged(grams, MASKS[-1])))
    flat = jax.ShapeDtypeStruct(right_sides.shape, F32)
    return tuple(call(finish_body, [flat, flat], 0, (p, q, right_sides, u, rest, ra, rb)))


def solution(mesh):
    return jax.shard_map(
        per_device,
        mesh=mesh,
        in_specs=(
            P(None, ("row", "col")),
            P(("row", "col"), None, None),
            P(("row", "col"), None, None),
            P(None, ("row", "col")),
        ),
        out_specs=(P(None, ("row", "col")), P(None, ("row", "col"))),
        check_vma=False,
    )
```

```python
import functools

import jax
import jax.numpy as jnp
from jax import lax
from jax.experimental import pallas as pl
from jax.experimental.pallas import tpu as pltpu
from jax.sharding import PartitionSpec as P

F32 = jnp.float32
BF16 = jnp.bfloat16
HIGHEST = lax.Precision.HIGHEST
VMEM_SPEC = pl.BlockSpec(memory_space=pltpu.VMEM)
SMEM_SPEC = pl.BlockSpec(memory_space=pltpu.SMEM)
CHUNK = 8
HALF = 4
PREPARED = 8
NEAR_TABLES = 7


def in_vmem(value):
    return pltpu.with_memory_space_constraint(value, pltpu.VMEM)


def in_hbm(value):
    return pltpu.with_memory_space_constraint(value, pltpu.HBM)


def pairs_of(count, shift):
    return [(place, (((place + shift) ^ 1) - shift) % count) for place in range(count)]


def swapped(value, axis, shift):
    return lax.ppermute(value, axis, pairs_of(lax.axis_size(axis), shift))


def slot_of(target, mine):
    return jnp.where(target == mine, 0, jnp.where(target == (mine ^ 1), 1, 2))


def split(value):
    high = value.astype(BF16)
    return high, (value - high.astype(F32)).astype(BF16)


def dot_nt(left, right):
    return lax.dot_general(left, right, (((1,), (1,)), ((), ())), preferred_element_type=F32)


def dot_nn(left, right):
    return lax.dot_general(left, right, (((1,), (0,)), ((), ())), preferred_element_type=F32)


def full_nn(left, right):
    return lax.dot_general(left, right, (((1,), (0,)), ((), ())), precision=HIGHEST, preferred_element_type=F32)


def full_tn(left, right):
    return lax.dot_general(left, right, (((0,), (0,)), ((), ())), precision=HIGHEST, preferred_element_type=F32)


def gram(left, right):
    both = dot_nt(left, right)
    half = both.shape[0] // 2
    return both[:half, :half] + both[:half, half:] + both[half:, :half] + both[half:, half:]


def times(dot, stacked, high, low):
    half = stacked.shape[0] // 2
    first = dot(stacked, high)
    return first[:half] + first[half:] + dot(stacked[:half], low)


def stacked_split(value):
    return jnp.concatenate(split(value), axis=0)


def call(body, out_shape, n_smem, args, scratch=(), aliases=None, limit=8 << 20):
    return pl.pallas_call(
        body,
        out_shape=out_shape,
        in_specs=[SMEM_SPEC] * n_smem + [VMEM_SPEC] * (len(args) - n_smem),
        out_specs=jax.tree.map(lambda _: VMEM_SPEC, out_shape),
        scratch_shapes=list(scratch),
        name=body.__name__,
        input_output_aliases=aliases or {},
        compiler_params=pltpu.CompilerParams(vmem_limit_bytes=limit),
    )(*args[:n_smem], *[in_vmem(a) for a in args[n_smem:]])


def route(pair, routes, blocks):
    count = pair.shape[1]
    block_bits, col_bits = blocks.bit_length() - 1, lax.axis_size("col").bit_length() - 1
    my_row, my_col = lax.axis_index("row"), lax.axis_index("col")
    row_of, col_of = pair[0:1, :], pair[1:2, :]
    owner = col_of >> block_bits
    row_slot = slot_of(owner >> col_bits, my_row)
    col_slot = slot_of(owner & (lax.axis_size("col") - 1), my_col)
    diagonal = (row_slot > 0) & (col_slot > 0)
    slot = jnp.where(diagonal, 2 + 2 * col_slot + row_slot, jnp.where(col_slot > 0, 2 + col_slot, row_slot))
    table_row = slot * blocks + (col_of & (blocks - 1))
    local_row = row_of & (blocks - 1)
    number = lax.broadcasted_iota(jnp.int32, (1, count), 1)
    late = jnp.where(slot >= NEAR_TABLES, 1, 0)
    key = (late * count + number).astype(F32)
    square = (count, count)
    down, across = (lax.broadcasted_iota(jnp.int32, square, axis) for axis in (0, 1))

    def upright(value):
        return jnp.sum(jnp.where(down == across, value.astype(F32), 0.0), axis=1, keepdims=True)

    rank = jnp.sum(jnp.where(key < upright(key), 1.0, 0.0), axis=1, keepdims=True)
    placed = rank == across.astype(F32)
    for i, value in enumerate((number, table_row, local_row)):
        routes[i:i + 1, :] = jnp.sum(jnp.where(placed, upright(value), 0.0), axis=0, keepdims=True).astype(jnp.int32)
    near = count - jnp.sum(late.astype(F32), axis=1, keepdims=True).astype(jnp.int32)
    routes[3:4, :] = jnp.broadcast_to(near >> (HALF.bit_length() - 1), (1, count))


def prepare_body(blocks, pair, couplings, c_high, c_low, routes, buffer, arrived):
    count = couplings.shape[0]
    copies = []
    for i in range(count // PREPARED):
        part = pl.ds(i * PREPARED, PREPARED)
        copies.append(pltpu.make_async_copy(couplings.at[part], buffer.at[part], arrived.at[i]))
    for copy in copies:
        copy.start()
    route(pair, routes, blocks)
    for i, copy in enumerate(copies):
        copy.wait()
        for k in range(i * PREPARED, (i + 1) * PREPARED):
            c_high[k], c_low[k] = split(buffer[k])


def prepare(pair_index, couplings, blocks):
    shape = pltpu.VMEM(couplings.shape, BF16)
    return pl.pallas_call(
        functools.partial(prepare_body, blocks),
        in_specs=[VMEM_SPEC, pl.BlockSpec(memory_space=pltpu.HBM)],
        out_specs=[VMEM_SPEC] * 3,
        out_shape=[shape, shape, pltpu.VMEM((4, pair_index.shape[1]), jnp.int32)],
        scratch_shapes=[
            pltpu.VMEM(couplings.shape, F32),
            pltpu.SemaphoreType.DMA((couplings.shape[0] // PREPARED,)),
        ],
        name="prepare",
        compiler_params=pltpu.CompilerParams(vmem_limit_bytes=18 << 20),
    )(in_vmem(pair_index), in_hbm(couplings))


def block_of(source, q, width):
    return source[q] if len(source.shape) == 3 else source[:, q * width:(q + 1) * width]


def stack_body(*refs):
    vectors, whole, pair = refs[-5:-2], refs[-2], refs[-1]
    blocks, width = whole.shape[1], whole.shape[3]
    for slot, source in enumerate(vectors):
        for q in range(blocks):
            block = block_of(source, q, width)
            whole[slot, q] = block
            if slot:
                pair[slot - 1, q] = block


def accumulate(dot, first, last, routes, source_row, target_row, source, target, c_high, c_low):
    def step(size, start):
        terms = []
        for place in range(size):
            i = start + place
            k = routes[0, i]
            terms.append((routes[target_row, i], times(dot, source[routes[source_row, i]], c_high[k], c_low[k])))
        for row, term in terms:
            target[row] += term

    def whole(i, carry):
        step(CHUNK, first * HALF + i * CHUNK)
        return carry

    def rest(i, carry):
        step(HALF, (last - 1) * HALF)
        return carry

    lax.fori_loop(0, (last - first) // 2, whole, 0)
    lax.fori_loop(0, (last - first) % 2, rest, 0)


def pull_near_body(routes, qa, whole, cb, *refs):
    c_high, c_low, table, strain = refs
    blocks = strain.shape[0]
    for place, (source, slot) in enumerate(
            ((whole, 0), (whole, 1), (whole, 2), (qa, 0), (cb, None), (qa, 1), (qa, 2))):
        for q in range(blocks):
            block = block_of(source, q, strain.shape[2]) if slot is None else source[slot, q]
            table[place * blocks + q] = stacked_split(block)
    strain[...] = jnp.zeros_like(strain)
    accumulate(dot_nt, 0, routes[3, 0], routes, 1, 2, table, strain, c_high, c_low)


def pull_late_body(routes, table_in, strain_in, db, *refs):
    c_high, c_low, *grams, table, strain_hl, g_out, strain = refs
    blocks = strain.shape[0]
    for slot in range(2):
        for q in range(blocks):
            table[(NEAR_TABLES + slot) * blocks + q] = stacked_split(db[slot, q])
    strain[...] = strain_in[...]
    accumulate(dot_nt, routes[3, 0], routes.shape[1] // HALF, routes, 1, 2, table, strain, c_high, c_low)
    total = jnp.zeros((strain.shape[1],) * 2, F32)
    for q in range(blocks):
        both = stacked_split(strain[q])
        strain_hl[q] = both
        total += gram(both, both)
    if not grams:
        g_out[...] = total
    else:
        g01, g1, g23 = grams
        size = total.shape[0]
        for i, part in enumerate((g01[0], g01[1] + g1[...], g23[0], g23[1] + total)):
            g_out[:, i * size:(i + 1) * size] = part


def push_late_body(routes, strain_hl, c_high, c_low, pieces, *targets):
    blocks = strain_hl.shape[0]
    pieces[...] = jnp.zeros_like(pieces)
    accumulate(dot_nn, routes[3, 0], routes.shape[1] // HALF, routes, 2, 1, strain_hl, pieces, c_high, c_low)
    for db in targets:
        for slot in range(2):
            for q in range(blocks):
                db[slot, q] = pieces[(NEAR_TABLES + slot) * blocks + q]


def push_near_body(routes, strain_hl, c_high, c_low, pieces_in, *refs):
    *outs, pieces = refs
    pieces[...] = pieces_in[:pieces.shape[0]]
    accumulate(dot_nn, 0, routes[3, 0], routes, 2, 1, strain_hl, pieces, c_high, c_low)
    for place, target in enumerate(outs):
        for q in range(target.shape[0]):
            target[q] = pieces[place * target.shape[0] + q]


def push_begin_body(routes, strain_hl, c_high, c_low, pieces_in, pieces):
    accumulate(dot_nn, 0, routes[3, 0] // 2, routes, 2, 1, strain_hl, pieces, c_high, c_low)


def push_end_body(routes, strain_hl, c_high, c_low, pieces_in, pieces):
    accumulate(dot_nn, routes[3, 0] // 2, routes[3, 0], routes, 2, 1, strain_hl, pieces, c_high, c_low)


def pack_body(pieces, grams, moved, own, ra, rb, qa, qb, total):
    total[...] = grams[...] + moved[...]
    blocks = own.shape[0]
    outs = (own, ra, rb, qa.at[0], qa.at[1], qa.at[2], qb.at[0], qb.at[1], qb.at[2])
    for target, place in zip(outs, (0, 1, 2, 3, 5, 6, 4, 7, 8)):
        for q in range(blocks):
            target[q] = pieces[place * blocks + q]


def add_body(grams, moved, after, total):
    total[...] = grams[...] + moved[...]


def diag_body(vector, diag, own, grams):
    size = grams.shape[1]
    first = jnp.zeros((size, size), F32)
    second = jnp.zeros((size, size), F32)
    width = diag.shape[1]
    for q in range(diag.shape[0]):
        both = stacked_split(block_of(vector, q, width))
        term = times(dot_nn, both, *split(diag[q]))
        own[q] = term
        first += gram(both, both)
        second += gram(stacked_split(term), both)
    grams[0] = first
    grams[1] = second


def middle_early_body(ra, rb, qa_first, qa_second, db, ma, mb):
    ma[...] = ra[...] + qa_first[...] + db[0]
    mb[...] = rb[...] + qa_second[...] + db[1]


def middle_last_body(own, diag, ra, rb, qa, qb, grams, rest, ma, mb):
    rest[...] = (own[...] + diag[...]) + (qa[0] + qb[0])
    ma[...] = ra[...] + qa[1] + qb[1]
    mb[...] = rb[...] + qa[2] + qb[2]


def sum_body(own, diag, ca, cb, ra, rb, out):
    out[...] = (own[...] + diag[...]) + (ca[...] + cb[...]) + (ra[...] + rb[...])


def eliminated(matrix, right):
    size = matrix.shape[0]
    on_diagonal = lax.broadcasted_iota(jnp.int32, (size, size), 0) == lax.broadcasted_iota(jnp.int32, (size, size), 1)
    diagonal = jnp.where(on_diagonal, matrix, 0.0)
    across = lax.rsqrt(jnp.sum(diagonal, axis=0, keepdims=True))
    down = lax.rsqrt(jnp.sum(diagonal, axis=1, keepdims=True))
    work = jnp.concatenate([matrix * down * across, right * down], axis=1)
    rows = lax.broadcasted_iota(jnp.int32, work.shape, 0)
    for k in range(0, size, 2):
        first = jnp.broadcast_to(work[:, k:k + 1], work.shape)
        second = jnp.broadcast_to(work[:, k + 1:k + 2], work.shape)
        upper, lower = work[k:k + 1, :], work[k + 1:k + 2, :]
        a, b, c, d = first[k:k + 1], second[k:k + 1], first[k + 1:k + 2], second[k + 1:k + 2]
        inverse = 1.0 / (a * d - b * c)
        new_upper = (d * upper - b * lower) * inverse
        new_lower = (a * lower - c * upper) * inverse
        rest = work - first * new_upper - second * new_lower
        work = jnp.where(rows == k, new_upper, jnp.where(rows == k + 1, new_lower, rest))
    return work[:, size:] * down


def solve_body(grams, moved, p, q):
    size = grams.shape[0]
    total = grams[...] + moved[...]
    g0, g1, g2, g3 = (total[:, i * size:(i + 1) * size] for i in range(4))
    eye = (lax.broadcasted_iota(jnp.int32, (size, size), 0) == lax.broadcasted_iota(jnp.int32, (size, size), 1)).astype(F32)
    alpha = eliminated(g1, g0)
    inverse = eliminated(g0, eye)
    fresh = (g0 - full_nn(g1, alpha)) - full_tn(alpha, g1 - full_nn(g2, alpha))
    mix = eye + full_nn(inverse, fresh)
    e1 = full_nn(g1, mix) - full_nn(g2, alpha)
    e2 = full_nn(g2, mix) - full_nn(g3, alpha)
    curvature = full_tn(mix, e1) - full_tn(alpha, e2)
    second = eliminated(curvature, fresh)
    p[...] = alpha + full_nn(mix, second)
    q[...] = full_nn(alpha, second)


def finish_body(p, q, right, u, rest, ra, rb, x_out, r_out):
    width = u.shape[2]
    for block in range(u.shape[0]):
        lanes = slice(block * width, (block + 1) * width)
        w = rest[block] + ra[block] + rb[block]
        x_out[:, lanes] = full_tn(p[...], right[:, lanes]) - full_tn(q[...], u[block])
        r_out[:, lanes] = right[:, lanes] - full_tn(p[...], u[block]) + full_tn(q[...], w)


MASKS = (2, 6, 8, 24, 1)
RING = (32, 96, 64)


def exchanged(value, mask):
    count = lax.axis_size("row") * lax.axis_size("col")
    return lax.ppermute(value, ("row", "col"), [(i, i ^ mask) for i in range(count)])


def per_device(right_sides, diag_blocks, couplings, pair_index):
    blocks, width = diag_blocks.shape[0], diag_blocks.shape[1]
    rows = right_sides.shape[0]
    block_shape = pltpu.VMEM((blocks, rows, width), F32)
    stack_shape = pltpu.VMEM((3, blocks, rows, width), F32)
    pair_shape = pltpu.VMEM((2, blocks, rows, width), F32)
    table_shape = pltpu.VMEM((9 * blocks, 2 * rows, width), BF16)
    split_shape = pltpu.VMEM((blocks, 2 * rows, width), BF16)
    pieces_shape = pltpu.VMEM((9 * blocks, rows, width), F32)
    near_pieces_shape = pltpu.VMEM((NEAR_TABLES * blocks, rows, width), F32)
    gram_shape = pltpu.VMEM((rows, rows), F32)
    grams_shape = pltpu.VMEM((2, rows, rows), F32)
    all_grams_shape = pltpu.VMEM((rows, 4 * rows), F32)

    def spread(vector, *after):
        cb = swapped(vector, "col", 1)
        ra, rb = swapped(vector, "row", 0), swapped(vector, "row", 1)
        whole, pair = call(stack_body, [stack_shape, pair_shape], 0, (*after, cb, vector, ra, rb))
        return (swapped(whole, "col", 0), whole, cb), swapped(pair, "col", 1)

    def pulled(near_tables, db, couplings, *grams):
        table, strain = call(pull_near_body, [table_shape, block_shape], 1, (routes, *near_tables, *couplings))
        _, strain_hl, g = call(
            pull_late_body, [table_shape, split_shape, all_grams_shape if grams else gram_shape], 1,
            (routes, table, strain, db, *couplings, *grams), [block_shape], aliases={1: 0})
        return strain_hl, g

    *couplings, routes = prepare(pair_index, couplings, blocks)
    near_tables, db = spread(right_sides, routes)
    strain_hl, g1s = pulled(near_tables, db, couplings)

    pieces, db = call(push_late_body, [pieces_shape, pair_shape], 1, (routes, strain_hl, *couplings))
    db = swapped(db, "col", 1)
    own, ra, rb, ca, cb, qa_first, qa_second = call(
        push_near_body, [block_shape] * NEAR_TABLES, 1,
        (routes, strain_hl, *couplings, pieces), [near_pieces_shape])
    ca, qa_first, qa_second = (swapped(a, "col", 0) for a in (ca, qa_first, qa_second))
    cb = swapped(cb, "col", 1)
    diag, g01 = call(diag_body, [block_shape, grams_shape], 0, (right_sides, diag_blocks))
    ra, rb = call(middle_early_body, [block_shape] * 2, 0, (ra, rb, qa_first, qa_second, db))
    ra, rb = swapped(ra, "row", 0), swapped(rb, "row", 1)
    u = call(sum_body, block_shape, 0, (own, diag, ca, cb, ra, rb))

    diag, g23 = call(diag_body, [block_shape, grams_shape], 0, (u, diag_blocks))
    near_tables, db = spread(u, g23)
    strain_hl, grams = pulled(near_tables, db, couplings, g01, g1s, g23)
    pieces, = call(push_late_body, [pieces_shape], 1, (routes, strain_hl, *couplings))
    grams = call(add_body, all_grams_shape, 0, (grams, exchanged(grams, MASKS[0]), pieces))
    pieces, = call(push_begin_body, [pieces_shape], 1, (routes, strain_hl, *couplings, pieces), aliases={4: 0})
    grams = call(add_body, all_grams_shape, 0, (grams, exchanged(grams, MASKS[1]), pieces))
    pieces, = call(push_end_body, [pieces_shape], 1, (routes, strain_hl, *couplings, pieces), aliases={4: 0})
    own, ra, rb, qa, qb, grams = call(
        pack_body, [block_shape] * 3 + [stack_shape] * 2 + [all_grams_shape], 0,
        (pieces, grams, exchanged(grams, MASKS[2])))
    qa, qb = swapped(qa, "col", 0), swapped(qb, "col", 1)
    grams = grams + exchanged(grams, MASKS[3])
    first, second, third = (exchanged(grams, mask) for mask in RING)
    grams = (grams + first) + (second + third)
    rest, ra, rb = call(middle_last_body, [block_shape] * 3, 0, (own, diag, ra, rb, qa, qb, grams))
    ra, rb = swapped(ra, "row", 0), swapped(rb, "row", 1)
    p, q = call(solve_body, [gram_shape] * 2, 0, (grams, exchanged(grams, MASKS[-1])))
    flat = jax.ShapeDtypeStruct(right_sides.shape, F32)
    return tuple(call(finish_body, [flat, flat], 0, (p, q, right_sides, u, rest, ra, rb)))


def solution(mesh):
    return jax.shard_map(
        per_device,
        mesh=mesh,
        in_specs=(
            P(None, ("row", "col")),
            P(("row", "col"), None, None),
            P(("row", "col"), None, None),
            P(None, ("row", "col")),
        ),
        out_specs=(P(None, ("row", "col")), P(None, ("row", "col"))),
        check_vma=False,
    )
```

```python
import functools

import jax
import jax.numpy as jnp
from jax import lax
from jax.experimental import pallas as pl
from jax.experimental.pallas import tpu as pltpu
from jax.sharding import PartitionSpec as P

F32 = jnp.float32
BF16 = jnp.bfloat16
HIGHEST = lax.Precision.HIGHEST
VMEM_SPEC = pl.BlockSpec(memory_space=pltpu.VMEM)
SMEM_SPEC = pl.BlockSpec(memory_space=pltpu.SMEM)
CHUNK = 8
HALF = 4
PREPARED = 8
SLOTS = 3
NEAR_TABLES = 7


def in_vmem(value):
    return pltpu.with_memory_space_constraint(value, pltpu.VMEM)


def in_hbm(value):
    return pltpu.with_memory_space_constraint(value, pltpu.HBM)


def pairs_of(count, shift):
    return [(place, (((place + shift) ^ 1) - shift) % count) for place in range(count)]


def swapped(value, axis, shift):
    return lax.ppermute(value, axis, pairs_of(lax.axis_size(axis), shift))


def slot_of(target, mine):
    return jnp.where(target == mine, 0, jnp.where(target == (mine ^ 1), 1, 2))


def split(value):
    high = value.astype(BF16)
    return high, (value - high.astype(F32)).astype(BF16)


def dot_nt(left, right):
    return lax.dot_general(left, right, (((1,), (1,)), ((), ())), preferred_element_type=F32)


def dot_nn(left, right):
    return lax.dot_general(left, right, (((1,), (0,)), ((), ())), preferred_element_type=F32)


def full_nn(left, right):
    return lax.dot_general(left, right, (((1,), (0,)), ((), ())), precision=HIGHEST, preferred_element_type=F32)


def full_tn(left, right):
    return lax.dot_general(left, right, (((0,), (0,)), ((), ())), precision=HIGHEST, preferred_element_type=F32)


def gram(left, right):
    both = dot_nt(left, right)
    half = both.shape[0] // 2
    return both[:half, :half] + both[:half, half:] + both[half:, :half] + both[half:, half:]


def times(stacked, high, low):
    half = stacked.shape[0] // 2
    first = dot_nn(stacked, high)
    return first[:half] + first[half:] + dot_nn(stacked[:half], low)


def stacked_split(value):
    return jnp.concatenate(split(value), axis=0)


def call(body, out_shape, n_smem, args, scratch=(), aliases=None, limit=4 << 20):
    return pl.pallas_call(
        body,
        out_shape=out_shape,
        in_specs=[SMEM_SPEC] * n_smem + [VMEM_SPEC] * (len(args) - n_smem),
        out_specs=jax.tree.map(lambda _: VMEM_SPEC, out_shape),
        scratch_shapes=list(scratch),
        name=body.__name__,
        input_output_aliases=aliases or {},
        compiler_params=pltpu.CompilerParams(vmem_limit_bytes=limit),
    )(*args[:n_smem], *[in_vmem(a) for a in args[n_smem:]])


def route(pair, routes, blocks):
    count = pair.shape[1]
    block_bits, col_bits = blocks.bit_length() - 1, lax.axis_size("col").bit_length() - 1
    my_row, my_col = lax.axis_index("row"), lax.axis_index("col")
    row_of, col_of = pair[0:1, :], pair[1:2, :]
    owner = col_of >> block_bits
    row_slot = slot_of(owner >> col_bits, my_row)
    col_slot = slot_of(owner & (lax.axis_size("col") - 1), my_col)
    diagonal = (row_slot > 0) & (col_slot > 0)
    slot = jnp.where(diagonal, 2 + 2 * col_slot + row_slot, jnp.where(col_slot > 0, 2 + col_slot, row_slot))
    table_row = slot * blocks + (col_of & (blocks - 1))
    local_row = row_of & (blocks - 1)
    number = lax.broadcasted_iota(jnp.int32, (1, count), 1)
    late = jnp.where(slot >= NEAR_TABLES, 1, 0)
    key = (late * count + number).astype(F32)
    square = (count, count)
    down, across = (lax.broadcasted_iota(jnp.int32, square, axis) for axis in (0, 1))

    def upright(value):
        return jnp.sum(jnp.where(down == across, value.astype(F32), 0.0), axis=1, keepdims=True)

    rank = jnp.sum(jnp.where(key < upright(key), 1.0, 0.0), axis=1, keepdims=True)
    placed = rank == across.astype(F32)
    for i, value in enumerate((number, table_row, local_row)):
        routes[i:i + 1, :] = jnp.sum(jnp.where(placed, upright(value), 0.0), axis=0, keepdims=True).astype(jnp.int32)
    near = count - jnp.sum(late.astype(F32), axis=1, keepdims=True).astype(jnp.int32)
    routes[3:4, :] = jnp.broadcast_to(near >> (HALF.bit_length() - 1), (1, count))


def prepare_body(blocks, pair, couplings, c_high, c_low, t_high, t_low, routes, buffer, arrived):
    groups = couplings.shape[0] // PREPARED
    copies = [
        pltpu.make_async_copy(
            couplings.at[pl.ds(i * PREPARED, PREPARED)], buffer.at[i % SLOTS], arrived.at[i])
        for i in range(groups)
    ]
    for copy in copies[:SLOTS]:
        copy.start()
    route(pair, routes, blocks)
    for i, copy in enumerate(copies):
        copy.wait()
        for place in range(PREPARED):
            k = i * PREPARED + place
            high, low = split(buffer[i % SLOTS, place])
            c_high[k], c_low[k] = high, low
            t_high[k], t_low[k] = high.T, low.T
        if i + SLOTS < groups:
            copies[i + SLOTS].start()


def prepare(pair_index, couplings, blocks):
    count, width = couplings.shape[:2]
    shape = pltpu.VMEM(couplings.shape, BF16)
    return pl.pallas_call(
        functools.partial(prepare_body, blocks),
        in_specs=[VMEM_SPEC, pl.BlockSpec(memory_space=pltpu.HBM)],
        out_specs=[VMEM_SPEC] * 5,
        out_shape=[shape] * 4 + [pltpu.VMEM((4, count), jnp.int32)],
        scratch_shapes=[
            pltpu.VMEM((SLOTS, PREPARED, width, width), F32),
            pltpu.SemaphoreType.DMA((count // PREPARED,)),
        ],
        name="prepare",
        compiler_params=pltpu.CompilerParams(vmem_limit_bytes=7 << 20),
    )(in_vmem(pair_index), in_hbm(couplings))


def block_of(source, q, width):
    return source[q] if len(source.shape) == 3 else source[:, q * width:(q + 1) * width]


def stack_body(*refs):
    vectors, whole, pair = refs[-5:-2], refs[-2], refs[-1]
    blocks, width = whole.shape[1], whole.shape[3]
    for slot, source in enumerate(vectors):
        for q in range(blocks):
            block = block_of(source, q, width)
            whole[slot, q] = block
            if slot:
                pair[slot - 1, q] = block


def accumulate(first, last, routes, source_row, target_row, source, target, c_high, c_low):
    def step(size, start):
        terms = []
        for place in range(size):
            i = start + place
            k = routes[0, i]
            terms.append((routes[target_row, i], times(source[routes[source_row, i]], c_high[k], c_low[k])))
        for row, term in terms:
            target[row] += term

    def whole(i, carry):
        step(CHUNK, first * HALF + i * CHUNK)
        return carry

    def rest(i, carry):
        step(HALF, (last - 1) * HALF)
        return carry

    lax.fori_loop(0, (last - first) // 2, whole, 0)
    lax.fori_loop(0, (last - first) % 2, rest, 0)


def pull_near_body(routes, qa, whole, cb, *refs):
    c_high, c_low, table, strain = refs
    blocks = strain.shape[0]
    for place, (source, slot) in enumerate(
            ((whole, 0), (whole, 1), (whole, 2), (qa, 0), (cb, None), (qa, 1), (qa, 2))):
        for q in range(blocks):
            block = block_of(source, q, strain.shape[2]) if slot is None else source[slot, q]
            table[place * blocks + q] = stacked_split(block)
    strain[...] = jnp.zeros_like(strain)
    accumulate(0, routes[3, 0], routes, 1, 2, table, strain, c_high, c_low)


def pull_late_body(routes, table_in, strain_in, db, *refs):
    c_high, c_low, *grams, table, strain_hl, g_out, strain = refs
    blocks = strain.shape[0]
    for slot in range(2):
        for q in range(blocks):
            table[(NEAR_TABLES + slot) * blocks + q] = stacked_split(db[slot, q])
    strain[...] = strain_in[...]
    accumulate(routes[3, 0], routes.shape[1] // HALF, routes, 1, 2, table, strain, c_high, c_low)
    total = jnp.zeros((strain.shape[1],) * 2, F32)
    for q in range(blocks):
        both = stacked_split(strain[q])
        strain_hl[q] = both
        total += gram(both, both)
    if not grams:
        g_out[...] = total
    else:
        g01, g1, g23 = grams
        size = total.shape[0]
        for i, part in enumerate((g01[0], g01[1] + g1[...], g23[0], g23[1] + total)):
            g_out[:, i * size:(i + 1) * size] = part


def push_late_body(routes, strain_hl, c_high, c_low, pieces, *targets):
    blocks = strain_hl.shape[0]
    pieces[...] = jnp.zeros_like(pieces)
    accumulate(routes[3, 0], routes.shape[1] // HALF, routes, 2, 1, strain_hl, pieces, c_high, c_low)
    for db in targets:
        for slot in range(2):
            for q in range(blocks):
                db[slot, q] = pieces[(NEAR_TABLES + slot) * blocks + q]


def push_near_body(routes, strain_hl, c_high, c_low, pieces_in, *refs):
    *outs, pieces = refs
    pieces[...] = pieces_in[:pieces.shape[0]]
    accumulate(0, routes[3, 0], routes, 2, 1, strain_hl, pieces, c_high, c_low)
    for place, target in enumerate(outs):
        for q in range(target.shape[0]):
            target[q] = pieces[place * target.shape[0] + q]


def push_begin_body(routes, strain_hl, c_high, c_low, pieces_in, pieces):
    accumulate(0, routes[3, 0] // 2, routes, 2, 1, strain_hl, pieces, c_high, c_low)


def push_end_body(routes, strain_hl, c_high, c_low, pieces_in, pieces):
    accumulate(routes[3, 0] // 2, routes[3, 0], routes, 2, 1, strain_hl, pieces, c_high, c_low)


def pack_body(pieces, grams, own, ra, rb, qa, qb):
    blocks = own.shape[0]
    outs = (own, ra, rb, qa.at[0], qa.at[1], qa.at[2], qb.at[0], qb.at[1], qb.at[2])
    for target, place in zip(outs, (0, 1, 2, 3, 5, 6, 4, 7, 8)):
        for q in range(blocks):
            target[q] = pieces[place * blocks + q]


def add_body(grams, moved, after, total):
    total[...] = grams[...] + moved[...]


def diag_body(vector, diag, own, grams):
    size = grams.shape[1]
    first = jnp.zeros((size, size), F32)
    second = jnp.zeros((size, size), F32)
    width = diag.shape[1]
    for q in range(diag.shape[0]):
        both = stacked_split(block_of(vector, q, width))
        term = times(both, *split(diag[q]))
        own[q] = term
        first += gram(both, both)
        second += gram(stacked_split(term), both)
    grams[0] = first
    grams[1] = second


def middle_early_body(ra, rb, qa_first, qa_second, db, ma, mb):
    ma[...] = ra[...] + qa_first[...] + db[0]
    mb[...] = rb[...] + qa_second[...] + db[1]


def middle_last_body(own, diag, ra, rb, qa, qb, grams, rest, ma, mb):
    rest[...] = (own[...] + diag[...]) + (qa[0] + qb[0])
    ma[...] = ra[...] + qa[1] + qb[1]
    mb[...] = rb[...] + qa[2] + qb[2]


def sum_body(own, diag, ca, cb, ra, rb, out):
    out[...] = (own[...] + diag[...]) + (ca[...] + cb[...]) + (ra[...] + rb[...])


def eliminated(matrix, right):
    size = matrix.shape[0]
    on_diagonal = lax.broadcasted_iota(jnp.int32, (size, size), 0) == lax.broadcasted_iota(jnp.int32, (size, size), 1)
    diagonal = jnp.where(on_diagonal, matrix, 0.0)
    across = lax.rsqrt(jnp.sum(diagonal, axis=0, keepdims=True))
    down = lax.rsqrt(jnp.sum(diagonal, axis=1, keepdims=True))
    work = jnp.concatenate([matrix * down * across, right * down], axis=1)
    rows = lax.broadcasted_iota(jnp.int32, work.shape, 0)
    for k in range(0, size, 2):
        first = jnp.broadcast_to(work[:, k:k + 1], work.shape)
        second = jnp.broadcast_to(work[:, k + 1:k + 2], work.shape)
        upper, lower = work[k:k + 1, :], work[k + 1:k + 2, :]
        a, b, c, d = first[k:k + 1], second[k:k + 1], first[k + 1:k + 2], second[k + 1:k + 2]
        inverse = 1.0 / (a * d - b * c)
        new_upper = (d * upper - b * lower) * inverse
        new_lower = (a * lower - c * upper) * inverse
        rest = work - first * new_upper - second * new_lower
        work = jnp.where(rows == k, new_upper, jnp.where(rows == k + 1, new_lower, rest))
    return work[:, size:] * down


def solve_body(grams, moved, p, q):
    size = grams.shape[0]
    total = grams[...] + moved[...]
    g0, g1, g2, g3 = (total[:, i * size:(i + 1) * size] for i in range(4))
    eye = (lax.broadcasted_iota(jnp.int32, (size, size), 0) == lax.broadcasted_iota(jnp.int32, (size, size), 1)).astype(F32)
    alpha = eliminated(g1, g0)
    inverse = eliminated(g0, eye)
    fresh = (g0 - full_nn(g1, alpha)) - full_tn(alpha, g1 - full_nn(g2, alpha))
    mix = eye + full_nn(inverse, fresh)
    e1 = full_nn(g1, mix) - full_nn(g2, alpha)
    e2 = full_nn(g2, mix) - full_nn(g3, alpha)
    curvature = full_tn(mix, e1) - full_tn(alpha, e2)
    second = eliminated(curvature, fresh)
    p[...] = alpha + full_nn(mix, second)
    q[...] = full_nn(alpha, second)


def finish_body(p, q, right, u, rest, x_out, r_part):
    width = u.shape[2]
    for block in range(u.shape[0]):
        lanes = slice(block * width, (block + 1) * width)
        x_out[:, lanes] = full_tn(p[...], right[:, lanes]) - full_tn(q[...], u[block])
        r_part[block] = right[:, lanes] - full_tn(p[...], u[block]) + full_tn(q[...], rest[block])


def finish_last_body(q, r_part, ra, rb, r_out):
    width = ra.shape[2]
    for block in range(ra.shape[0]):
        lanes = slice(block * width, (block + 1) * width)
        r_out[:, lanes] = r_part[block] + full_tn(q[...], ra[block] + rb[block])


MASKS = (2, 6, 8, 24, 1)
RING = (32, 96, 64)


def exchanged(value, mask):
    count = lax.axis_size("row") * lax.axis_size("col")
    return lax.ppermute(value, ("row", "col"), [(i, i ^ mask) for i in range(count)])


def per_device(right_sides, diag_blocks, couplings, pair_index):
    blocks, width = diag_blocks.shape[0], diag_blocks.shape[1]
    rows = right_sides.shape[0]
    block_shape = pltpu.VMEM((blocks, rows, width), F32)
    stack_shape = pltpu.VMEM((3, blocks, rows, width), F32)
    pair_shape = pltpu.VMEM((2, blocks, rows, width), F32)
    table_shape = pltpu.VMEM((9 * blocks, 2 * rows, width), BF16)
    split_shape = pltpu.VMEM((blocks, 2 * rows, width), BF16)
    pieces_shape = pltpu.VMEM((9 * blocks, rows, width), F32)
    near_pieces_shape = pltpu.VMEM((NEAR_TABLES * blocks, rows, width), F32)
    gram_shape = pltpu.VMEM((rows, rows), F32)
    grams_shape = pltpu.VMEM((2, rows, rows), F32)
    all_grams_shape = pltpu.VMEM((rows, 4 * rows), F32)

    def spread(vector, *after):
        cb = swapped(vector, "col", 1)
        ra, rb = swapped(vector, "row", 0), swapped(vector, "row", 1)
        whole, pair = call(stack_body, [stack_shape, pair_shape], 0, (*after, cb, vector, ra, rb))
        return (swapped(whole, "col", 0), whole, cb), swapped(pair, "col", 1)

    def pulled(near_tables, db, *grams):
        table, strain = call(pull_near_body, [table_shape, block_shape], 1, (routes, *near_tables, *transposes))
        _, strain_hl, g = call(
            pull_late_body, [table_shape, split_shape, all_grams_shape if grams else gram_shape], 1,
            (routes, table, strain, db, *transposes, *grams), [block_shape], aliases={1: 0})
        return strain_hl, g

    *halves, routes = prepare(pair_index, couplings, blocks)
    couplings, transposes = halves[:2], halves[2:]
    near_tables, db = spread(right_sides, routes)
    strain_hl, g1s = pulled(near_tables, db)

    pieces, db = call(push_late_body, [pieces_shape, pair_shape], 1, (routes, strain_hl, *couplings))
    db = swapped(db, "col", 1)
    own, ra, rb, ca, cb, qa_first, qa_second = call(
        push_near_body, [block_shape] * NEAR_TABLES, 1,
        (routes, strain_hl, *couplings, pieces), [near_pieces_shape])
    ca, qa_first, qa_second = (swapped(a, "col", 0) for a in (ca, qa_first, qa_second))
    cb = swapped(cb, "col", 1)
    diag, g01 = call(diag_body, [block_shape, grams_shape], 0, (right_sides, diag_blocks))
    ra, rb = call(middle_early_body, [block_shape] * 2, 0, (ra, rb, qa_first, qa_second, db))
    ra, rb = swapped(ra, "row", 0), swapped(rb, "row", 1)
    u = call(sum_body, block_shape, 0, (own, diag, ca, cb, ra, rb))

    diag, g23 = call(diag_body, [block_shape, grams_shape], 0, (u, diag_blocks))
    near_tables, db = spread(u, g23)
    strain_hl, grams = pulled(near_tables, db, g01, g1s, g23)
    pieces, = call(push_late_body, [pieces_shape], 1, (routes, strain_hl, *couplings))
    grams = call(add_body, all_grams_shape, 0, (grams, exchanged(grams, MASKS[0]), pieces))
    pieces, = call(push_begin_body, [pieces_shape], 1, (routes, strain_hl, *couplings, pieces), aliases={4: 0})
    grams = call(add_body, all_grams_shape, 0, (grams, exchanged(grams, MASKS[1]), pieces))
    pieces, = call(push_end_body, [pieces_shape], 1, (routes, strain_hl, *couplings, pieces), aliases={4: 0})
    grams = call(add_body, all_grams_shape, 0, (grams, exchanged(grams, MASKS[2]), pieces))
    own, ra, rb, qa, qb = call(pack_body, [block_shape] * 3 + [stack_shape] * 2, 0, (pieces, grams))
    qa, qb = swapped(qa, "col", 0), swapped(qb, "col", 1)
    grams = grams + exchanged(grams, MASKS[3])
    first, second, third = (exchanged(grams, mask) for mask in RING)
    grams = (grams + first) + (second + third)
    rest, ra, rb = call(middle_last_body, [block_shape] * 3, 0, (own, diag, ra, rb, qa, qb, grams))
    ra, rb = swapped(ra, "row", 0), swapped(rb, "row", 1)
    p, q = call(solve_body, [gram_shape] * 2, 0, (grams, exchanged(grams, MASKS[-1])))
    flat = jax.ShapeDtypeStruct(right_sides.shape, F32)
    x_out, r_part = call(finish_body, [flat, block_shape], 0, (p, q, right_sides, u, rest))
    return x_out, call(finish_last_body, flat, 0, (q, r_part, ra, rb))


def solution(mesh):
    return jax.shard_map(
        per_device,
        mesh=mesh,
        in_specs=(
            P(None, ("row", "col")),
            P(("row", "col"), None, None),
            P(("row", "col"), None, None),
            P(None, ("row", "col")),
        ),
        out_specs=(P(None, ("row", "col")), P(None, ("row", "col"))),
        check_vma=False,
    )
```

```python
import functools

import jax
import jax.numpy as jnp
from jax import lax
from jax.experimental import pallas as pl
from jax.experimental.pallas import tpu as pltpu
from jax.sharding import PartitionSpec as P

F32 = jnp.float32
BF16 = jnp.bfloat16
HIGHEST = lax.Precision.HIGHEST
VMEM_SPEC = pl.BlockSpec(memory_space=pltpu.VMEM)
SMEM_SPEC = pl.BlockSpec(memory_space=pltpu.SMEM)
CHUNK = 8
HALF = 4
PREPARED = 8
SLOTS = 3
NEAR_TABLES = 7


def in_vmem(value):
    return pltpu.with_memory_space_constraint(value, pltpu.VMEM)


def in_hbm(value):
    return pltpu.with_memory_space_constraint(value, pltpu.HBM)


def pairs_of(count, shift):
    return [(place, (((place + shift) ^ 1) - shift) % count) for place in range(count)]


def swapped(value, axis, shift):
    return lax.ppermute(value, axis, pairs_of(lax.axis_size(axis), shift))


def slot_of(target, mine):
    return jnp.where(target == mine, 0, jnp.where(target == (mine ^ 1), 1, 2))


def split(value):
    high = value.astype(BF16)
    return high, (value - high.astype(F32)).astype(BF16)


def dot_nt(left, right):
    return lax.dot_general(left, right, (((1,), (1,)), ((), ())), preferred_element_type=F32)


def dot_nn(left, right):
    return lax.dot_general(left, right, (((1,), (0,)), ((), ())), preferred_element_type=F32)


def full_nn(left, right):
    return lax.dot_general(left, right, (((1,), (0,)), ((), ())), precision=HIGHEST, preferred_element_type=F32)


def full_tn(left, right):
    return lax.dot_general(left, right, (((0,), (0,)), ((), ())), precision=HIGHEST, preferred_element_type=F32)


def gram(left, right):
    both = dot_nt(left, right)
    half = both.shape[0] // 2
    return both[:half, :half] + both[:half, half:] + both[half:, :half] + both[half:, half:]


def times(stacked, high, low):
    half = stacked.shape[0] // 2
    first = dot_nn(stacked, high)
    return first[:half] + first[half:] + dot_nn(stacked[:half], low)


def stacked_split(value):
    return jnp.concatenate(split(value), axis=0)


def call(body, out_shape, n_smem, args, scratch=(), aliases=None, limit=4 << 20):
    return pl.pallas_call(
        body,
        out_shape=out_shape,
        in_specs=[SMEM_SPEC] * n_smem + [VMEM_SPEC] * (len(args) - n_smem),
        out_specs=jax.tree.map(lambda _: VMEM_SPEC, out_shape),
        scratch_shapes=list(scratch),
        name=body.__name__,
        input_output_aliases=aliases or {},
        compiler_params=pltpu.CompilerParams(vmem_limit_bytes=limit),
    )(*args[:n_smem], *[in_vmem(a) for a in args[n_smem:]])


def route(pair, routes, blocks):
    count = pair.shape[1]
    block_bits, col_bits = blocks.bit_length() - 1, lax.axis_size("col").bit_length() - 1
    my_row, my_col = lax.axis_index("row"), lax.axis_index("col")
    row_of, col_of = pair[0:1, :], pair[1:2, :]
    owner = col_of >> block_bits
    row_slot = slot_of(owner >> col_bits, my_row)
    col_slot = slot_of(owner & (lax.axis_size("col") - 1), my_col)
    diagonal = (row_slot > 0) & (col_slot > 0)
    slot = jnp.where(diagonal, 2 + 2 * col_slot + row_slot, jnp.where(col_slot > 0, 2 + col_slot, row_slot))
    table_row = slot * blocks + (col_of & (blocks - 1))
    local_row = row_of & (blocks - 1)
    number = lax.broadcasted_iota(jnp.int32, (1, count), 1)
    late = jnp.where(slot >= NEAR_TABLES, 1, 0)
    key = (late * count + number).astype(F32)
    square = (count, count)
    down, across = (lax.broadcasted_iota(jnp.int32, square, axis) for axis in (0, 1))

    def upright(value):
        return jnp.sum(jnp.where(down == across, value.astype(F32), 0.0), axis=1, keepdims=True)

    rank = jnp.sum(jnp.where(key < upright(key), 1.0, 0.0), axis=1, keepdims=True)
    placed = rank == across.astype(F32)
    for i, value in enumerate((number, table_row, local_row)):
        routes[i:i + 1, :] = jnp.sum(jnp.where(placed, upright(value), 0.0), axis=0, keepdims=True).astype(jnp.int32)
    near = count - jnp.sum(late.astype(F32), axis=1, keepdims=True).astype(jnp.int32)
    routes[3:4, :] = jnp.broadcast_to(near >> (HALF.bit_length() - 1), (1, count))


def prepare_body(blocks, pair, couplings, c_high, c_low, t_high, t_low, routes, buffer, arrived):
    groups = couplings.shape[0] // PREPARED
    copies = [
        pltpu.make_async_copy(
            couplings.at[pl.ds(i * PREPARED, PREPARED)], buffer.at[i % SLOTS], arrived.at[i])
        for i in range(groups)
    ]
    for copy in copies[:SLOTS]:
        copy.start()
    route(pair, routes, blocks)
    for i, copy in enumerate(copies):
        copy.wait()
        for place in range(PREPARED):
            k = i * PREPARED + place
            high, low = split(buffer[i % SLOTS, place])
            c_high[k], c_low[k] = high, low
            t_high[k], t_low[k] = high.T, low.T
        if i + SLOTS < groups:
            copies[i + SLOTS].start()


def prepare(pair_index, couplings, blocks):
    count, width = couplings.shape[:2]
    shape = pltpu.VMEM(couplings.shape, BF16)
    return pl.pallas_call(
        functools.partial(prepare_body, blocks),
        in_specs=[VMEM_SPEC, pl.BlockSpec(memory_space=pltpu.HBM)],
        out_specs=[VMEM_SPEC] * 5,
        out_shape=[shape] * 4 + [pltpu.VMEM((4, count), jnp.int32)],
        scratch_shapes=[
            pltpu.VMEM((SLOTS, PREPARED, width, width), F32),
            pltpu.SemaphoreType.DMA((count // PREPARED,)),
        ],
        name="prepare",
        compiler_params=pltpu.CompilerParams(vmem_limit_bytes=7 << 20),
    )(in_vmem(pair_index), in_hbm(couplings))


def block_of(source, q, width):
    return source[q] if len(source.shape) == 3 else source[:, q * width:(q + 1) * width]


def stack_body(*refs):
    vectors, whole, pair = refs[-5:-2], refs[-2], refs[-1]
    blocks, width = whole.shape[1], whole.shape[3]
    for slot, source in enumerate(vectors):
        for q in range(blocks):
            block = block_of(source, q, width)
            whole[slot, q] = block
            if slot:
                pair[slot - 1, q] = block


def accumulate(first, last, routes, source_row, target_row, source, target, c_high, c_low):
    def step(size, start):
        terms = []
        for place in range(size):
            i = start + place
            k = routes[0, i]
            terms.append((routes[target_row, i], times(source[routes[source_row, i]], c_high[k], c_low[k])))
        for row, term in terms:
            target[row] += term

    def whole(i, carry):
        step(CHUNK, first * HALF + i * CHUNK)
        return carry

    def rest(i, carry):
        step(HALF, (last - 1) * HALF)
        return carry

    lax.fori_loop(0, (last - first) // 2, whole, 0)
    lax.fori_loop(0, (last - first) % 2, rest, 0)


def pull_near_body(routes, qa, whole, cb, *refs):
    c_high, c_low, table, strain = refs
    blocks = strain.shape[0]
    for place, (source, slot) in enumerate(
            ((whole, 0), (whole, 1), (whole, 2), (qa, 0), (cb, None), (qa, 1), (qa, 2))):
        for q in range(blocks):
            block = block_of(source, q, strain.shape[2]) if slot is None else source[slot, q]
            table[place * blocks + q] = stacked_split(block)
    strain[...] = jnp.zeros_like(strain)
    accumulate(0, routes[3, 0], routes, 1, 2, table, strain, c_high, c_low)


def pull_late_body(routes, table_in, strain_in, db, *refs):
    c_high, c_low, *grams, table, strain_hl, g_out, strain = refs
    blocks = strain.shape[0]
    for slot in range(2):
        for q in range(blocks):
            table[(NEAR_TABLES + slot) * blocks + q] = stacked_split(db[slot, q])
    strain[...] = strain_in[...]
    accumulate(routes[3, 0], routes.shape[1] // HALF, routes, 1, 2, table, strain, c_high, c_low)
    total = jnp.zeros((strain.shape[1],) * 2, F32)
    for q in range(blocks):
        both = stacked_split(strain[q])
        strain_hl[q] = both
        total += gram(both, both)
    if not grams:
        g_out[...] = total
    else:
        g01, g1, g23 = grams
        size = total.shape[0]
        for i, part in enumerate((g01[0], g01[1] + g1[...], g23[0], g23[1] + total)):
            g_out[:, i * size:(i + 1) * size] = part


def push_late_body(routes, strain_hl, c_high, c_low, pieces, *targets):
    blocks = strain_hl.shape[0]
    pieces[...] = jnp.zeros_like(pieces)
    accumulate(routes[3, 0], routes.shape[1] // HALF, routes, 2, 1, strain_hl, pieces, c_high, c_low)
    for db in targets:
        for slot in range(2):
            for q in range(blocks):
                db[slot, q] = pieces[(NEAR_TABLES + slot) * blocks + q]


def push_near_body(routes, strain_hl, c_high, c_low, pieces_in, *refs):
    *outs, pieces = refs
    pieces[...] = pieces_in[:pieces.shape[0]]
    accumulate(0, routes[3, 0], routes, 2, 1, strain_hl, pieces, c_high, c_low)
    for place, target in enumerate(outs):
        for q in range(target.shape[0]):
            target[q] = pieces[place * target.shape[0] + q]


def push_begin_body(routes, strain_hl, c_high, c_low, pieces_in, pieces):
    accumulate(0, routes[3, 0] // 2, routes, 2, 1, strain_hl, pieces, c_high, c_low)


def push_end_body(routes, strain_hl, c_high, c_low, pieces_in, pieces):
    accumulate(routes[3, 0] // 2, routes[3, 0], routes, 2, 1, strain_hl, pieces, c_high, c_low)


def pack_body(pieces, grams, own, ra, rb, qa, qb):
    blocks = own.shape[0]
    outs = (own, ra, rb, qa.at[0], qa.at[1], qa.at[2], qb.at[0], qb.at[1], qb.at[2])
    for target, place in zip(outs, (0, 1, 2, 3, 5, 6, 4, 7, 8)):
        for q in range(blocks):
            target[q] = pieces[place * blocks + q]


def add_body(grams, moved, after, total):
    total[...] = grams[...] + moved[...]


def diag_body(vector, diag, own, grams):
    size = grams.shape[1]
    first = jnp.zeros((size, size), F32)
    second = jnp.zeros((size, size), F32)
    width = diag.shape[1]
    for q in range(diag.shape[0]):
        both = stacked_split(block_of(vector, q, width))
        term = times(both, *split(diag[q]))
        own[q] = term
        first += gram(both, both)
        second += gram(stacked_split(term), both)
    grams[0] = first
    grams[1] = second


def middle_early_body(ra, rb, qa_first, qa_second, db, ma, mb):
    ma[...] = ra[...] + qa_first[...] + db[0]
    mb[...] = rb[...] + qa_second[...] + db[1]


def middle_last_body(own, diag, ra, rb, qa, qb, grams, rest, ma, mb):
    rest[...] = (own[...] + diag[...]) + (qa[0] + qb[0])
    ma[...] = ra[...] + qa[1] + qb[1]
    mb[...] = rb[...] + qa[2] + qb[2]


def sum_body(own, diag, ca, cb, rb, ra, out):
    out[...] = (own[...] + diag[...]) + (ca[...] + cb[...]) + (ra[...] + rb[...])


def eliminated(matrix, right):
    size = matrix.shape[0]
    on_diagonal = lax.broadcasted_iota(jnp.int32, (size, size), 0) == lax.broadcasted_iota(jnp.int32, (size, size), 1)
    diagonal = jnp.where(on_diagonal, matrix, 0.0)
    across = lax.rsqrt(jnp.sum(diagonal, axis=0, keepdims=True))
    down = lax.rsqrt(jnp.sum(diagonal, axis=1, keepdims=True))
    work = jnp.concatenate([matrix * down * across, right * down], axis=1)
    rows = lax.broadcasted_iota(jnp.int32, work.shape, 0)
    for k in range(0, size, 2):
        first = jnp.broadcast_to(work[:, k:k + 1], work.shape)
        second = jnp.broadcast_to(work[:, k + 1:k + 2], work.shape)
        upper, lower = work[k:k + 1, :], work[k + 1:k + 2, :]
        a, b, c, d = first[k:k + 1], second[k:k + 1], first[k + 1:k + 2], second[k + 1:k + 2]
        inverse = 1.0 / (a * d - b * c)
        new_upper = (d * upper - b * lower) * inverse
        new_lower = (a * lower - c * upper) * inverse
        rest = work - first * new_upper - second * new_lower
        work = jnp.where(rows == k, new_upper, jnp.where(rows == k + 1, new_lower, rest))
    return work[:, size:] * down


def solve_body(grams, moved, p, q):
    size = grams.shape[0]
    total = grams[...] + moved[...]
    g0, g1, g2, g3 = (total[:, i * size:(i + 1) * size] for i in range(4))
    eye = (lax.broadcasted_iota(jnp.int32, (size, size), 0) == lax.broadcasted_iota(jnp.int32, (size, size), 1)).astype(F32)
    alpha = eliminated(g1, g0)
    inverse = eliminated(g0, eye)
    fresh = (g0 - full_nn(g1, alpha)) - full_tn(alpha, g1 - full_nn(g2, alpha))
    mix = eye + full_nn(inverse, fresh)
    e1 = full_nn(g1, mix) - full_nn(g2, alpha)
    e2 = full_nn(g2, mix) - full_nn(g3, alpha)
    curvature = full_tn(mix, e1) - full_tn(alpha, e2)
    second = eliminated(curvature, fresh)
    p[...] = alpha + full_nn(mix, second)
    q[...] = full_nn(alpha, second)


def finish_body(p, q, right, u, rest, rb, ra, x_out, r_out):
    width = u.shape[2]
    for block in range(u.shape[0]):
        lanes = slice(block * width, (block + 1) * width)
        w = rest[block] + (ra[block] + rb[block])
        x_out[:, lanes] = full_tn(p[...], right[:, lanes]) - full_tn(q[...], u[block])
        r_out[:, lanes] = right[:, lanes] - full_tn(p[...], u[block]) + full_tn(q[...], w)


MASKS = (2, 6, 32, 96, 8, 1, 24)


def exchanged(value, mask):
    count = lax.axis_size("row") * lax.axis_size("col")
    return lax.ppermute(value, ("row", "col"), [(i, i ^ mask) for i in range(count)])


def per_device(right_sides, diag_blocks, couplings, pair_index):
    blocks, width = diag_blocks.shape[0], diag_blocks.shape[1]
    rows = right_sides.shape[0]
    block_shape = pltpu.VMEM((blocks, rows, width), F32)
    stack_shape = pltpu.VMEM((3, blocks, rows, width), F32)
    pair_shape = pltpu.VMEM((2, blocks, rows, width), F32)
    table_shape = pltpu.VMEM((9 * blocks, 2 * rows, width), BF16)
    split_shape = pltpu.VMEM((blocks, 2 * rows, width), BF16)
    pieces_shape = pltpu.VMEM((9 * blocks, rows, width), F32)
    near_pieces_shape = pltpu.VMEM((NEAR_TABLES * blocks, rows, width), F32)
    gram_shape = pltpu.VMEM((rows, rows), F32)
    grams_shape = pltpu.VMEM((2, rows, rows), F32)
    all_grams_shape = pltpu.VMEM((rows, 4 * rows), F32)

    def spread(vector, *after):
        cb = swapped(vector, "col", 1)
        ra, rb = swapped(vector, "row", 0), swapped(vector, "row", 1)
        whole, pair = call(stack_body, [stack_shape, pair_shape], 0, (*after, cb, vector, ra, rb))
        return (swapped(whole, "col", 0), whole, cb), swapped(pair, "col", 1)

    def pulled(near_tables, db, *grams):
        table, strain = call(pull_near_body, [table_shape, block_shape], 1, (routes, *near_tables, *transposes))
        _, strain_hl, g = call(
            pull_late_body, [table_shape, split_shape, all_grams_shape if grams else gram_shape], 1,
            (routes, table, strain, db, *transposes, *grams), [block_shape], aliases={1: 0})
        return strain_hl, g

    *halves, routes = prepare(pair_index, couplings, blocks)
    couplings, transposes = halves[:2], halves[2:]
    near_tables, db = spread(right_sides, routes)
    strain_hl, g1s = pulled(near_tables, db)

    pieces, db = call(push_late_body, [pieces_shape, pair_shape], 1, (routes, strain_hl, *couplings))
    db = swapped(db, "col", 1)
    own, ra, rb, ca, cb, qa_first, qa_second = call(
        push_near_body, [block_shape] * NEAR_TABLES, 1,
        (routes, strain_hl, *couplings, pieces), [near_pieces_shape])
    ca, qa_first, qa_second = (swapped(a, "col", 0) for a in (ca, qa_first, qa_second))
    cb = swapped(cb, "col", 1)
    diag, g01 = call(diag_body, [block_shape, grams_shape], 0, (right_sides, diag_blocks))
    ra, rb = call(middle_early_body, [block_shape] * 2, 0, (ra, rb, qa_first, qa_second, db))
    rb, ra = swapped(rb, "row", 1), swapped(ra, "row", 0)
    u = call(sum_body, block_shape, 0, (own, diag, ca, cb, rb, ra))

    diag, g23 = call(diag_body, [block_shape, grams_shape], 0, (u, diag_blocks))
    near_tables, db = spread(u, g23)
    strain_hl, grams = pulled(near_tables, db, g01, g1s, g23)
    pieces, = call(push_late_body, [pieces_shape], 1, (routes, strain_hl, *couplings))
    grams = call(add_body, all_grams_shape, 0, (grams, exchanged(grams, MASKS[0]), pieces))
    pieces, = call(push_begin_body, [pieces_shape], 1, (routes, strain_hl, *couplings, pieces), aliases={4: 0})
    grams = call(add_body, all_grams_shape, 0, (grams, exchanged(grams, MASKS[1]), pieces))
    pieces, = call(push_end_body, [pieces_shape], 1, (routes, strain_hl, *couplings, pieces), aliases={4: 0})
    grams = call(add_body, all_grams_shape, 0, (grams, exchanged(grams, MASKS[2]), pieces))
    own, ra, rb, qa, qb = call(pack_body, [block_shape] * 3 + [stack_shape] * 2, 0, (pieces, grams))
    qa, qb = swapped(qa, "col", 0), swapped(qb, "col", 1)
    for mask in MASKS[3:-1]:
        grams = grams + exchanged(grams, mask)
    moved = exchanged(grams, MASKS[-1])
    rest, ra, rb = call(middle_last_body, [block_shape] * 3, 0, (own, diag, ra, rb, qa, qb, moved))
    rb, ra = swapped(rb, "row", 1), swapped(ra, "row", 0)
    p, q = call(solve_body, [gram_shape] * 2, 0, (grams, moved))
    flat = jax.ShapeDtypeStruct(right_sides.shape, F32)
    return tuple(call(finish_body, [flat, flat], 0, (p, q, right_sides, u, rest, rb, ra)))


def solution(mesh):
    return jax.shard_map(
        per_device,
        mesh=mesh,
        in_specs=(
            P(None, ("row", "col")),
            P(("row", "col"), None, None),
            P(("row", "col"), None, None),
            P(None, ("row", "col")),
        ),
        out_specs=(P(None, ("row", "col")), P(None, ("row", "col"))),
        check_vma=False,
    )
```

```python
import functools

import jax
import jax.numpy as jnp
from jax import lax
from jax.experimental import pallas as pl
from jax.experimental.pallas import tpu as pltpu
from jax.sharding import PartitionSpec as P

F32 = jnp.float32
BF16 = jnp.bfloat16
HIGHEST = lax.Precision.HIGHEST
VMEM_SPEC = pl.BlockSpec(memory_space=pltpu.VMEM)
SMEM_SPEC = pl.BlockSpec(memory_space=pltpu.SMEM)
CHUNK = 8
HALF = 4
PREPARED = 8
SLOTS = 8
NEAR_TABLES = 7


def in_vmem(value):
    return pltpu.with_memory_space_constraint(value, pltpu.VMEM)


def in_hbm(value):
    return pltpu.with_memory_space_constraint(value, pltpu.HBM)


def pairs_of(count, shift):
    return [(place, (((place + shift) ^ 1) - shift) % count) for place in range(count)]


def swapped(value, axis, shift):
    return lax.ppermute(value, axis, pairs_of(lax.axis_size(axis), shift))


def slot_of(target, mine):
    return jnp.where(target == mine, 0, jnp.where(target == (mine ^ 1), 1, 2))


def split(value):
    high = value.astype(BF16)
    return high, (value - high.astype(F32)).astype(BF16)


def dot_nt(left, right):
    return lax.dot_general(left, right, (((1,), (1,)), ((), ())), preferred_element_type=F32)


def dot_nn(left, right):
    return lax.dot_general(left, right, (((1,), (0,)), ((), ())), preferred_element_type=F32)


def full_nn(left, right):
    return lax.dot_general(left, right, (((1,), (0,)), ((), ())), precision=HIGHEST, preferred_element_type=F32)


def full_tn(left, right):
    return lax.dot_general(left, right, (((0,), (0,)), ((), ())), precision=HIGHEST, preferred_element_type=F32)


def gram(left, right):
    both = dot_nt(left, right)
    half = both.shape[0] // 2
    return both[:half, :half] + both[:half, half:] + both[half:, :half] + both[half:, half:]


def times(stacked, high, low):
    half = stacked.shape[0] // 2
    first = dot_nn(stacked, high)
    return first[:half] + first[half:] + dot_nn(stacked[:half], low)


def stacked_split(value):
    return jnp.concatenate(split(value), axis=0)


def call(body, out_shape, n_smem, args, scratch=(), aliases=None, limit=4 << 20):
    return pl.pallas_call(
        body,
        out_shape=out_shape,
        in_specs=[SMEM_SPEC] * n_smem + [VMEM_SPEC] * (len(args) - n_smem),
        out_specs=jax.tree.map(lambda _: VMEM_SPEC, out_shape),
        scratch_shapes=list(scratch),
        name=body.__name__,
        input_output_aliases=aliases or {},
        compiler_params=pltpu.CompilerParams(vmem_limit_bytes=limit),
    )(*args[:n_smem], *[in_vmem(a) for a in args[n_smem:]])


def route(pair, routes, blocks):
    count = pair.shape[1]
    block_bits, col_bits = blocks.bit_length() - 1, lax.axis_size("col").bit_length() - 1
    my_row, my_col = lax.axis_index("row"), lax.axis_index("col")
    row_of, col_of = pair[0:1, :], pair[1:2, :]
    owner = col_of >> block_bits
    row_slot = slot_of(owner >> col_bits, my_row)
    col_slot = slot_of(owner & (lax.axis_size("col") - 1), my_col)
    diagonal = (row_slot > 0) & (col_slot > 0)
    slot = jnp.where(diagonal, 2 + 2 * col_slot + row_slot, jnp.where(col_slot > 0, 2 + col_slot, row_slot))
    table_row = slot * blocks + (col_of & (blocks - 1))
    local_row = row_of & (blocks - 1)
    number = lax.broadcasted_iota(jnp.int32, (1, count), 1)
    late = jnp.where(slot >= NEAR_TABLES, 1, 0)
    key = (late * count + number).astype(F32)
    square = (count, count)
    down, across = (lax.broadcasted_iota(jnp.int32, square, axis) for axis in (0, 1))

    def upright(value):
        return jnp.sum(jnp.where(down == across, value.astype(F32), 0.0), axis=1, keepdims=True)

    rank = jnp.sum(jnp.where(key < upright(key), 1.0, 0.0), axis=1, keepdims=True)
    placed = rank == across.astype(F32)
    for i, value in enumerate((number, table_row, local_row)):
        routes[i:i + 1, :] = jnp.sum(jnp.where(placed, upright(value), 0.0), axis=0, keepdims=True).astype(jnp.int32)
    near = count - jnp.sum(late.astype(F32), axis=1, keepdims=True).astype(jnp.int32)
    routes[3:4, :] = jnp.broadcast_to(near >> (HALF.bit_length() - 1), (1, count))


def prepare_body(blocks, pairs, couplings, c_high, c_low, t_high, t_low, routes, pair, buffer, arrived, pair_arrived):
    groups = couplings.shape[0] // PREPARED
    copies = [
        pltpu.make_async_copy(
            couplings.at[pl.ds(i * PREPARED, PREPARED)], buffer.at[i % SLOTS], arrived.at[i])
        for i in range(groups)
    ]
    pair_copy = pltpu.make_async_copy(pairs, pair, pair_arrived)
    pair_copy.start()
    for copy in copies[:SLOTS]:
        copy.start()
    pair_copy.wait()
    route(pair, routes, blocks)
    for i, copy in enumerate(copies):
        copy.wait()
        for place in range(PREPARED):
            k = i * PREPARED + place
            high, low = split(buffer[i % SLOTS, place])
            c_high[k], c_low[k] = high, low
            t_high[k], t_low[k] = high.T, low.T
        if i + SLOTS < groups:
            copies[i + SLOTS].start()


def prepare(pair_index, couplings, blocks):
    count, width = couplings.shape[:2]
    shape = pltpu.VMEM(couplings.shape, BF16)
    return pl.pallas_call(
        functools.partial(prepare_body, blocks),
        in_specs=[pl.BlockSpec(memory_space=pltpu.HBM)] * 2,
        out_specs=[VMEM_SPEC] * 5,
        out_shape=[shape] * 4 + [pltpu.VMEM((4, count), jnp.int32)],
        scratch_shapes=[
            pltpu.VMEM(pair_index.shape, jnp.int32),
            pltpu.VMEM((SLOTS, PREPARED, width, width), F32),
            pltpu.SemaphoreType.DMA((count // PREPARED,)),
            pltpu.SemaphoreType.DMA,
        ],
        name="prepare",
        compiler_params=pltpu.CompilerParams(vmem_limit_bytes=17 << 20),
    )(in_hbm(pair_index), in_hbm(couplings))


def block_of(source, q, width):
    return source[q] if len(source.shape) == 3 else source[:, q * width:(q + 1) * width]


def stack_body(*refs):
    vectors, whole, pair = refs[-5:-2], refs[-2], refs[-1]
    blocks, width = whole.shape[1], whole.shape[3]
    for slot, source in enumerate(vectors):
        for q in range(blocks):
            block = block_of(source, q, width)
            whole[slot, q] = block
            if slot:
                pair[slot - 1, q] = block


def accumulate(first, last, routes, source_row, target_row, source, target, c_high, c_low):
    def step(size, start):
        terms = []
        for place in range(size):
            i = start + place
            k = routes[0, i]
            terms.append((routes[target_row, i], times(source[routes[source_row, i]], c_high[k], c_low[k])))
        for row, term in terms:
            target[row] += term

    def whole(i, carry):
        step(CHUNK, first * HALF + i * CHUNK)
        return carry

    def rest(i, carry):
        step(HALF, (last - 1) * HALF)
        return carry

    lax.fori_loop(0, (last - first) // 2, whole, 0)
    lax.fori_loop(0, (last - first) % 2, rest, 0)


def pull_near_body(routes, qa, whole, cb, *refs):
    c_high, c_low, table, strain = refs
    blocks = strain.shape[0]
    for place, (source, slot) in enumerate(
            ((whole, 0), (whole, 1), (whole, 2), (qa, 0), (cb, None), (qa, 1), (qa, 2))):
        for q in range(blocks):
            block = block_of(source, q, strain.shape[2]) if slot is None else source[slot, q]
            table[place * blocks + q] = stacked_split(block)
    strain[...] = jnp.zeros_like(strain)
    accumulate(0, routes[3, 0], routes, 1, 2, table, strain, c_high, c_low)


def pull_late_body(routes, table_in, strain_in, db, *refs):
    c_high, c_low, *grams, table, strain_hl, g_out, strain = refs
    blocks = strain.shape[0]
    for slot in range(2):
        for q in range(blocks):
            table[(NEAR_TABLES + slot) * blocks + q] = stacked_split(db[slot, q])
    strain[...] = strain_in[...]
    accumulate(routes[3, 0], routes.shape[1] // HALF, routes, 1, 2, table, strain, c_high, c_low)
    total = jnp.zeros((strain.shape[1],) * 2, F32)
    for q in range(blocks):
        both = stacked_split(strain[q])
        strain_hl[q] = both
        total += gram(both, both)
    if not grams:
        g_out[...] = total
    else:
        g01, g1, g23 = grams
        size = total.shape[0]
        for i, part in enumerate((g01[0], g01[1] + g1[...], g23[0], g23[1] + total)):
            g_out[:, i * size:(i + 1) * size] = part


def push_late_body(routes, strain_hl, c_high, c_low, pieces, *targets):
    blocks = strain_hl.shape[0]
    pieces[...] = jnp.zeros_like(pieces)
    accumulate(routes[3, 0], routes.shape[1] // HALF, routes, 2, 1, strain_hl, pieces, c_high, c_low)
    for db in targets:
        for slot in range(2):
            for q in range(blocks):
                db[slot, q] = pieces[(NEAR_TABLES + slot) * blocks + q]


def push_near_body(routes, strain_hl, c_high, c_low, pieces_in, *refs):
    *outs, pieces = refs
    pieces[...] = pieces_in[:pieces.shape[0]]
    accumulate(0, routes[3, 0], routes, 2, 1, strain_hl, pieces, c_high, c_low)
    for place, target in enumerate(outs):
        for q in range(target.shape[0]):
            target[q] = pieces[place * target.shape[0] + q]


def push_begin_body(routes, strain_hl, c_high, c_low, pieces_in, pieces):
    accumulate(0, routes[3, 0] // 2, routes, 2, 1, strain_hl, pieces, c_high, c_low)


def push_end_body(routes, strain_hl, c_high, c_low, pieces_in, pieces):
    accumulate(routes[3, 0] // 2, routes[3, 0], routes, 2, 1, strain_hl, pieces, c_high, c_low)


def pack_body(pieces, grams, own, ra, rb, qa, qb):
    blocks = own.shape[0]
    outs = (own, ra, rb, qa.at[0], qa.at[1], qa.at[2], qb.at[0], qb.at[1], qb.at[2])
    for target, place in zip(outs, (0, 1, 2, 3, 5, 6, 4, 7, 8)):
        for q in range(blocks):
            target[q] = pieces[place * blocks + q]


def add_body(grams, moved, after, total):
    total[...] = grams[...] + moved[...]


def diag_body(vector, diag, own, grams):
    size = grams.shape[1]
    first = jnp.zeros((size, size), F32)
    second = jnp.zeros((size, size), F32)
    width = diag.shape[1]
    for q in range(diag.shape[0]):
        both = stacked_split(block_of(vector, q, width))
        term = times(both, *split(diag[q]))
        own[q] = term
        first += gram(both, both)
        second += gram(stacked_split(term), both)
    grams[0] = first
    grams[1] = second


def middle_early_body(ra, rb, qa_first, qa_second, db, ma, mb):
    ma[...] = ra[...] + qa_first[...] + db[0]
    mb[...] = rb[...] + qa_second[...] + db[1]


def middle_last_body(own, diag, ra, rb, qa, qb, grams, rest, ma, mb):
    rest[...] = (own[...] + diag[...]) + (qa[0] + qb[0])
    ma[...] = ra[...] + qa[1] + qb[1]
    mb[...] = rb[...] + qa[2] + qb[2]


def sum_body(own, diag, ca, cb, rb, ra, out):
    out[...] = (own[...] + diag[...]) + (ca[...] + cb[...]) + (ra[...] + rb[...])


def eliminated(matrix, right):
    size = matrix.shape[0]
    on_diagonal = lax.broadcasted_iota(jnp.int32, (size, size), 0) == lax.broadcasted_iota(jnp.int32, (size, size), 1)
    diagonal = jnp.where(on_diagonal, matrix, 0.0)
    across = lax.rsqrt(jnp.sum(diagonal, axis=0, keepdims=True))
    down = lax.rsqrt(jnp.sum(diagonal, axis=1, keepdims=True))
    work = jnp.concatenate([matrix * down * across, right * down], axis=1)
    rows = lax.broadcasted_iota(jnp.int32, work.shape, 0)
    for k in range(0, size, 2):
        first = jnp.broadcast_to(work[:, k:k + 1], work.shape)
        second = jnp.broadcast_to(work[:, k + 1:k + 2], work.shape)
        upper, lower = work[k:k + 1, :], work[k + 1:k + 2, :]
        a, b, c, d = first[k:k + 1], second[k:k + 1], first[k + 1:k + 2], second[k + 1:k + 2]
        inverse = 1.0 / (a * d - b * c)
        new_upper = (d * upper - b * lower) * inverse
        new_lower = (a * lower - c * upper) * inverse
        rest = work - first * new_upper - second * new_lower
        work = jnp.where(rows == k, new_upper, jnp.where(rows == k + 1, new_lower, rest))
    return work[:, size:] * down


def solve_body(grams, moved, p, q):
    size = grams.shape[0]
    total = grams[...] + moved[...]
    g0, g1, g2, g3 = (total[:, i * size:(i + 1) * size] for i in range(4))
    eye = (lax.broadcasted_iota(jnp.int32, (size, size), 0) == lax.broadcasted_iota(jnp.int32, (size, size), 1)).astype(F32)
    alpha = eliminated(g1, g0)
    inverse = eliminated(g0, eye)
    fresh = (g0 - full_nn(g1, alpha)) - full_tn(alpha, g1 - full_nn(g2, alpha))
    mix = eye + full_nn(inverse, fresh)
    e1 = full_nn(g1, mix) - full_nn(g2, alpha)
    e2 = full_nn(g2, mix) - full_nn(g3, alpha)
    curvature = full_tn(mix, e1) - full_tn(alpha, e2)
    second = eliminated(curvature, fresh)
    p[...] = alpha + full_nn(mix, second)
    q[...] = full_nn(alpha, second)


def finish_body(p, q, right, u, rest, rb, ra, x_out, r_out):
    width = u.shape[2]
    for block in range(u.shape[0]):
        lanes = slice(block * width, (block + 1) * width)
        w = rest[block] + (ra[block] + rb[block])
        x_out[:, lanes] = full_tn(p[...], right[:, lanes]) - full_tn(q[...], u[block])
        r_out[:, lanes] = right[:, lanes] - full_tn(p[...], u[block]) + full_tn(q[...], w)


MASKS = (2, 6, 8, 24, 1)
RING = (32, 96, 64)


def exchanged(value, mask):
    count = lax.axis_size("row") * lax.axis_size("col")
    return lax.ppermute(value, ("row", "col"), [(i, i ^ mask) for i in range(count)])


def per_device(right_sides, diag_blocks, couplings, pair_index):
    blocks, width = diag_blocks.shape[0], diag_blocks.shape[1]
    rows = right_sides.shape[0]
    block_shape = pltpu.VMEM((blocks, rows, width), F32)
    stack_shape = pltpu.VMEM((3, blocks, rows, width), F32)
    pair_shape = pltpu.VMEM((2, blocks, rows, width), F32)
    table_shape = pltpu.VMEM((9 * blocks, 2 * rows, width), BF16)
    split_shape = pltpu.VMEM((blocks, 2 * rows, width), BF16)
    pieces_shape = pltpu.VMEM((9 * blocks, rows, width), F32)
    near_pieces_shape = pltpu.VMEM((NEAR_TABLES * blocks, rows, width), F32)
    gram_shape = pltpu.VMEM((rows, rows), F32)
    grams_shape = pltpu.VMEM((2, rows, rows), F32)
    all_grams_shape = pltpu.VMEM((rows, 4 * rows), F32)

    def spread(vector, *after):
        cb = swapped(vector, "col", 1)
        ra, rb = swapped(vector, "row", 0), swapped(vector, "row", 1)
        whole, pair = call(stack_body, [stack_shape, pair_shape], 0, (*after, cb, vector, ra, rb))
        return (swapped(whole, "col", 0), whole, cb), swapped(pair, "col", 1)

    def pulled(near_tables, db, *grams):
        table, strain = call(pull_near_body, [table_shape, block_shape], 1, (routes, *near_tables, *transposes))
        _, strain_hl, g = call(
            pull_late_body, [table_shape, split_shape, all_grams_shape if grams else gram_shape], 1,
            (routes, table, strain, db, *transposes, *grams), [block_shape], aliases={1: 0})
        return strain_hl, g

    *halves, routes = prepare(pair_index, couplings, blocks)
    couplings, transposes = halves[:2], halves[2:]
    near_tables, db = spread(right_sides, routes)
    strain_hl, g1s = pulled(near_tables, db)

    pieces, db = call(push_late_body, [pieces_shape, pair_shape], 1, (routes, strain_hl, *couplings))
    db = swapped(db, "col", 1)
    own, ra, rb, ca, cb, qa_first, qa_second = call(
        push_near_body, [block_shape] * NEAR_TABLES, 1,
        (routes, strain_hl, *couplings, pieces), [near_pieces_shape])
    ca, qa_first, qa_second = (swapped(a, "col", 0) for a in (ca, qa_first, qa_second))
    cb = swapped(cb, "col", 1)
    diag, g01 = call(diag_body, [block_shape, grams_shape], 0, (right_sides, diag_blocks))
    ra, rb = call(middle_early_body, [block_shape] * 2, 0, (ra, rb, qa_first, qa_second, db))
    rb, ra = swapped(rb, "row", 1), swapped(ra, "row", 0)
    u = call(sum_body, block_shape, 0, (own, diag, ca, cb, rb, ra))

    diag, g23 = call(diag_body, [block_shape, grams_shape], 0, (u, diag_blocks))
    near_tables, db = spread(u, g23)
    strain_hl, grams = pulled(near_tables, db, g01, g1s, g23)
    pieces, = call(push_late_body, [pieces_shape], 1, (routes, strain_hl, *couplings))
    grams = call(add_body, all_grams_shape, 0, (grams, exchanged(grams, MASKS[0]), pieces))
    pieces, = call(push_begin_body, [pieces_shape], 1, (routes, strain_hl, *couplings, pieces), aliases={4: 0})
    grams = call(add_body, all_grams_shape, 0, (grams, exchanged(grams, MASKS[1]), pieces))
    pieces, = call(push_end_body, [pieces_shape], 1, (routes, strain_hl, *couplings, pieces), aliases={4: 0})
    grams = call(add_body, all_grams_shape, 0, (grams, exchanged(grams, MASKS[2]), pieces))
    own, ra, rb, qa, qb = call(pack_body, [block_shape] * 3 + [stack_shape] * 2, 0, (pieces, grams))
    qa, qb = swapped(qa, "col", 0), swapped(qb, "col", 1)
    grams = grams + exchanged(grams, MASKS[3])
    first, second, third = (exchanged(grams, mask) for mask in RING)
    grams = (grams + first) + (second + third)
    rest, ra, rb = call(middle_last_body, [block_shape] * 3, 0, (own, diag, ra, rb, qa, qb, grams))
    rb, ra = swapped(rb, "row", 1), swapped(ra, "row", 0)
    p, q = call(solve_body, [gram_shape] * 2, 0, (grams, exchanged(grams, MASKS[4])))
    flat = jax.ShapeDtypeStruct(right_sides.shape, F32)
    return tuple(call(finish_body, [flat, flat], 0, (p, q, right_sides, u, rest, rb, ra)))


def solution(mesh):
    return jax.shard_map(
        per_device,
        mesh=mesh,
        in_specs=(
            P(None, ("row", "col")),
            P(("row", "col"), None, None),
            P(("row", "col"), None, None),
            P(None, ("row", "col")),
        ),
        out_specs=(P(None, ("row", "col")), P(None, ("row", "col"))),
        check_vma=False,
    )
```

```python
import functools

import jax
import jax.numpy as jnp
from jax import lax
from jax.experimental import pallas as pl
from jax.experimental.pallas import tpu as pltpu
from jax.sharding import PartitionSpec as P

F32 = jnp.float32
BF16 = jnp.bfloat16
HIGHEST = lax.Precision.HIGHEST
VMEM_SPEC = pl.BlockSpec(memory_space=pltpu.VMEM)
SMEM_SPEC = pl.BlockSpec(memory_space=pltpu.SMEM)
CHUNK = 8
HALF = 4
PREPARED = 8
SLOTS = 8
NEAR_TABLES = 7


def in_vmem(value):
    return pltpu.with_memory_space_constraint(value, pltpu.VMEM)


def in_hbm(value):
    return pltpu.with_memory_space_constraint(value, pltpu.HBM)


def pairs_of(count, shift):
    return [(place, (((place + shift) ^ 1) - shift) % count) for place in range(count)]


def swapped(value, axis, shift):
    return lax.ppermute(value, axis, pairs_of(lax.axis_size(axis), shift))


def slot_of(target, mine):
    return jnp.where(target == mine, 0, jnp.where(target == (mine ^ 1), 1, 2))


def split(value):
    high = value.astype(BF16)
    return high, (value - high.astype(F32)).astype(BF16)


def dot_nt(left, right):
    return lax.dot_general(left, right, (((1,), (1,)), ((), ())), preferred_element_type=F32)


def dot_nn(left, right):
    return lax.dot_general(left, right, (((1,), (0,)), ((), ())), preferred_element_type=F32)


def full_nn(left, right):
    return lax.dot_general(left, right, (((1,), (0,)), ((), ())), precision=HIGHEST, preferred_element_type=F32)


def full_tn(left, right):
    return lax.dot_general(left, right, (((0,), (0,)), ((), ())), precision=HIGHEST, preferred_element_type=F32)


def gram(left, right):
    both = dot_nt(left, right)
    half = both.shape[0] // 2
    return both[:half, :half] + both[:half, half:] + both[half:, :half] + both[half:, half:]


def times(stacked, high, low):
    half = stacked.shape[0] // 2
    first = dot_nn(stacked, high)
    return first[:half] + first[half:] + dot_nn(stacked[:half], low)


def stacked_split(value):
    return jnp.concatenate(split(value), axis=0)


def call(body, out_shape, n_smem, args, scratch=(), aliases=None, limit=4 << 20):
    return pl.pallas_call(
        body,
        out_shape=out_shape,
        in_specs=[SMEM_SPEC] * n_smem + [VMEM_SPEC] * (len(args) - n_smem),
        out_specs=jax.tree.map(lambda _: VMEM_SPEC, out_shape),
        scratch_shapes=list(scratch),
        name=body.__name__,
        input_output_aliases=aliases or {},
        compiler_params=pltpu.CompilerParams(vmem_limit_bytes=limit),
    )(*args[:n_smem], *[in_vmem(a) for a in args[n_smem:]])


def route(pair, routes, blocks):
    count = pair.shape[1]
    block_bits, col_bits = blocks.bit_length() - 1, lax.axis_size("col").bit_length() - 1
    my_row, my_col = lax.axis_index("row"), lax.axis_index("col")
    row_of, col_of = pair[0:1, :], pair[1:2, :]
    owner = col_of >> block_bits
    row_slot = slot_of(owner >> col_bits, my_row)
    col_slot = slot_of(owner & (lax.axis_size("col") - 1), my_col)
    diagonal = (row_slot > 0) & (col_slot > 0)
    slot = jnp.where(diagonal, 2 + 2 * col_slot + row_slot, jnp.where(col_slot > 0, 2 + col_slot, row_slot))
    table_row = slot * blocks + (col_of & (blocks - 1))
    local_row = row_of & (blocks - 1)
    number = lax.broadcasted_iota(jnp.int32, (1, count), 1)
    late = jnp.where(slot >= NEAR_TABLES, 1, 0)
    key = (late * count + number).astype(F32)
    square = (count, count)
    down, across = (lax.broadcasted_iota(jnp.int32, square, axis) for axis in (0, 1))

    def upright(value):
        return jnp.sum(jnp.where(down == across, value.astype(F32), 0.0), axis=1, keepdims=True)

    rank = jnp.sum(jnp.where(key < upright(key), 1.0, 0.0), axis=1, keepdims=True)
    placed = rank == across.astype(F32)
    for i, value in enumerate((number, table_row, local_row)):
        routes[i:i + 1, :] = jnp.sum(jnp.where(placed, upright(value), 0.0), axis=0, keepdims=True).astype(jnp.int32)
    near = count - jnp.sum(late.astype(F32), axis=1, keepdims=True).astype(jnp.int32)
    routes[3:4, :] = jnp.broadcast_to(near >> (HALF.bit_length() - 1), (1, count))


def prepare_body(blocks, pairs, couplings, c_high, c_low, t_high, t_low, routes, pair, buffer, arrived, pair_arrived):
    groups = couplings.shape[0] // PREPARED
    copies = [
        pltpu.make_async_copy(
            couplings.at[pl.ds(i * PREPARED, PREPARED)], buffer.at[i % SLOTS], arrived.at[i])
        for i in range(groups)
    ]
    pair_copy = pltpu.make_async_copy(pairs, pair, pair_arrived)
    pair_copy.start()
    for copy in copies[:SLOTS]:
        copy.start()
    for i, copy in enumerate(copies):
        if i == groups - 1:
            pair_copy.wait()
            route(pair, routes, blocks)
        copy.wait()
        for place in range(PREPARED):
            k = i * PREPARED + place
            high, low = split(buffer[i % SLOTS, place])
            c_high[k], c_low[k] = high, low
            t_high[k], t_low[k] = high.T, low.T
        if i + SLOTS < groups:
            copies[i + SLOTS].start()


def prepare(pair_index, couplings, blocks):
    count, width = couplings.shape[:2]
    shape = pltpu.VMEM(couplings.shape, BF16)
    return pl.pallas_call(
        functools.partial(prepare_body, blocks),
        in_specs=[pl.BlockSpec(memory_space=pltpu.HBM)] * 2,
        out_specs=[VMEM_SPEC] * 5,
        out_shape=[shape] * 4 + [pltpu.VMEM((4, count), jnp.int32)],
        scratch_shapes=[
            pltpu.VMEM(pair_index.shape, jnp.int32),
            pltpu.VMEM((SLOTS, PREPARED, width, width), F32),
            pltpu.SemaphoreType.DMA((count // PREPARED,)),
            pltpu.SemaphoreType.DMA,
        ],
        name="prepare",
        compiler_params=pltpu.CompilerParams(vmem_limit_bytes=17 << 20),
    )(in_hbm(pair_index), in_hbm(couplings))


def block_of(source, q, width):
    return source[q] if len(source.shape) == 3 else source[:, q * width:(q + 1) * width]


def stack_body(*refs):
    vectors, whole, pair = refs[-5:-2], refs[-2], refs[-1]
    blocks, width = whole.shape[1], whole.shape[3]
    for slot, source in enumerate(vectors):
        for q in range(blocks):
            block = block_of(source, q, width)
            whole[slot, q] = block
            if slot:
                pair[slot - 1, q] = block


def accumulate(first, last, routes, source_row, target_row, source, target, c_high, c_low):
    def step(size, start):
        terms = []
        for place in range(size):
            i = start + place
            k = routes[0, i]
            terms.append((routes[target_row, i], times(source[routes[source_row, i]], c_high[k], c_low[k])))
        for row, term in terms:
            target[row] += term

    def whole(i, carry):
        step(CHUNK, first * HALF + i * CHUNK)
        return carry

    def rest(i, carry):
        step(HALF, (last - 1) * HALF)
        return carry

    lax.fori_loop(0, (last - first) // 2, whole, 0)
    lax.fori_loop(0, (last - first) % 2, rest, 0)


def pull_near_body(routes, qa, whole, cb, *refs):
    c_high, c_low, table, strain = refs
    blocks = strain.shape[0]
    for place, (source, slot) in enumerate(
            ((whole, 0), (whole, 1), (whole, 2), (qa, 0), (cb, None), (qa, 1), (qa, 2))):
        for q in range(blocks):
            block = block_of(source, q, strain.shape[2]) if slot is None else source[slot, q]
            table[place * blocks + q] = stacked_split(block)
    strain[...] = jnp.zeros_like(strain)
    accumulate(0, routes[3, 0], routes, 1, 2, table, strain, c_high, c_low)


def pull_late_body(routes, table_in, strain_in, db, *refs):
    c_high, c_low, *grams, table, strain_hl, g_out, strain = refs
    blocks = strain.shape[0]
    for slot in range(2):
        for q in range(blocks):
            table[(NEAR_TABLES + slot) * blocks + q] = stacked_split(db[slot, q])
    strain[...] = strain_in[...]
    accumulate(routes[3, 0], routes.shape[1] // HALF, routes, 1, 2, table, strain, c_high, c_low)
    total = jnp.zeros((strain.shape[1],) * 2, F32)
    for q in range(blocks):
        both = stacked_split(strain[q])
        strain_hl[q] = both
        total += gram(both, both)
    if not grams:
        g_out[...] = total
    else:
        g01, g1, g23 = grams
        size = total.shape[0]
        for i, part in enumerate((g01[0], g01[1] + g1[...], g23[0], g23[1] + total)):
            g_out[:, i * size:(i + 1) * size] = part


def push_late_body(routes, strain_hl, c_high, c_low, pieces, *targets):
    blocks = strain_hl.shape[0]
    pieces[...] = jnp.zeros_like(pieces)
    accumulate(routes[3, 0], routes.shape[1] // HALF, routes, 2, 1, strain_hl, pieces, c_high, c_low)
    for db in targets:
        for slot in range(2):
            for q in range(blocks):
                db[slot, q] = pieces[(NEAR_TABLES + slot) * blocks + q]


def push_near_body(routes, strain_hl, c_high, c_low, pieces_in, *refs):
    *outs, pieces = refs
    pieces[...] = pieces_in[:pieces.shape[0]]
    accumulate(0, routes[3, 0], routes, 2, 1, strain_hl, pieces, c_high, c_low)
    for place, target in enumerate(outs):
        for q in range(target.shape[0]):
            target[q] = pieces[place * target.shape[0] + q]


def push_begin_body(routes, strain_hl, c_high, c_low, pieces_in, pieces):
    accumulate(0, routes[3, 0] // 2, routes, 2, 1, strain_hl, pieces, c_high, c_low)


def push_end_body(routes, strain_hl, c_high, c_low, pieces_in, pieces):
    accumulate(routes[3, 0] // 2, routes[3, 0], routes, 2, 1, strain_hl, pieces, c_high, c_low)


def pack_body(pieces, grams, own, ra, rb, qa, qb):
    blocks = own.shape[0]
    outs = (own, ra, rb, qa.at[0], qa.at[1], qa.at[2], qb.at[0], qb.at[1], qb.at[2])
    for target, place in zip(outs, (0, 1, 2, 3, 5, 6, 4, 7, 8)):
        for q in range(blocks):
            target[q] = pieces[place * blocks + q]


def add_body(grams, moved, after, total):
    total[...] = grams[...] + moved[...]


def diag_body(vector, diag, own, grams):
    size = grams.shape[1]
    first = jnp.zeros((size, size), F32)
    second = jnp.zeros((size, size), F32)
    width = diag.shape[1]
    for q in range(diag.shape[0]):
        both = stacked_split(block_of(vector, q, width))
        term = times(both, *split(diag[q]))
        own[q] = term
        first += gram(both, both)
        second += gram(stacked_split(term), both)
    grams[0] = first
    grams[1] = second


def middle_early_body(ra, rb, qa_first, qa_second, db, ma, mb):
    ma[...] = ra[...] + qa_first[...] + db[0]
    mb[...] = rb[...] + qa_second[...] + db[1]


def middle_last_body(own, diag, ra, rb, qa, qb, grams, rest, ma, mb):
    rest[...] = (own[...] + diag[...]) + (qa[0] + qb[0])
    ma[...] = ra[...] + qa[1] + qb[1]
    mb[...] = rb[...] + qa[2] + qb[2]


def sum_body(own, diag, ca, cb, rb, ra, out):
    out[...] = (own[...] + diag[...]) + (ca[...] + cb[...]) + (ra[...] + rb[...])


def eliminated(matrix, right):
    size = matrix.shape[0]
    on_diagonal = lax.broadcasted_iota(jnp.int32, (size, size), 0) == lax.broadcasted_iota(jnp.int32, (size, size), 1)
    diagonal = jnp.where(on_diagonal, matrix, 0.0)
    across = lax.rsqrt(jnp.sum(diagonal, axis=0, keepdims=True))
    down = lax.rsqrt(jnp.sum(diagonal, axis=1, keepdims=True))
    work = jnp.concatenate([matrix * down * across, right * down], axis=1)
    rows = lax.broadcasted_iota(jnp.int32, work.shape, 0)
    for k in range(0, size, 2):
        first = jnp.broadcast_to(work[:, k:k + 1], work.shape)
        second = jnp.broadcast_to(work[:, k + 1:k + 2], work.shape)
        upper, lower = work[k:k + 1, :], work[k + 1:k + 2, :]
        a, b, c, d = first[k:k + 1], second[k:k + 1], first[k + 1:k + 2], second[k + 1:k + 2]
        inverse = 1.0 / (a * d - b * c)
        new_upper = (d * upper - b * lower) * inverse
        new_lower = (a * lower - c * upper) * inverse
        rest = work - first * new_upper - second * new_lower
        work = jnp.where(rows == k, new_upper, jnp.where(rows == k + 1, new_lower, rest))
    return work[:, size:] * down


def solve_body(grams, moved, p, q):
    size = grams.shape[0]
    total = grams[...] + moved[...]
    g0, g1, g2, g3 = (total[:, i * size:(i + 1) * size] for i in range(4))
    eye = (lax.broadcasted_iota(jnp.int32, (size, size), 0) == lax.broadcasted_iota(jnp.int32, (size, size), 1)).astype(F32)
    alpha = eliminated(g1, g0)
    inverse = eliminated(g0, eye)
    fresh = (g0 - full_nn(g1, alpha)) - full_tn(alpha, g1 - full_nn(g2, alpha))
    mix = eye + full_nn(inverse, fresh)
    e1 = full_nn(g1, mix) - full_nn(g2, alpha)
    e2 = full_nn(g2, mix) - full_nn(g3, alpha)
    curvature = full_tn(mix, e1) - full_tn(alpha, e2)
    second = eliminated(curvature, fresh)
    p[...] = alpha + full_nn(mix, second)
    q[...] = full_nn(alpha, second)


def finish_body(p, q, right, u, rest, rb, ra, x_out, r_out):
    width = u.shape[2]
    for block in range(u.shape[0]):
        lanes = slice(block * width, (block + 1) * width)
        w = rest[block] + (ra[block] + rb[block])
        x_out[:, lanes] = full_tn(p[...], right[:, lanes]) - full_tn(q[...], u[block])
        r_out[:, lanes] = right[:, lanes] - full_tn(p[...], u[block]) + full_tn(q[...], w)


MASKS = (2, 6, 8, 24, 1)
RING = (32, 96, 64)


def exchanged(value, mask):
    count = lax.axis_size("row") * lax.axis_size("col")
    return lax.ppermute(value, ("row", "col"), [(i, i ^ mask) for i in range(count)])


def per_device(right_sides, diag_blocks, couplings, pair_index):
    blocks, width = diag_blocks.shape[0], diag_blocks.shape[1]
    rows = right_sides.shape[0]
    block_shape = pltpu.VMEM((blocks, rows, width), F32)
    stack_shape = pltpu.VMEM((3, blocks, rows, width), F32)
    pair_shape = pltpu.VMEM((2, blocks, rows, width), F32)
    table_shape = pltpu.VMEM((9 * blocks, 2 * rows, width), BF16)
    split_shape = pltpu.VMEM((blocks, 2 * rows, width), BF16)
    pieces_shape = pltpu.VMEM((9 * blocks, rows, width), F32)
    near_pieces_shape = pltpu.VMEM((NEAR_TABLES * blocks, rows, width), F32)
    gram_shape = pltpu.VMEM((rows, rows), F32)
    grams_shape = pltpu.VMEM((2, rows, rows), F32)
    all_grams_shape = pltpu.VMEM((rows, 4 * rows), F32)

    def spread(vector, *after):
        cb = swapped(vector, "col", 1)
        ra, rb = swapped(vector, "row", 0), swapped(vector, "row", 1)
        whole, pair = call(stack_body, [stack_shape, pair_shape], 0, (*after, cb, vector, ra, rb))
        return (swapped(whole, "col", 0), whole, cb), swapped(pair, "col", 1)

    def pulled(near_tables, db, *grams):
        table, strain = call(pull_near_body, [table_shape, block_shape], 1, (routes, *near_tables, *transposes))
        _, strain_hl, g = call(
            pull_late_body, [table_shape, split_shape, all_grams_shape if grams else gram_shape], 1,
            (routes, table, strain, db, *transposes, *grams), [block_shape], aliases={1: 0})
        return strain_hl, g

    *halves, routes = prepare(pair_index, couplings, blocks)
    couplings, transposes = halves[:2], halves[2:]
    near_tables, db = spread(right_sides, routes)
    strain_hl, g1s = pulled(near_tables, db)

    pieces, db = call(push_late_body, [pieces_shape, pair_shape], 1, (routes, strain_hl, *couplings))
    db = swapped(db, "col", 1)
    own, ra, rb, ca, cb, qa_first, qa_second = call(
        push_near_body, [block_shape] * NEAR_TABLES, 1,
        (routes, strain_hl, *couplings, pieces), [near_pieces_shape])
    ca, qa_first, qa_second = (swapped(a, "col", 0) for a in (ca, qa_first, qa_second))
    cb = swapped(cb, "col", 1)
    diag, g01 = call(diag_body, [block_shape, grams_shape], 0, (right_sides, diag_blocks))
    ra, rb = call(middle_early_body, [block_shape] * 2, 0, (ra, rb, qa_first, qa_second, db))
    rb, ra = swapped(rb, "row", 1), swapped(ra, "row", 0)
    u = call(sum_body, block_shape, 0, (own, diag, ca, cb, rb, ra))

    diag, g23 = call(diag_body, [block_shape, grams_shape], 0, (u, diag_blocks))
    near_tables, db = spread(u, g23)
    strain_hl, grams = pulled(near_tables, db, g01, g1s, g23)
    pieces, = call(push_late_body, [pieces_shape], 1, (routes, strain_hl, *couplings))
    grams = call(add_body, all_grams_shape, 0, (grams, exchanged(grams, MASKS[0]), pieces))
    pieces, = call(push_begin_body, [pieces_shape], 1, (routes, strain_hl, *couplings, pieces), aliases={4: 0})
    grams = call(add_body, all_grams_shape, 0, (grams, exchanged(grams, MASKS[1]), pieces))
    pieces, = call(push_end_body, [pieces_shape], 1, (routes, strain_hl, *couplings, pieces), aliases={4: 0})
    grams = call(add_body, all_grams_shape, 0, (grams, exchanged(grams, MASKS[2]), pieces))
    own, ra, rb, qa, qb = call(pack_body, [block_shape] * 3 + [stack_shape] * 2, 0, (pieces, grams))
    qa, qb = swapped(qa, "col", 0), swapped(qb, "col", 1)
    grams = grams + exchanged(grams, MASKS[3])
    first, second, third = (exchanged(grams, mask) for mask in RING)
    grams = (grams + first) + (second + third)
    rest, ra, rb = call(middle_last_body, [block_shape] * 3, 0, (own, diag, ra, rb, qa, qb, grams))
    rb, ra = swapped(rb, "row", 1), swapped(ra, "row", 0)
    p, q = call(solve_body, [gram_shape] * 2, 0, (grams, exchanged(grams, MASKS[4])))
    flat = jax.ShapeDtypeStruct(right_sides.shape, F32)
    return tuple(call(finish_body, [flat, flat], 0, (p, q, right_sides, u, rest, rb, ra)))


def solution(mesh):
    return jax.shard_map(
        per_device,
        mesh=mesh,
        in_specs=(
            P(None, ("row", "col")),
            P(("row", "col"), None, None),
            P(("row", "col"), None, None),
            P(None, ("row", "col")),
        ),
        out_specs=(P(None, ("row", "col")), P(None, ("row", "col"))),
        check_vma=False,
    )
```

```python
import functools

import jax
import jax.numpy as jnp
from jax import lax
from jax.experimental import pallas as pl
from jax.experimental.pallas import tpu as pltpu
from jax.sharding import PartitionSpec as P

F32 = jnp.float32
BF16 = jnp.bfloat16
HIGHEST = lax.Precision.HIGHEST
VMEM_SPEC = pl.BlockSpec(memory_space=pltpu.VMEM)
SMEM_SPEC = pl.BlockSpec(memory_space=pltpu.SMEM)
CHUNK = 8
HALF = 4
PREPARED = 4
SLOTS = 16
NEAR_TABLES = 7


def in_vmem(value):
    return pltpu.with_memory_space_constraint(value, pltpu.VMEM)


def in_hbm(value):
    return pltpu.with_memory_space_constraint(value, pltpu.HBM)


def pairs_of(count, shift):
    return [(place, (((place + shift) ^ 1) - shift) % count) for place in range(count)]


def swapped(value, axis, shift):
    return lax.ppermute(value, axis, pairs_of(lax.axis_size(axis), shift))


def slot_of(target, mine):
    return jnp.where(target == mine, 0, jnp.where(target == (mine ^ 1), 1, 2))


def split(value):
    high = value.astype(BF16)
    return high, (value - high.astype(F32)).astype(BF16)


def dot_nt(left, right):
    return lax.dot_general(left, right, (((1,), (1,)), ((), ())), preferred_element_type=F32)


def dot_nn(left, right):
    return lax.dot_general(left, right, (((1,), (0,)), ((), ())), preferred_element_type=F32)


def full_nn(left, right):
    return lax.dot_general(left, right, (((1,), (0,)), ((), ())), precision=HIGHEST, preferred_element_type=F32)


def full_tn(left, right):
    return lax.dot_general(left, right, (((0,), (0,)), ((), ())), precision=HIGHEST, preferred_element_type=F32)


def gram(left, right):
    both = dot_nt(left, right)
    half = both.shape[0] // 2
    return both[:half, :half] + both[:half, half:] + both[half:, :half] + both[half:, half:]


def times(stacked, high, low):
    half = stacked.shape[0] // 2
    first = dot_nn(stacked, high)
    return first[:half] + first[half:] + dot_nn(stacked[:half], low)


def stacked_split(value):
    return jnp.concatenate(split(value), axis=0)


def call(body, out_shape, n_smem, args, scratch=(), aliases=None, limit=4 << 20):
    return pl.pallas_call(
        body,
        out_shape=out_shape,
        in_specs=[SMEM_SPEC] * n_smem + [VMEM_SPEC] * (len(args) - n_smem),
        out_specs=jax.tree.map(lambda _: VMEM_SPEC, out_shape),
        scratch_shapes=list(scratch),
        name=body.__name__,
        input_output_aliases=aliases or {},
        compiler_params=pltpu.CompilerParams(vmem_limit_bytes=limit),
    )(*args[:n_smem], *[in_vmem(a) for a in args[n_smem:]])


def route(pair, routes, blocks):
    count = pair.shape[1]
    block_bits, col_bits = blocks.bit_length() - 1, lax.axis_size("col").bit_length() - 1
    my_row, my_col = lax.axis_index("row"), lax.axis_index("col")
    row_of, col_of = pair[0:1, :], pair[1:2, :]
    owner = col_of >> block_bits
    row_slot = slot_of(owner >> col_bits, my_row)
    col_slot = slot_of(owner & (lax.axis_size("col") - 1), my_col)
    diagonal = (row_slot > 0) & (col_slot > 0)
    slot = jnp.where(diagonal, 2 + 2 * col_slot + row_slot, jnp.where(col_slot > 0, 2 + col_slot, row_slot))
    table_row = slot * blocks + (col_of & (blocks - 1))
    local_row = row_of & (blocks - 1)
    number = lax.broadcasted_iota(jnp.int32, (1, count), 1)
    late = jnp.where(slot >= NEAR_TABLES, 1, 0)
    key = (late * count + number).astype(F32)
    square = (count, count)
    down, across = (lax.broadcasted_iota(jnp.int32, square, axis) for axis in (0, 1))

    def upright(value):
        return jnp.sum(jnp.where(down == across, value.astype(F32), 0.0), axis=1, keepdims=True)

    rank = jnp.sum(jnp.where(key < upright(key), 1.0, 0.0), axis=1, keepdims=True)
    placed = rank == across.astype(F32)
    for i, value in enumerate((number, table_row, local_row)):
        routes[i:i + 1, :] = jnp.sum(jnp.where(placed, upright(value), 0.0), axis=0, keepdims=True).astype(jnp.int32)
    near = count - jnp.sum(late.astype(F32), axis=1, keepdims=True).astype(jnp.int32)
    routes[3:4, :] = jnp.broadcast_to(near >> (HALF.bit_length() - 1), (1, count))


def prepare_body(blocks, pairs, couplings, c_high, c_low, t_high, t_low, routes, pair, buffer, arrived, pair_arrived):
    groups = couplings.shape[0] // PREPARED
    copies = [
        pltpu.make_async_copy(
            couplings.at[pl.ds(i * PREPARED, PREPARED)], buffer.at[i % SLOTS], arrived.at[i])
        for i in range(groups)
    ]
    pair_copy = pltpu.make_async_copy(pairs, pair, pair_arrived)
    pair_copy.start()
    for copy in copies[:SLOTS]:
        copy.start()
    for i, copy in enumerate(copies):
        if i == groups - 1:
            pair_copy.wait()
            route(pair, routes, blocks)
        copy.wait()
        for place in range(PREPARED):
            k = i * PREPARED + place
            high, low = split(buffer[i % SLOTS, place])
            c_high[k], c_low[k] = high, low
            t_high[k], t_low[k] = high.T, low.T
        if i + SLOTS < groups:
            copies[i + SLOTS].start()


def prepare(pair_index, couplings, blocks):
    count, width = couplings.shape[:2]
    shape = pltpu.VMEM(couplings.shape, BF16)
    return pl.pallas_call(
        functools.partial(prepare_body, blocks),
        in_specs=[pl.BlockSpec(memory_space=pltpu.HBM)] * 2,
        out_specs=[VMEM_SPEC] * 5,
        out_shape=[shape] * 4 + [pltpu.VMEM((4, count), jnp.int32)],
        scratch_shapes=[
            pltpu.VMEM(pair_index.shape, jnp.int32),
            pltpu.VMEM((SLOTS, PREPARED, width, width), F32),
            pltpu.SemaphoreType.DMA((count // PREPARED,)),
            pltpu.SemaphoreType.DMA,
        ],
        name="prepare",
        compiler_params=pltpu.CompilerParams(vmem_limit_bytes=17 << 20),
    )(in_hbm(pair_index), in_hbm(couplings))


def block_of(source, q, width):
    return source[q] if len(source.shape) == 3 else source[:, q * width:(q + 1) * width]


def stack_body(*refs):
    vectors, whole, pair = refs[-5:-2], refs[-2], refs[-1]
    blocks, width = whole.shape[1], whole.shape[3]
    for slot, source in enumerate(vectors):
        for q in range(blocks):
            block = block_of(source, q, width)
            whole[slot, q] = block
            if slot:
                pair[slot - 1, q] = block


def accumulate(first, last, routes, source_row, target_row, source, target, c_high, c_low):
    def step(size, start):
        terms = []
        for place in range(size):
            i = start + place
            k = routes[0, i]
            terms.append((routes[target_row, i], times(source[routes[source_row, i]], c_high[k], c_low[k])))
        for row, term in terms:
            target[row] += term

    def whole(i, carry):
        step(CHUNK, first * HALF + i * CHUNK)
        return carry

    def rest(i, carry):
        step(HALF, (last - 1) * HALF)
        return carry

    lax.fori_loop(0, (last - first) // 2, whole, 0)
    lax.fori_loop(0, (last - first) % 2, rest, 0)


def pull_near_body(routes, qa, whole, cb, *refs):
    c_high, c_low, table, strain = refs
    blocks = strain.shape[0]
    for place, (source, slot) in enumerate(
            ((whole, 0), (whole, 1), (whole, 2), (qa, 0), (cb, None), (qa, 1), (qa, 2))):
        for q in range(blocks):
            block = block_of(source, q, strain.shape[2]) if slot is None else source[slot, q]
            table[place * blocks + q] = stacked_split(block)
    strain[...] = jnp.zeros_like(strain)
    accumulate(0, routes[3, 0], routes, 1, 2, table, strain, c_high, c_low)


def pull_late_body(routes, table_in, strain_in, db, *refs):
    c_high, c_low, *grams, table, strain_hl, g_out, strain = refs
    blocks = strain.shape[0]
    for slot in range(2):
        for q in range(blocks):
            table[(NEAR_TABLES + slot) * blocks + q] = stacked_split(db[slot, q])
    strain[...] = strain_in[...]
    accumulate(routes[3, 0], routes.shape[1] // HALF, routes, 1, 2, table, strain, c_high, c_low)
    total = jnp.zeros((strain.shape[1],) * 2, F32)
    for q in range(blocks):
        both = stacked_split(strain[q])
        strain_hl[q] = both
        total += gram(both, both)
    if not grams:
        g_out[...] = total
    else:
        g01, g1, g23 = grams
        size = total.shape[0]
        for i, part in enumerate((g01[0], g01[1] + g1[...], g23[0], g23[1] + total)):
            g_out[:, i * size:(i + 1) * size] = part


def push_late_body(routes, strain_hl, c_high, c_low, pieces, *targets):
    blocks = strain_hl.shape[0]
    pieces[...] = jnp.zeros_like(pieces)
    accumulate(routes[3, 0], routes.shape[1] // HALF, routes, 2, 1, strain_hl, pieces, c_high, c_low)
    for db in targets:
        for slot in range(2):
            for q in range(blocks):
                db[slot, q] = pieces[(NEAR_TABLES + slot) * blocks + q]


def push_near_body(routes, strain_hl, c_high, c_low, pieces_in, *refs):
    *outs, pieces = refs
    pieces[...] = pieces_in[:pieces.shape[0]]
    accumulate(0, routes[3, 0], routes, 2, 1, strain_hl, pieces, c_high, c_low)
    for place, target in enumerate(outs):
        for q in range(target.shape[0]):
            target[q] = pieces[place * target.shape[0] + q]


def push_begin_body(routes, strain_hl, c_high, c_low, pieces_in, pieces):
    accumulate(0, routes[3, 0] // 2, routes, 2, 1, strain_hl, pieces, c_high, c_low)


def push_end_body(routes, strain_hl, c_high, c_low, pieces_in, pieces):
    accumulate(routes[3, 0] // 2, routes[3, 0], routes, 2, 1, strain_hl, pieces, c_high, c_low)


def pack_body(pieces, grams, own, ra, rb, qa, qb):
    blocks = own.shape[0]
    outs = (own, ra, rb, qa.at[0], qa.at[1], qa.at[2], qb.at[0], qb.at[1], qb.at[2])
    for target, place in zip(outs, (0, 1, 2, 3, 5, 6, 4, 7, 8)):
        for q in range(blocks):
            target[q] = pieces[place * blocks + q]


def add_body(grams, moved, after, total):
    total[...] = grams[...] + moved[...]


def diag_body(vector, diag, own, grams):
    size = grams.shape[1]
    first = jnp.zeros((size, size), F32)
    second = jnp.zeros((size, size), F32)
    width = diag.shape[1]
    for q in range(diag.shape[0]):
        both = stacked_split(block_of(vector, q, width))
        term = times(both, *split(diag[q]))
        own[q] = term
        first += gram(both, both)
        second += gram(stacked_split(term), both)
    grams[0] = first
    grams[1] = second


def middle_early_body(ra, rb, qa_first, qa_second, db, ma, mb):
    ma[...] = ra[...] + qa_first[...] + db[0]
    mb[...] = rb[...] + qa_second[...] + db[1]


def middle_last_body(own, diag, ra, rb, qa, qb, grams, rest, ma, mb):
    rest[...] = (own[...] + diag[...]) + (qa[0] + qb[0])
    ma[...] = ra[...] + qa[1] + qb[1]
    mb[...] = rb[...] + qa[2] + qb[2]


def sum_body(own, diag, ca, cb, rb, ra, out):
    out[...] = (own[...] + diag[...]) + (ca[...] + cb[...]) + (ra[...] + rb[...])


def eliminated(matrix, right):
    size = matrix.shape[0]
    on_diagonal = lax.broadcasted_iota(jnp.int32, (size, size), 0) == lax.broadcasted_iota(jnp.int32, (size, size), 1)
    diagonal = jnp.where(on_diagonal, matrix, 0.0)
    across = lax.rsqrt(jnp.sum(diagonal, axis=0, keepdims=True))
    down = lax.rsqrt(jnp.sum(diagonal, axis=1, keepdims=True))
    work = jnp.concatenate([matrix * down * across, right * down], axis=1)
    rows = lax.broadcasted_iota(jnp.int32, work.shape, 0)
    for k in range(0, size, 2):
        first = jnp.broadcast_to(work[:, k:k + 1], work.shape)
        second = jnp.broadcast_to(work[:, k + 1:k + 2], work.shape)
        upper, lower = work[k:k + 1, :], work[k + 1:k + 2, :]
        a, b, c, d = first[k:k + 1], second[k:k + 1], first[k + 1:k + 2], second[k + 1:k + 2]
        inverse = 1.0 / (a * d - b * c)
        new_upper = (d * upper - b * lower) * inverse
        new_lower = (a * lower - c * upper) * inverse
        rest = work - first * new_upper - second * new_lower
        work = jnp.where(rows == k, new_upper, jnp.where(rows == k + 1, new_lower, rest))
    return work[:, size:] * down


def solve_body(grams, moved, p, q):
    size = grams.shape[0]
    total = grams[...] + moved[...]
    g0, g1, g2, g3 = (total[:, i * size:(i + 1) * size] for i in range(4))
    eye = (lax.broadcasted_iota(jnp.int32, (size, size), 0) == lax.broadcasted_iota(jnp.int32, (size, size), 1)).astype(F32)
    alpha = eliminated(g1, g0)
    inverse = eliminated(g0, eye)
    fresh = (g0 - full_nn(g1, alpha)) - full_tn(alpha, g1 - full_nn(g2, alpha))
    mix = eye + full_nn(inverse, fresh)
    e1 = full_nn(g1, mix) - full_nn(g2, alpha)
    e2 = full_nn(g2, mix) - full_nn(g3, alpha)
    curvature = full_tn(mix, e1) - full_tn(alpha, e2)
    second = eliminated(curvature, fresh)
    p[...] = alpha + full_nn(mix, second)
    q[...] = full_nn(alpha, second)


def finish_body(p, q, right, u, rest, rb, ra, x_out, r_out):
    width = u.shape[2]
    for block in range(u.shape[0]):
        lanes = slice(block * width, (block + 1) * width)
        w = rest[block] + (ra[block] + rb[block])
        x_out[:, lanes] = full_tn(p[...], right[:, lanes]) - full_tn(q[...], u[block])
        r_out[:, lanes] = right[:, lanes] - full_tn(p[...], u[block]) + full_tn(q[...], w)


MASKS = (2, 6, 8, 24, 1)
RING = (32, 96, 64)


def exchanged(value, mask):
    count = lax.axis_size("row") * lax.axis_size("col")
    return lax.ppermute(value, ("row", "col"), [(i, i ^ mask) for i in range(count)])


def per_device(right_sides, diag_blocks, couplings, pair_index):
    blocks, width = diag_blocks.shape[0], diag_blocks.shape[1]
    rows = right_sides.shape[0]
    block_shape = pltpu.VMEM((blocks, rows, width), F32)
    stack_shape = pltpu.VMEM((3, blocks, rows, width), F32)
    pair_shape = pltpu.VMEM((2, blocks, rows, width), F32)
    table_shape = pltpu.VMEM((9 * blocks, 2 * rows, width), BF16)
    split_shape = pltpu.VMEM((blocks, 2 * rows, width), BF16)
    pieces_shape = pltpu.VMEM((9 * blocks, rows, width), F32)
    near_pieces_shape = pltpu.VMEM((NEAR_TABLES * blocks, rows, width), F32)
    gram_shape = pltpu.VMEM((rows, rows), F32)
    grams_shape = pltpu.VMEM((2, rows, rows), F32)
    all_grams_shape = pltpu.VMEM((rows, 4 * rows), F32)

    def spread(vector, *after):
        cb = swapped(vector, "col", 1)
        ra, rb = swapped(vector, "row", 0), swapped(vector, "row", 1)
        whole, pair = call(stack_body, [stack_shape, pair_shape], 0, (*after, cb, vector, ra, rb))
        return (swapped(whole, "col", 0), whole, cb), swapped(pair, "col", 1)

    def pulled(near_tables, db, *grams):
        table, strain = call(pull_near_body, [table_shape, block_shape], 1, (routes, *near_tables, *transposes))
        _, strain_hl, g = call(
            pull_late_body, [table_shape, split_shape, all_grams_shape if grams else gram_shape], 1,
            (routes, table, strain, db, *transposes, *grams), [block_shape], aliases={1: 0})
        return strain_hl, g

    *halves, routes = prepare(pair_index, couplings, blocks)
    couplings, transposes = halves[:2], halves[2:]
    near_tables, db = spread(right_sides, routes)
    strain_hl, g1s = pulled(near_tables, db)

    pieces, db = call(push_late_body, [pieces_shape, pair_shape], 1, (routes, strain_hl, *couplings))
    db = swapped(db, "col", 1)
    own, ra, rb, ca, cb, qa_first, qa_second = call(
        push_near_body, [block_shape] * NEAR_TABLES, 1,
        (routes, strain_hl, *couplings, pieces), [near_pieces_shape])
    ca, qa_first, qa_second = (swapped(a, "col", 0) for a in (ca, qa_first, qa_second))
    cb = swapped(cb, "col", 1)
    diag, g01 = call(diag_body, [block_shape, grams_shape], 0, (right_sides, diag_blocks))
    ra, rb = call(middle_early_body, [block_shape] * 2, 0, (ra, rb, qa_first, qa_second, db))
    rb, ra = swapped(rb, "row", 1), swapped(ra, "row", 0)
    u = call(sum_body, block_shape, 0, (own, diag, ca, cb, rb, ra))

    diag, g23 = call(diag_body, [block_shape, grams_shape], 0, (u, diag_blocks))
    near_tables, db = spread(u, g23)
    strain_hl, grams = pulled(near_tables, db, g01, g1s, g23)
    pieces, = call(push_late_body, [pieces_shape], 1, (routes, strain_hl, *couplings))
    grams = call(add_body, all_grams_shape, 0, (grams, exchanged(grams, MASKS[0]), pieces))
    pieces, = call(push_begin_body, [pieces_shape], 1, (routes, strain_hl, *couplings, pieces), aliases={4: 0})
    grams = call(add_body, all_grams_shape, 0, (grams, exchanged(grams, MASKS[1]), pieces))
    pieces, = call(push_end_body, [pieces_shape], 1, (routes, strain_hl, *couplings, pieces), aliases={4: 0})
    grams = call(add_body, all_grams_shape, 0, (grams, exchanged(grams, MASKS[2]), pieces))
    own, ra, rb, qa, qb = call(pack_body, [block_shape] * 3 + [stack_shape] * 2, 0, (pieces, grams))
    qa, qb = swapped(qa, "col", 0), swapped(qb, "col", 1)
    grams = grams + exchanged(grams, MASKS[3])
    first, second, third = (exchanged(grams, mask) for mask in RING)
    grams = (grams + first) + (second + third)
    rest, ra, rb = call(middle_last_body, [block_shape] * 3, 0, (own, diag, ra, rb, qa, qb, grams))
    rb, ra = swapped(rb, "row", 1), swapped(ra, "row", 0)
    p, q = call(solve_body, [gram_shape] * 2, 0, (grams, exchanged(grams, MASKS[4])))
    flat = jax.ShapeDtypeStruct(right_sides.shape, F32)
    return tuple(call(finish_body, [flat, flat], 0, (p, q, right_sides, u, rest, rb, ra)))


def solution(mesh):
    return jax.shard_map(
        per_device,
        mesh=mesh,
        in_specs=(
            P(None, ("row", "col")),
            P(("row", "col"), None, None),
            P(("row", "col"), None, None),
            P(None, ("row", "col")),
        ),
        out_specs=(P(None, ("row", "col")), P(None, ("row", "col"))),
        check_vma=False,
    )
```
